32 devices in a mesh: grp: 4 (over x, core), tok: 8 (over z, y).
Axes of the slice: x: 2, y: 2, z: 4, core: 2. Of those that a mesh axis runs over, the one named last changes fastest.
Arguments:
- kept_tokens: float32 [32, 768, 1152], P('grp', 'tok'), may hold values from -6 to 6
- kept_index: int32 [32, 768], P(('grp', 'tok')), may hold values from 0 to 1023, as said below
- kept_count: int32 [32], P(('grp', 'tok')), may hold values from 256 to 768, as said below
- condition: float32 [32, 1152], P(('grp', 'tok')), may hold values from -6 to 6
- mask_token: float32 [1152], P('tok'), may hold values from -6 to 6
- position_table: float32 [1024, 1152], P('tok'), may hold values from -3 to 3
- modulation_weight: float32 [1152, 6912], P(None, 'tok'), may hold values from -0.1875 to 0.1875
- modulation_bias: float32 [6912], P('tok'), may hold values from -3 to 3
- input_weight: float32 [1152, 3456], P('tok'), may hold values from -0.1875 to 0.1875
- query_bias: float32 [1152], P('tok'), may hold values from -2 to 2
- value_bias: float32 [1152], P('tok'), may hold values from -2 to 2
- output_weight: float32 [1152, 1152], P('tok'), may hold values from -3 to 3
- output_bias: float32 [1152], P('tok'), may hold values from -2 to 2
- up_weight: float32 [1152, 4608], P('tok'), may hold values from -0.1875 to 0.1875
- up_bias: float32 [4608], P('tok'), may hold values from -2 to 2
- down_weight: float32 [4608, 1152], P('tok'), may hold values from -0.09375 to 0.09375
- down_bias: float32 [1152], P('tok'), may hold values from -2 to 2
- cotangent: float32 [32, 1024, 1152], P(('grp', 'tok')), may hold values from -6 to 6
Outputs:
- block_output: float32 [32, 1024, 1152], P(('grp', 'tok'))
- kept_grad: float32 [32, 768, 1152], P('grp', 'tok')
- condition_grad: float32 [32, 1152], P(('grp', 'tok'))
- mask_grad: float32 [1152], P('tok')
- position_grad: float32 [1024, 1152], P('tok')
- modulation_weight_grad: float32 [1152, 6912], P(None, 'tok')
- modulation_bias_grad: float32 [6912], P('tok')
- input_weight_grad: float32 [1152, 3456], P('tok')
- query_bias_grad: float32 [1152], P('tok')
- value_bias_grad: float32 [1152], P('tok')
- output_weight_grad: float32 [1152, 1152], P('tok')
- output_bias_grad: float32 [1152], P('tok')
- up_weight_grad: float32 [1152, 4608], P('tok')
- up_bias_grad: float32 [4608], P('tok')
- down_weight_grad: float32 [4608, 1152], P('tok')
- down_bias_grad: float32 [1152], P('tok')
The draws below stay inside these ranges and needn't reach their ends.
Inputs may be any that keep to these rules, and one draw needn't show every extreme that they name: `kept_index`: each image's row holds 768 distinct positions; its first kept_count entries are the positions that the image keeps. `kept_count`: in every group of 8 consecutive images, one image keeps 768 positions and another keeps a quarter of 1024.
All inputs are finite; a program needn't handle non-finite values.
Results may differ from the reference program's by a relative error of at most 0.019.
The reference program's roundings to bfloat16 on the way count: a program that leaves them out, or rounds other values in their place, can miss the bound.
Values may be sent and summed in bfloat16 or wider, within the bound.
No kernel may reach another device: no remote copies, remote signals or barrier semaphores. Data moves between devices by JAX's collectives and lax.ppermute only.
A program may use at most 384 MiB of HBM per device.

```python
import math
import jax
import jax.numpy as jnp
from jax import lax

D = 1152
H = 16
HD = 72
FF = 4608
SEQ = 1024
KMAX = 768
IMG_GRP = 8
IMAGES = 32


def draw_kept_index(key, part):
    key = jax.random.fold_in(key, 11)
    image_keys = jax.random.split(key, IMAGES)
    orders = jax.vmap(lambda image_key: jax.random.permutation(image_key, SEQ))(image_keys)
    return orders[:, :KMAX].astype(jnp.int32)


def draw_kept_count(key, part):
    key = jax.random.fold_in(key, 23)
    first_key, second_key, third_key = jax.random.split(key, 3)
    counts = jax.random.randint(first_key, (IMAGES,), SEQ // 4, KMAX + 1)
    groups = IMAGES // IMG_GRP
    highest = jax.random.randint(second_key, (groups,), 0, IMG_GRP)
    lowest = (highest + 1 + jax.random.randint(third_key, (groups,), 0, IMG_GRP - 1)) % IMG_GRP
    within = jnp.arange(IMAGES) % IMG_GRP
    group_of = jnp.arange(IMAGES) // IMG_GRP
    counts = jnp.where(within == highest[group_of], KMAX, counts)
    counts = jnp.where(within == lowest[group_of], SEQ // 4, counts)
    return counts.astype(jnp.int32)


def steps_of(stream_key, dims, cuts, smallest, high):
    def one(position, blocks):
        heights = jax.random.uniform(jax.random.fold_in(jax.random.fold_in(stream_key, 6), position), (blocks,), jnp.float32, smallest / len(cuts), high / len(cuts))
        return jnp.repeat(jnp.exp(heights), dims[position] // blocks).reshape((-1,) + (1,) * (len(dims) - position - 1))

    gain = one(*cuts[0])
    for cut in cuts[1:]:
        gain = gain * one(*cut)
    return gain


def normal_values(key, dims, deviation, bound, shards=(), dtype=jnp.bfloat16):
    values = deviation * jax.random.normal(key, dims, jnp.float32)
    if shards:
        values = values * steps_of(key, dims, shards, -0.22, 0.18)
    return jnp.clip(values, -bound, bound).astype(dtype)


def setup_inputs(seed: int = 0) -> dict:
    key_list = jax.random.split(jax.random.key(seed), 19)
    kept_tokens = normal_values(key_list[0], (IMAGES, KMAX, D), 1.0, 6.0, ((0, 4), (1, 8)), jnp.float32)
    kept_index = draw_kept_index(jax.random.fold_in(key_list[18], 71), 0)
    kept_count = draw_kept_count(jax.random.fold_in(key_list[18], 71), 0)
    condition = normal_values(key_list[3], (IMAGES, D), 1.0, 6.0, ((0, 32),), jnp.float32)
    mask_token = normal_values(key_list[4], (D,), 1.0, 6.0, ((0, 8),), jnp.float32)
    position_table = normal_values(key_list[5], (SEQ, D), 0.5, 3.0, ((0, 8),), jnp.float32)
    modulation_weight = normal_values(key_list[6], (D, 6 * D), D ** -0.5, 0.1875, ((1, 8),), jnp.float32)
    modulation_bias = normal_values(key_list[7], (6 * D,), 0.5, 3.0, ((0, 8),), jnp.float32)
    input_weight = normal_values(key_list[8], (D, 3 * D), D ** -0.5, 0.1875, ((0, 8),), jnp.float32)
    query_bias = normal_values(key_list[9], (D,), 0.3, 2.0, ((0, 8),), jnp.float32)
    value_bias = normal_values(key_list[10], (D,), 0.3, 2.0, ((0, 8),), jnp.float32)
    output_weight = normal_values(key_list[11], (D, D), (max(D // 256, 1)) ** -0.5, 3.0, ((0, 8),), jnp.float32)
    output_bias = normal_values(key_list[12], (D,), 0.3, 2.0, ((0, 8),), jnp.float32)
    up_weight = normal_values(key_list[13], (D, FF), D ** -0.5, 0.1875, ((0, 8),), jnp.float32)
    up_bias = normal_values(key_list[14], (FF,), 0.3, 2.0, ((0, 8),), jnp.float32)
    down_weight = normal_values(key_list[15], (FF, D), FF ** -0.5, 0.09375, ((0, 8),), jnp.float32)
    down_bias = normal_values(key_list[16], (D,), 0.3, 2.0, ((0, 8),), jnp.float32)
    cotangent = normal_values(key_list[17], (IMAGES, SEQ, D), 1.0, 6.0, ((0, 32),), jnp.float32)
    return {"kept_tokens": kept_tokens, "kept_index": kept_index, "kept_count": kept_count, "condition": condition, "mask_token": mask_token, "position_table": position_table, "modulation_weight": modulation_weight, "modulation_bias": modulation_bias, "input_weight": input_weight, "query_bias": query_bias, "value_bias": value_bias, "output_weight": output_weight, "output_bias": output_bias, "up_weight": up_weight, "up_bias": up_bias, "down_weight": down_weight, "down_bias": down_bias, "cotangent": cotangent}


epsilon = 1e-06

@jax.custom_vjp
def low(v):
    return lax.optimization_barrier(v.astype(jnp.bfloat16)).astype(jnp.float32)

@jax.custom_vjp
def low_back(v):
    return v

def low_keep(v):
    return (low(v), None)

def low_pass(kept, grad):
    return (grad,)

def back_keep(v):
    return (v, None)

def back_low(kept, grad):
    return (low(grad),)
low.defvjp(low_keep, low_pass)
low_back.defvjp(back_keep, back_low)

def layer_norm(values):
    center = values - lax.optimization_barrier(jnp.mean(values, axis=-1, keepdims=True))
    spread = lax.optimization_barrier(jnp.mean(center * center, axis=-1, keepdims=True))
    return center * lax.rsqrt(spread + epsilon)

def matmul(left, right):
    return jnp.dot(left, right, precision=lax.Precision.HIGHEST, preferred_element_type=jnp.float32)

def forward(kept_tokens, condition, mask_token, position_table, modulation_weight, modulation_bias, input_weight, query_bias, value_bias, output_weight, output_bias, up_weight, up_bias, down_weight, down_bias, kept_index, kept_count):
    kept_low = low(kept_tokens)
    mask_low = low(mask_token)
    position_low = low(position_table)
    modulation_low = low(modulation_weight)
    modulation_bias_low = low(modulation_bias)
    input_low = low(input_weight)
    output_low = low(output_weight)
    output_bias_low = low(output_bias)
    up_low = low(up_weight)
    up_bias_low = low(up_bias)
    down_low = low(down_weight)
    down_bias_low = low(down_bias)
    projected_bias = jnp.concatenate([low(query_bias), jnp.zeros((D,), jnp.float32), low(value_bias)])
    condition_low = low(jax.nn.silu(condition))
    modulation = low_back(matmul(condition_low, modulation_low) + modulation_bias_low)
    factor = 1.0 / math.sqrt(HD)

    def one_image(inputs):
        kept_rows, index_row, count_value, modulation_row = inputs
        live_row = jnp.arange(KMAX) < count_value
        values = jnp.where(live_row[:, None], kept_rows, 0.0)
        filled = jnp.zeros((SEQ, D), jnp.float32).at[index_row].set(values)
        marker = jnp.zeros((SEQ,), jnp.float32).at[index_row].set(live_row.astype(jnp.float32))
        start_rows = filled + (1.0 - marker)[:, None] * mask_low[None, :] + position_low
        pieces = [modulation_row[number * D:(number + 1) * D] for number in range(6)]
        normed_one = low(layer_norm(start_rows) * (1.0 + pieces[1]) + pieces[0])
        projected = matmul(normed_one, input_low) + projected_bias
        queries = low(low_back(projected[:, :D])).reshape(SEQ, H, HD)
        keys_all = low(low_back(projected[:, D:2 * D])).reshape(SEQ, H, HD)
        values_all = low(low_back(projected[:, 2 * D:])).reshape(SEQ, H, HD)
        scores = low_back(jnp.einsum('qhd,khd->hqk', queries, keys_all, precision=lax.Precision.HIGHEST) * factor)
        probabilities = low(jax.nn.softmax(scores, axis=-1))
        mixture = jnp.einsum('hqk,khd->qhd', probabilities, values_all, precision=lax.Precision.HIGHEST).reshape(SEQ, D)
        mixture = low(low_back(mixture))
        branch_one = low_back(matmul(mixture, output_low) + output_bias_low)
        middle = start_rows + pieces[2] * branch_one
        normed_two = low(layer_norm(middle) * (1.0 + pieces[4]) + pieces[3])
        hidden_pre = low_back(matmul(normed_two, up_low) + up_bias_low)
        hidden = low(jax.nn.gelu(hidden_pre, approximate=True))
        branch_two = low_back(matmul(hidden, down_low) + down_bias_low)
        return middle + pieces[5] * branch_two
    return lax.map(jax.checkpoint(one_image), (kept_low, kept_index, kept_count, modulation))

def reference(kept_tokens, kept_index, kept_count, condition, mask_token, position_table, modulation_weight, modulation_bias, input_weight, query_bias, value_bias, output_weight, output_bias, up_weight, up_bias, down_weight, down_bias, cotangent):
    floats = tuple((array.astype(jnp.float32) for array in (kept_tokens, condition, mask_token, position_table, modulation_weight, modulation_bias, input_weight, query_bias, value_bias, output_weight, output_bias, up_weight, up_bias, down_weight, down_bias)))

    def tied(*inputs):
        return forward(*inputs, kept_index, kept_count)
    block_output, pullback = jax.vjp(tied, *floats)
    grads = pullback(cotangent.astype(jnp.float32))
    return (block_output, grads[0], grads[1], grads[2], grads[3], grads[4], grads[5], grads[6], grads[7], grads[8], grads[9], grads[10], grads[11], grads[12], grads[13], grads[14])
```

```python
import math

import jax
import jax.numpy as jnp
from jax import lax
from jax.sharding import PartitionSpec as P

H = 16
HD = 72


epsilon = 1e-06
block_limit = 512


def layer_norm(values):
    center = values - jnp.mean(values, axis=-1, keepdims=True)
    spread = jnp.mean(center * center, axis=-1, keepdims=True)
    return center * lax.rsqrt(spread + epsilon)


def modulate(values, scale_part, shift_part):
    return layer_norm(values) * (1.0 + scale_part) + shift_part


def gelu_tanh(values):
    return jax.nn.gelu(values, approximate=True)


def attend_image(query_rows, key_rows, value_rows, factor):
    seq_len, head_count, head_width = query_rows.shape
    block_size = min(block_limit, seq_len)
    query_blocks = query_rows.reshape(seq_len // block_size, block_size, head_count, head_width)

    def one_block(query_block):
        scores = (
            jnp.einsum("qhd,khd->hqk", query_block, key_rows, preferred_element_type=jnp.float32)
            * factor
        )
        row_max = jnp.max(scores, axis=-1, keepdims=True)
        weights = jnp.exp(scores - row_max)
        row_total = jnp.sum(weights, axis=-1, keepdims=True)
        probabilities = (weights / row_total).astype(jnp.bfloat16)
        mixture = jnp.einsum(
            "hqk,khd->qhd", probabilities, value_rows, preferred_element_type=jnp.float32
        )
        return (mixture.astype(jnp.bfloat16), (row_max + jnp.log(row_total))[..., 0])

    mixture, log_totals = lax.map(one_block, query_blocks)
    return (mixture.reshape(query_rows.shape), log_totals)


def attend_back(query_rows, key_rows, value_rows, log_totals, grad_rows, factor):
    seq_len, head_count, head_width = query_rows.shape
    block_size = min(block_limit, seq_len)
    query_blocks = query_rows.reshape(seq_len // block_size, block_size, head_count, head_width)
    grad_blocks = grad_rows.reshape(seq_len // block_size, block_size, head_count, head_width)

    def back_block(running, inputs):
        key_grad, value_grad = running
        query_block, grad_block, log_block = inputs
        scores = (
            jnp.einsum("qhd,khd->hqk", query_block, key_rows, preferred_element_type=jnp.float32)
            * factor
        )
        probabilities = jnp.exp(scores - log_block[..., None])
        value_grad = value_grad + jnp.einsum(
            "hqk,qhd->khd",
            probabilities.astype(jnp.bfloat16),
            grad_block,
            preferred_element_type=jnp.float32,
        )
        prob_grad = jnp.einsum(
            "qhd,khd->hqk", grad_block, value_rows, preferred_element_type=jnp.float32
        )
        inner = jnp.sum(probabilities * prob_grad, axis=-1, keepdims=True)
        score_grad = (probabilities * (prob_grad - inner)).astype(jnp.bfloat16)
        query_grad = (
            jnp.einsum("hqk,khd->qhd", score_grad, key_rows, preferred_element_type=jnp.float32)
            * factor
        )
        key_grad = (
            key_grad
            + jnp.einsum(
                "hqk,qhd->khd", score_grad, query_block, preferred_element_type=jnp.float32
            )
            * factor
        )
        return ((key_grad, value_grad), query_grad.astype(jnp.bfloat16))

    empty_grad = jnp.zeros((seq_len, head_count, head_width), jnp.float32)
    (key_grad, value_grad), query_grad = lax.scan(
        back_block, (empty_grad, empty_grad), (query_blocks, grad_blocks, log_totals)
    )
    return (
        query_grad.reshape(query_rows.shape),
        key_grad.astype(jnp.bfloat16),
        value_grad.astype(jnp.bfloat16),
    )


def on_device(
    kept_tokens,
    kept_index,
    kept_count,
    condition,
    mask_token,
    position_table,
    modulation_weight,
    modulation_bias,
    input_weight,
    query_bias,
    value_bias,
    output_weight,
    output_bias,
    up_weight,
    up_bias,
    down_weight,
    down_bias,
    cotangent,
):
    images_here, seq_len, model_width = cotangent.shape
    slot_count = kept_index.shape[1]
    factor = 1.0 / math.sqrt(HD)
    grp_count, tok_count = lax.axis_size("grp"), lax.axis_size("tok")
    grp_index = lax.axis_index("grp")
    low = jnp.bfloat16

    def gather_rows(shard):
        if shard.shape[0] % grp_count:
            return lax.all_gather(shard.astype(low), "tok", axis=0, tiled=True)
        quarter = shard.shape[0] // grp_count
        part = lax.dynamic_slice_in_dim(shard, grp_index * quarter, quarter, 0).astype(low)
        return lax.all_gather(part, ("tok", "grp"), axis=0, tiled=True)

    condition_low = jax.nn.silu(condition).astype(low)
    condition_group = lax.all_gather(condition_low, "tok", axis=0, tiled=True)
    modulation_low = modulation_weight.astype(low)
    modulation_part = jnp.dot(
        condition_group, modulation_low, preferred_element_type=jnp.float32
    ) + modulation_bias.astype(low).astype(jnp.float32)
    modulation = lax.all_to_all(
        modulation_part, "tok", split_axis=0, concat_axis=1, tiled=True
    )
    small_parts = [mask_token, query_bias, value_bias, output_bias, down_bias, up_bias]
    small_widths = [part.shape[0] for part in small_parts]
    small_full = lax.all_gather(jnp.concatenate(small_parts).astype(low), "tok", axis=0)

    def small_piece(number):
        start = sum(small_widths[:number])
        return small_full[:, start : start + small_widths[number]].reshape(-1)

    mask_full, query_bias_full, value_bias_full, output_bias_full, down_bias_full, up_bias_full = (
        small_piece(number) for number in range(6)
    )
    position_full = gather_rows(position_table)
    input_full = gather_rows(input_weight)
    output_full = gather_rows(output_weight)
    up_full = gather_rows(up_weight)
    down_full = gather_rows(down_weight)
    shift_one, scale_one, gate_one, shift_two, scale_two, gate_two = (
        modulation[:, None, number * model_width : (number + 1) * model_width]
        for number in range(6)
    )
    routed = lax.all_to_all(
        kept_tokens.astype(jnp.bfloat16), "tok", split_axis=0, concat_axis=1, tiled=True
    )
    live_mask = jnp.arange(slot_count)[None, :] < kept_count[:, None]

    def place_rows(index_row, live_row, routed_rows):
        values = jnp.where(live_row[:, None], routed_rows.astype(jnp.float32), 0.0)
        filled = jnp.zeros((seq_len, model_width), jnp.float32).at[index_row].set(values)
        marker = jnp.zeros((seq_len,), jnp.float32).at[index_row].set(live_row.astype(jnp.float32))
        return (filled, marker)

    filled, marker = jax.vmap(place_rows)(kept_index, live_mask, routed)
    empty_rows = (1.0 - marker)[..., None]
    start_rows = (
        filled
        + empty_rows * mask_full.astype(jnp.float32)
        + position_full.astype(jnp.float32)[None]
    )
    normed_one = modulate(start_rows, scale_one, shift_one).astype(jnp.bfloat16)
    projected_bias = jnp.concatenate(
        [
            query_bias_full.astype(jnp.float32),
            jnp.zeros((model_width,), jnp.float32),
            value_bias_full.astype(jnp.float32),
        ]
    )
    projected = (
        jnp.einsum("isd,de->ise", normed_one, input_full, preferred_element_type=jnp.float32)
        + projected_bias
    )
    head_shape = (images_here, seq_len, H, HD)
    queries = projected[..., :model_width].astype(jnp.bfloat16).reshape(head_shape)
    keys_all = (
        projected[..., model_width : 2 * model_width].astype(jnp.bfloat16).reshape(head_shape)
    )
    values_all = projected[..., 2 * model_width :].astype(jnp.bfloat16).reshape(head_shape)

    def attend_item(triple):
        return attend_image(triple[0], triple[1], triple[2], factor)

    mixture, log_totals = lax.map(attend_item, (queries, keys_all, values_all))
    mixture = mixture.reshape(images_here, seq_len, model_width)
    branch_one = jnp.einsum(
        "isd,de->ise", mixture, output_full, preferred_element_type=jnp.float32
    ) + output_bias_full.astype(jnp.float32)
    middle = start_rows + gate_one * branch_one
    normed_two = modulate(middle, scale_two, shift_two).astype(jnp.bfloat16)
    hidden_pre = jnp.einsum(
        "isd,df->isf", normed_two, up_full, preferred_element_type=jnp.float32
    ) + up_bias_full.astype(jnp.float32)
    hidden = gelu_tanh(hidden_pre).astype(jnp.bfloat16)
    branch_two = jnp.einsum(
        "isf,fd->isd", hidden, down_full, preferred_element_type=jnp.float32
    ) + down_bias_full.astype(jnp.float32)
    block_output = middle + gate_two * branch_two
    grad_two = (gate_two * cotangent).astype(jnp.bfloat16)
    gate_two_grad = jnp.sum(cotangent * branch_two, axis=1)
    down_bias_term = jnp.sum(grad_two.astype(jnp.float32), axis=(0, 1))
    hidden_grad = jnp.einsum("isd,fd->isf", grad_two, down_full, preferred_element_type=jnp.float32)
    _, gelu_back = jax.vjp(gelu_tanh, hidden_pre)
    pre_grad = gelu_back(hidden_grad)[0].astype(jnp.bfloat16)
    up_bias_term = jnp.sum(pre_grad.astype(jnp.float32), axis=(0, 1))
    normed_two_grad = jnp.einsum(
        "isf,df->isd", pre_grad, up_full, preferred_element_type=jnp.float32
    )
    _, norm_two_back = jax.vjp(modulate, middle, scale_two, shift_two)
    middle_part, scale_two_grad, shift_two_grad = norm_two_back(normed_two_grad)
    middle_grad = cotangent + middle_part
    grad_one = (gate_one * middle_grad).astype(jnp.bfloat16)
    gate_one_grad = jnp.sum(middle_grad * branch_one, axis=1)
    output_bias_term = jnp.sum(grad_one.astype(jnp.float32), axis=(0, 1))
    mixture_grad = (
        jnp.einsum("ise,de->isd", grad_one, output_full, preferred_element_type=jnp.float32)
        .astype(jnp.bfloat16)
        .reshape(head_shape)
    )

    def back_item(group_rows):
        return attend_back(
            group_rows[0], group_rows[1], group_rows[2], group_rows[3], group_rows[4], factor
        )

    queries_grad, keys_grad, values_grad = lax.map(
        back_item, (queries, keys_all, values_all, log_totals, mixture_grad)
    )
    flat_shape = (images_here, seq_len, model_width)
    projected_grad = jnp.concatenate(
        [
            queries_grad.reshape(flat_shape),
            keys_grad.reshape(flat_shape),
            values_grad.reshape(flat_shape),
        ],
        axis=-1,
    )
    query_bias_term = jnp.sum(queries_grad.reshape(flat_shape).astype(jnp.float32), axis=(0, 1))
    value_bias_term = jnp.sum(values_grad.reshape(flat_shape).astype(jnp.float32), axis=(0, 1))
    normed_one_grad = jnp.einsum(
        "ise,de->isd", projected_grad, input_full, preferred_element_type=jnp.float32
    )
    _, norm_one_back = jax.vjp(modulate, start_rows, scale_one, shift_one)
    start_part, scale_one_grad, shift_one_grad = norm_one_back(normed_one_grad)
    start_grad = middle_grad + start_part
    modulation_grad = jnp.concatenate(
        [
            shift_one_grad[:, 0],
            scale_one_grad[:, 0],
            gate_one_grad,
            shift_two_grad[:, 0],
            scale_two_grad[:, 0],
            gate_two_grad,
        ],
        axis=1,
    ).astype(jnp.bfloat16)
    position_term = jnp.sum(start_grad, axis=0)
    mask_term = jnp.sum(start_grad * empty_rows, axis=(0, 1))

    def pick_rows(grad_rows, index_row, live_row):
        return jnp.where(live_row[:, None], grad_rows[index_row], 0.0)

    slot_grad = jax.vmap(pick_rows)(start_grad, kept_index, live_mask)
    kept_grad = lax.all_to_all(
        slot_grad.astype(jnp.bfloat16), "tok", split_axis=1, concat_axis=0, tiled=True
    ).astype(slot_grad.dtype)
    condition_all = lax.all_gather(condition_group, "grp", axis=0, tiled=True)
    modulation_grad_group = lax.all_to_all(
        modulation_grad, "tok", split_axis=1, concat_axis=0, tiled=True
    )
    modulation_grad_all = lax.all_gather(modulation_grad_group, "grp", axis=0, tiled=True)
    modulation_total = jnp.einsum(
        "id,ie->de", condition_all, modulation_grad_all, preferred_element_type=jnp.float32
    )
    modulation_bias_total = jnp.sum(modulation_grad_all.astype(jnp.float32), axis=0)
    condition_part = jnp.einsum(
        "ie,de->id", modulation_grad_group, modulation_low, preferred_element_type=jnp.float32
    )
    condition_low_grad = jnp.sum(
        lax.all_to_all(condition_part, "tok", split_axis=0, concat_axis=0, tiled=True),
        axis=0,
        keepdims=True,
    )
    _, silu_back = jax.vjp(jax.nn.silu, condition)
    condition_grad = silu_back(condition_low_grad)[0]
    input_term = jnp.einsum(
        "isd,ise->de", normed_one, projected_grad, preferred_element_type=jnp.float32
    )
    output_term = jnp.einsum("isd,ise->de", mixture, grad_one, preferred_element_type=jnp.float32)
    up_term = jnp.einsum("isd,isf->df", normed_two, pre_grad, preferred_element_type=jnp.float32)
    down_term = jnp.einsum("isf,isd->fd", hidden, grad_two, preferred_element_type=jnp.float32)
    swap = lambda bit: [(g, g ^ bit) for g in range(grp_count)]
    core = grp_index % 2

    def reduce_rows(term):
        halves = term.reshape(term.shape[0], 2, term.shape[1] // 2)
        mine = lax.dynamic_index_in_dim(halves, core, 1, keepdims=False)
        other = lax.dynamic_index_in_dim(halves, 1 - core, 1, keepdims=False).astype(low)
        got = lax.ppermute(other, "grp", swap(1))
        chip = (mine + got.astype(jnp.float32)).astype(low)
        shard = lax.psum_scatter(chip, "tok", scatter_dimension=0, tiled=True)
        bit = 2
        while bit < grp_count:
            got = lax.ppermute(shard, "grp", swap(bit))
            shard = (shard.astype(jnp.float32) + got.astype(jnp.float32)).astype(low)
            bit *= 2
        got = lax.ppermute(shard, "grp", swap(1))
        left = jnp.where(core == 0, shard, got)
        right = jnp.where(core == 0, got, shard)
        return jnp.concatenate([left, right], axis=1).astype(jnp.float32)

    down_total = reduce_rows(down_term)
    up_total = reduce_rows(up_term)
    output_total = reduce_rows(output_term)
    input_total = reduce_rows(input_term)
    position_total = reduce_rows(position_term)
    small_terms = [
        mask_term, query_bias_term, value_bias_term, output_bias_term, down_bias_term, up_bias_term
    ]
    small_term = jnp.concatenate(
        [term.reshape(tok_count, -1) for term in small_terms], axis=1
    )
    small_sum = lax.psum(
        lax.psum_scatter(small_term, "tok", scatter_dimension=0), "grp"
    )
    cut = [sum(small_widths[:number]) for number in range(7)]
    (
        mask_total,
        query_bias_total,
        value_bias_total,
        output_bias_total,
        down_bias_total,
        up_bias_total,
    ) = (small_sum[cut[number] : cut[number + 1]] for number in range(6))
    return (
        block_output,
        kept_grad,
        condition_grad,
        mask_total,
        position_total,
        modulation_total,
        modulation_bias_total,
        input_total,
        query_bias_total,
        value_bias_total,
        output_total,
        output_bias_total,
        up_total,
        up_bias_total,
        down_total,
        down_bias_total,
    )


def solution(mesh):
    return jax.shard_map(
        on_device,
        mesh=mesh,
        in_specs=(
            P("grp", "tok", None),
            P(("grp", "tok"), None),
            P(("grp", "tok")),
            P(("grp", "tok"), None),
            P("tok"),
            P("tok", None),
            P(None, "tok"),
            P("tok"),
            P("tok", None),
            P("tok"),
            P("tok"),
            P("tok", None),
            P("tok"),
            P("tok", None),
            P("tok"),
            P("tok", None),
            P("tok"),
            P(("grp", "tok"), None, None),
        ),
        out_specs=(
            P(("grp", "tok"), None, None),
            P("grp", "tok", None),
            P(("grp", "tok"), None),
            P("tok"),
            P("tok", None),
            P(None, "tok"),
            P("tok"),
            P("tok", None),
            P("tok"),
            P("tok"),
            P("tok", None),
            P("tok"),
            P("tok", None),
            P("tok"),
            P("tok", None),
            P("tok"),
        ),
        check_vma=False,
    )
```

```python
import functools
import math

import jax
import jax.numpy as jnp
from jax import lax
from jax.experimental import pallas as pl
from jax.experimental.pallas import tpu as pltpu
from jax.sharding import PartitionSpec as P

H = 16
HD = 72
LANES = 128

epsilon = 1e-06
f32 = jnp.float32
bf16 = jnp.bfloat16
plain = (((1,), (0,)), ((), ()))
right_turned = (((1,), (1,)), ((), ()))
left_turned = (((0,), (0,)), ((), ()))
vmem_limit = 60 << 20


def product(left, right, dims=plain):
    return lax.dot_general(left, right, dims, preferred_element_type=f32)


def whole_block(array):
    zeros = (0,) * array.ndim
    return pl.BlockSpec(array.shape, lambda *_: zeros)


def row_block(rows, *rest):
    return pl.BlockSpec((rows,) + rest, lambda i: (i,) + (0,) * len(rest))


smem = pl.BlockSpec(memory_space=pltpu.SMEM)
anywhere = pl.BlockSpec(memory_space=pl.ANY)


def params():
    return pltpu.CompilerParams(vmem_limit_bytes=vmem_limit)


def cost(flops, moved, exps=0):
    return pl.CostEstimate(flops=int(flops), bytes_accessed=int(moved), transcendentals=int(exps))


def column_sum(values):
    return jnp.sum(values, axis=0, keepdims=True)


def normalize(values):
    center = values - jnp.mean(values, axis=-1, keepdims=True)
    spread = jnp.mean(center * center, axis=-1, keepdims=True)
    inverse = lax.rsqrt(spread + epsilon)
    return center * inverse, inverse


def normalize_back(grad, unit, inverse, scale):
    scaled = grad * (1.0 + scale)
    first = jnp.mean(scaled, axis=-1, keepdims=True)
    second = jnp.mean(scaled * unit, axis=-1, keepdims=True)
    return (scaled - first - unit * second) * inverse


def start_kernel(count_ref, index_ref, kept_ref, position_ref, mask_ref, mod_ref, start_ref, norm_ref):
    rows, slots = position_ref.shape[0], kept_ref.shape[0]
    base = pl.program_id(0) * rows
    here = lax.broadcasted_iota(jnp.int32, (rows, slots), 0) + base
    slot = lax.broadcasted_iota(jnp.int32, (rows, slots), 1)
    chosen = jnp.where((index_ref[...] == here) & (slot < count_ref[0]), 1.0, 0.0)
    filled = product(chosen.astype(bf16), kept_ref[...])
    empty = 1.0 - jnp.sum(chosen, axis=1, keepdims=True)
    start = filled + empty * mask_ref[...] + position_ref[...].astype(f32)
    start_ref[...] = start
    unit, _ = normalize(start)
    norm_ref[...] = (unit * (1.0 + mod_ref[1:2]) + mod_ref[0:1]).astype(bf16)


def start_call(count, index, kept, position, mask, mod):
    seq_len, width = position.shape
    rows = seq_len // 4
    return pl.pallas_call(
        start_kernel,
        grid=(4,),
        in_specs=[
            smem,
            whole_block(index),
            whole_block(kept),
            row_block(rows, width),
            whole_block(mask),
            whole_block(mod),
        ],
        out_specs=[row_block(rows, width)] * 2,
        out_shape=[
            jax.ShapeDtypeStruct((seq_len, width), f32),
            jax.ShapeDtypeStruct((seq_len, width), bf16),
        ],
        compiler_params=params(),
        cost_estimate=cost(2 * seq_len * width * kept.shape[0], 14 * seq_len * width),
    )(count, index, kept, position, mask, mod)


def block_copy(core_ref, mine_ref, other_ref, block, target, sem):
    owner, place = block // 2, block % 2

    @pl.when(core_ref[0] == owner)
    def _():
        pltpu.make_async_copy(mine_ref.at[place], target, sem).start()

    @pl.when(core_ref[0] != owner)
    def _():
        pltpu.make_async_copy(other_ref.at[place], target, sem).start()


def block_wait(mine_ref, target, sem):
    pltpu.make_async_copy(mine_ref.at[0], target, sem).wait()


def split_heads(values, store):
    rows = values.shape[0]
    blank = jnp.zeros((rows, LANES - HD), values.dtype)
    for head in range(H):
        store(head, jnp.concatenate([values[:, head * HD : (head + 1) * HD], blank], axis=1))


def project_kernel(core_ref, norm_ref, mine_ref, other_ref, bias_ref, out_ref, weight, sems):
    step = pl.program_id(0)

    @pl.when(step == 0)
    def _():
        for block in range(3):
            block_copy(core_ref, mine_ref, other_ref, block, weight.at[block], sems.at[block])

    block_wait(mine_ref, weight.at[step], sems.at[step])
    half = norm_ref.shape[0] // 2
    for part in range(2):
        rows = slice(part * half, (part + 1) * half)
        result = product(norm_ref[rows], weight[step]) + bias_ref[0]

        def store(head, value):
            out_ref[0, head, rows] = value

        split_heads(result.astype(bf16), store)


def project_call(core, norm, mine, other, bias):
    seq_len, width = norm.shape
    return pl.pallas_call(
        project_kernel,
        grid=(3,),
        in_specs=[
            smem,
            whole_block(norm),
            anywhere,
            anywhere,
            pl.BlockSpec((1, 1, width), lambda i: (i, 0, 0)),
        ],
        out_specs=pl.BlockSpec((1, H, seq_len, LANES), lambda i: (i, 0, 0, 0)),
        out_shape=jax.ShapeDtypeStruct((3, H, seq_len, LANES), bf16),
        scratch_shapes=[pltpu.VMEM((3, width, width), bf16), pltpu.SemaphoreType.DMA((3,))],
        compiler_params=params(),
        cost_estimate=cost(6 * seq_len * width * width, 12 * seq_len * width + 6 * width * width),
    )(core, norm, mine, other, bias)


def attend_kernel(query_ref, key_ref, value_ref, mix_ref, log_ref, *, size, factor):
    turned_value = value_ref[0, 0].T
    for part in range(query_ref.shape[2] // size):
        rows = slice(part * size, (part + 1) * size)
        scores = product(key_ref[0, 0], query_ref[0, 0, rows], right_turned)
        top = jnp.max(scores, axis=0, keepdims=True)
        weights = jnp.exp2((scores - top) * factor)
        total = jnp.sum(weights, axis=0, keepdims=True)
        mix = product(turned_value, weights.astype(bf16))
        mix_ref[0, rows] = (mix / total).T.astype(bf16)
        log_ref[0, :, rows] = top * factor + jnp.log2(total)


def head_block(place, seq_len):
    return pl.BlockSpec((1, 1, seq_len, LANES), lambda h: (place, h, 0, 0))


def attend_call(projected):
    seq_len = projected.shape[2]
    flat = pl.BlockSpec((1, seq_len, LANES), lambda h: (h, 0, 0))
    return pl.pallas_call(
        functools.partial(
            attend_kernel, size=seq_len, factor=math.log2(math.e) / math.sqrt(HD)
        ),
        grid=(H,),
        in_specs=[head_block(place, seq_len) for place in range(3)],
        out_specs=[flat, pl.BlockSpec((1, 1, seq_len), lambda h: (h, 0, 0))],
        out_shape=[
            jax.ShapeDtypeStruct((H, seq_len, LANES), bf16),
            jax.ShapeDtypeStruct((H, 1, seq_len), f32),
        ],
        compiler_params=params(),
        cost_estimate=cost(4 * H * seq_len * seq_len * 256, 8 * H * seq_len * LANES, H * seq_len * seq_len),
    )(projected, projected, projected)


def attend_back_kernel(
    query_ref, key_ref, value_ref, mix_ref, log_ref, grad_ref, query_grad_ref, key_grad_ref,
    value_grad_ref, key_sum, value_sum, *, size, factor
):
    key, value = key_ref[0, 0], value_ref[0, 0]
    turned_key = key.T
    base_two = factor * math.log2(math.e)
    for part in range(query_ref.shape[2] // size):
        rows = slice(part * size, (part + 1) * size)
        query, grad = query_ref[0, 0, rows], grad_ref[0, rows]
        scores = product(key, query, right_turned)
        weights = jnp.exp2(scores * base_two - log_ref[0, :, rows])
        value_part = product(weights.astype(bf16), grad)
        weight_grad = product(value, grad, right_turned)
        inner = column_sum((grad.astype(f32) * mix_ref[0, rows].astype(f32)).T)
        score_grad = (weights * (weight_grad - inner)).astype(bf16)
        key_part = product(score_grad, query)
        query_grad_ref[0, rows] = (product(turned_key, score_grad) * factor).T.astype(bf16)
        if part == 0:
            key_sum[...] = key_part
            value_sum[...] = value_part
        else:
            key_sum[...] += key_part
            value_sum[...] += value_part
    key_grad_ref[0] = (key_sum[...] * factor).astype(bf16)
    value_grad_ref[0] = value_sum[...].astype(bf16)


def attend_back_call(projected, mix, logs, grad):
    seq_len = projected.shape[2]
    flat = pl.BlockSpec((1, seq_len, LANES), lambda h: (h, 0, 0))
    return pl.pallas_call(
        functools.partial(attend_back_kernel, size=seq_len // 2, factor=1.0 / math.sqrt(HD)),
        grid=(H,),
        in_specs=[head_block(place, seq_len) for place in range(3)]
        + [flat, pl.BlockSpec((1, 1, seq_len), lambda h: (h, 0, 0)), flat],
        out_specs=[flat] * 3,
        out_shape=[jax.ShapeDtypeStruct((H, seq_len, LANES), bf16)] * 3,
        scratch_shapes=[pltpu.VMEM((seq_len, LANES), f32)] * 2,
        compiler_params=params(),
        cost_estimate=cost(10 * H * seq_len * seq_len * 256, 16 * H * seq_len * LANES, H * seq_len * seq_len),
    )(projected, projected, projected, mix, logs, grad)


def join_heads(read):
    return jnp.concatenate([read(head)[:, :HD] for head in range(H)], axis=1)


def mix_kernel(
    core_ref, mix_ref, start_ref, mine_ref, other_ref, bias_ref, mod_ref, joined_ref, branch_ref,
    middle_ref, norm_ref, weight, sem
):
    @pl.when(pl.program_id(0) == 0)
    def _():
        block_copy(core_ref, mine_ref, other_ref, 3, weight, sem)
        block_wait(mine_ref, weight, sem)

    joined = join_heads(lambda head: mix_ref[head])
    joined_ref[...] = joined
    branch = product(joined, weight[...]) + bias_ref[...]
    branch_ref[...] = branch
    middle = start_ref[...] + mod_ref[2:3] * branch
    middle_ref[...] = middle
    unit, _ = normalize(middle)
    norm_ref[...] = (unit * (1.0 + mod_ref[4:5]) + mod_ref[3:4]).astype(bf16)


def mix_call(core, mix, start, mine, other, bias, mod):
    seq_len, width = start.shape
    rows = seq_len // 4
    block = row_block(rows, width)
    return pl.pallas_call(
        mix_kernel,
        grid=(4,),
        in_specs=[
            smem,
            pl.BlockSpec((H, rows, LANES), lambda i: (0, i, 0)),
            block,
            anywhere,
            anywhere,
            whole_block(bias),
            whole_block(mod),
        ],
        out_specs=[block] * 4,
        out_shape=[
            jax.ShapeDtypeStruct((seq_len, width), kind) for kind in (bf16, f32, f32, bf16)
        ],
        scratch_shapes=[pltpu.VMEM((width, width), bf16), pltpu.SemaphoreType.DMA],
        compiler_params=params(),
        cost_estimate=cost(2 * seq_len * width * width, 18 * seq_len * width),
    )(core, mix, start, mine, other, bias, mod)


def gelu_parts(values):
    inner = 0.7978845608028654 * (values + 0.044715 * values * values * values)
    turned = jnp.tanh(inner)
    half = 0.5 * (1.0 + turned)
    slope = half + 0.5 * values * (1.0 - turned * turned) * (
        0.7978845608028654 * (1.0 + 0.134145 * values * values)
    )
    return values * half, slope


def feed_kernel(
    norm_ref, middle_ref, cot_ref, branch_ref, mod_ref, up_bias_ref, down_bias_ref, up_mine, up_other,
    down_mine, down_other, out_ref, hidden_ref, pre_ref, grad_two_ref, middle_grad_ref, grad_one_ref,
    sums_ref, up_sums_ref, up, down, slopes, sems
):
    step = pl.program_id(0)
    chunks = 4

    def copies(chunk):
        up_from, down_from = (up_mine, down_mine) if chunk < 2 else (up_other, down_other)
        place = chunk % 2
        return (
            pltpu.make_async_copy(up_from.at[place], up.at[chunk], sems.at[0, chunk]),
            pltpu.make_async_copy(down_from.at[place], down.at[chunk], sems.at[1, chunk]),
        )

    @pl.when(step == 0)
    def _():
        for chunk in range(chunks):
            for copy in copies(chunk):
                copy.start()
        sums_ref[...] = jnp.zeros_like(sums_ref)
        up_sums_ref[...] = jnp.zeros_like(up_sums_ref)

    norm = norm_ref[...]
    total = None
    for chunk in range(chunks):

        @pl.when(step == 0)
        def _():
            for copy in copies(chunk):
                copy.wait()

        before = product(norm, up[chunk]) + up_bias_ref[chunk]
        hidden, slope = gelu_parts(before)
        hidden = hidden.astype(bf16)
        hidden_ref[chunk] = hidden
        slopes[chunk] = slope.astype(slopes.dtype)
        part = product(hidden, down[chunk])
        total = part if total is None else total + part
    branch_two = total + down_bias_ref[...]
    middle, cot = middle_ref[...], cot_ref[...]
    gate_two = mod_ref[5:6]
    out_ref[...] = middle + gate_two * branch_two
    grad_two = (gate_two * cot).astype(bf16)
    grad_two_ref[...] = grad_two
    sums_ref[0:1] += column_sum(cot * branch_two)
    sums_ref[1:2] += column_sum(grad_two.astype(f32))
    total = None
    for chunk in range(chunks):
        pre = (product(grad_two, down[chunk], right_turned) * slopes[chunk].astype(f32)).astype(bf16)
        pre_ref[chunk] = pre
        up_sums_ref[chunk] += column_sum(pre.astype(f32))
        part = product(pre, up[chunk], right_turned)
        total = part if total is None else total + part
    unit, inverse = normalize(middle)
    sums_ref[2:3] += column_sum(total * unit)
    sums_ref[3:4] += column_sum(total)
    middle_grad = cot + normalize_back(total, unit, inverse, mod_ref[4:5])
    middle_grad_ref[...] = middle_grad
    sums_ref[4:5] += column_sum(middle_grad * branch_ref[...])
    grad_one = (mod_ref[2:3] * middle_grad).astype(bf16)
    grad_one_ref[...] = grad_one
    sums_ref[5:6] += column_sum(grad_one.astype(f32))


def feed_call(norm, middle, cot, branch, mod, up_bias, down_bias, up_mine, up_other, down_mine, down_other):
    seq_len, width = middle.shape
    steps = 4
    rows = seq_len // steps
    block = row_block(rows, width)
    chunked = pl.BlockSpec((4, rows, width), lambda i: (0, i, 0))
    wide = jax.ShapeDtypeStruct((4, seq_len, width), bf16)
    return pl.pallas_call(
        feed_kernel,
        grid=(steps,),
        in_specs=[
            block,
            block,
            block,
            block,
            whole_block(mod),
            whole_block(up_bias),
            whole_block(down_bias),
            anywhere,
            anywhere,
            anywhere,
            anywhere,
        ],
        out_specs=[
            block,
            chunked,
            chunked,
            block,
            block,
            block,
            pl.BlockSpec((8, width), lambda i: (0, 0)),
            pl.BlockSpec((4, 1, width), lambda i: (0, 0, 0)),
        ],
        out_shape=[
            jax.ShapeDtypeStruct((seq_len, width), f32),
            wide,
            wide,
            jax.ShapeDtypeStruct((seq_len, width), bf16),
            jax.ShapeDtypeStruct((seq_len, width), f32),
            jax.ShapeDtypeStruct((seq_len, width), bf16),
            jax.ShapeDtypeStruct((8, width), f32),
            jax.ShapeDtypeStruct((4, 1, width), f32),
        ],
        scratch_shapes=[
            pltpu.VMEM((4, width, width), bf16),
            pltpu.VMEM((4, width, width), bf16),
            pltpu.VMEM((4, rows, width), f32),
            pltpu.SemaphoreType.DMA((2, 4)),
        ],
        compiler_params=params(),
        cost_estimate=cost(32 * seq_len * width * width, 60 * seq_len * width, 4 * seq_len * width),
    )(norm, middle, cot, branch, mod, up_bias, down_bias, up_mine, up_other, down_mine, down_other)


def feed_weight_kernel(norm_ref, pre_ref, hidden_ref, grad_ref, out_ref):
    step = pl.program_id(0)

    @pl.when(step < 2)
    def _():
        out_ref[0] = product(norm_ref[...], pre_ref[0], left_turned).astype(bf16)

    @pl.when(step >= 2)
    def _():
        out_ref[0] = product(hidden_ref[0], grad_ref[...], left_turned).astype(bf16)


def feed_weight_call(norm, pre, hidden, grad, first):
    seq_len, width = norm.shape
    block = (1, seq_len, width)
    return pl.pallas_call(
        feed_weight_kernel,
        grid=(4,),
        in_specs=[
            whole_block(norm),
            pl.BlockSpec(block, lambda i: (first + jnp.minimum(i, 1), 0, 0)),
            pl.BlockSpec(block, lambda i: (first + jnp.maximum(i - 2, 0), 0, 0)),
            whole_block(grad),
        ],
        out_specs=pl.BlockSpec((1, width, width), lambda i: (i, 0, 0)),
        out_shape=jax.ShapeDtypeStruct((4, width, width), bf16),
        compiler_params=params(),
        cost_estimate=cost(8 * seq_len * width * width, 12 * seq_len * width + 8 * width * width),
    )(norm, pre, hidden, grad)


def attention_weight_kernel(block_ref, norm_ref, joined_ref, projected_ref, grad_ref, out_ref):
    block = block_ref[pl.program_id(0)]

    @pl.when(block < 3)
    def _():
        out_ref[0] = product(norm_ref[...], projected_ref[0], left_turned).astype(bf16)

    @pl.when(block == 3)
    def _():
        out_ref[0] = product(joined_ref[...], grad_ref[...], left_turned).astype(bf16)


def attention_weight_call(blocks, norm, joined, projected_grad, grad_one):
    seq_len, width = norm.shape
    full = pl.BlockSpec((seq_len, width), lambda i, b: (0, 0))
    return pl.pallas_call(
        attention_weight_kernel,
        grid_spec=pltpu.PrefetchScalarGridSpec(
            num_scalar_prefetch=1,
            grid=(2,),
            in_specs=[
                full,
                full,
                pl.BlockSpec((1, seq_len, width), lambda i, b: (jnp.minimum(b[i], 2), 0, 0)),
                full,
            ],
            out_specs=pl.BlockSpec((1, width, width), lambda i, b: (i, 0, 0)),
        ),
        out_shape=jax.ShapeDtypeStruct((2, width, width), bf16),
        compiler_params=params(),
        cost_estimate=cost(4 * seq_len * width * width, 10 * seq_len * width + 4 * width * width),
    )(blocks, norm, joined, projected_grad, grad_one)


def mix_grad_kernel(core_ref, grad_ref, mine_ref, other_ref, out_ref, weight, sem):
    @pl.when(pl.program_id(0) == 0)
    def _():
        block_copy(core_ref, mine_ref, other_ref, 3, weight, sem)
        block_wait(mine_ref, weight, sem)

    def store(head, value):
        out_ref[head] = value

    split_heads(product(grad_ref[...], weight[...], right_turned).astype(bf16), store)


def mix_grad_call(core, grad_one, mine, other):
    seq_len, width = grad_one.shape
    rows = seq_len // 2
    return pl.pallas_call(
        mix_grad_kernel,
        grid=(2,),
        in_specs=[smem, row_block(rows, width), anywhere, anywhere],
        out_specs=pl.BlockSpec((H, rows, LANES), lambda i: (0, i, 0)),
        out_shape=jax.ShapeDtypeStruct((H, seq_len, LANES), bf16),
        scratch_shapes=[pltpu.VMEM((width, width), bf16), pltpu.SemaphoreType.DMA],
        compiler_params=params(),
        cost_estimate=cost(2 * seq_len * width * width, 8 * seq_len * width),
    )(core, grad_one, mine, other)


def start_back_kernel(
    core_ref, count_ref, index_row_ref, index_ref, query_ref, key_ref, value_ref, mine_ref, other_ref,
    middle_grad_ref, start_ref, mod_ref, joined_ref, row_grad_ref, slot_ref, sums_ref, weight, slots, sems
):
    step = pl.program_id(0)
    rows, width = start_ref.shape
    slot_count = slots.shape[0]

    @pl.when(step == 0)
    def _():
        for block in range(3):
            block_copy(core_ref, mine_ref, other_ref, block, weight.at[block], sems.at[block])
        sums_ref[...] = jnp.zeros_like(sums_ref)

    total = None
    for block, ref in enumerate((query_ref, key_ref, value_ref)):
        joined = join_heads(lambda head: ref[head])
        joined_ref[block] = joined
        if block != 1:
            place = block // 2
            sums_ref[place : place + 1] += column_sum(joined.astype(f32))

        @pl.when(step == 0)
        def _():
            block_wait(mine_ref, weight.at[block], sems.at[block])

        part = product(joined, weight[block], right_turned)
        total = part if total is None else total + part
    unit, inverse = normalize(start_ref[...])
    sums_ref[2:3] += column_sum(total * unit)
    sums_ref[3:4] += column_sum(total)
    row_grad = middle_grad_ref[...] + normalize_back(total, unit, inverse, mod_ref[1:2])
    row_low = row_grad.astype(bf16)
    row_grad_ref[...] = row_low
    base = step * rows
    place = lax.broadcasted_iota(jnp.int32, (slot_count, rows), 1) + base
    slot = lax.broadcasted_iota(jnp.int32, (slot_count, rows), 0)
    chosen = jnp.where((index_ref[...] == place) & (slot < count_ref[0]), 1.0, 0.0)
    part = product(chosen.astype(bf16), row_low)

    @pl.when(step == 0)
    def _():
        slots[...] = part

    @pl.when(step > 0)
    def _():
        slots[...] += part

    here = lax.broadcasted_iota(jnp.int32, (rows, slot_count), 0) + base
    lane = lax.broadcasted_iota(jnp.int32, (rows, slot_count), 1)
    taken = jnp.where((index_row_ref[...] == here) & (lane < count_ref[0]), 1.0, 0.0)
    empty = 1.0 - jnp.sum(taken, axis=1, keepdims=True)
    sums_ref[4:5] += column_sum(row_grad * empty)

    @pl.when(step == pl.num_programs(0) - 1)
    def _():
        slot_ref[...] = slots[...].astype(bf16)


def start_back_call(core, count, index, query_grad, key_grad, value_grad, mine, other, middle_grad, start, mod):
    seq_len, width = start.shape
    slot_count = index.shape[1]
    steps = 4
    rows = seq_len // steps
    heads = pl.BlockSpec((H, rows, LANES), lambda i: (0, i, 0))
    block = row_block(rows, width)
    column = index.reshape(slot_count, 1)
    return pl.pallas_call(
        start_back_kernel,
        grid=(steps,),
        in_specs=[
            smem,
            smem,
            whole_block(index),
            whole_block(column),
            heads,
            heads,
            heads,
            anywhere,
            anywhere,
            block,
            block,
            whole_block(mod),
        ],
        out_specs=[
            pl.BlockSpec((3, rows, width), lambda i: (0, i, 0)),
            block,
            pl.BlockSpec((slot_count, width), lambda i: (0, 0)),
            pl.BlockSpec((8, width), lambda i: (0, 0)),
        ],
        out_shape=[
            jax.ShapeDtypeStruct((3, seq_len, width), bf16),
            jax.ShapeDtypeStruct((seq_len, width), bf16),
            jax.ShapeDtypeStruct((slot_count, width), bf16),
            jax.ShapeDtypeStruct((8, width), f32),
        ],
        scratch_shapes=[
            pltpu.VMEM((3, width, width), bf16),
            pltpu.VMEM((slot_count, width), f32),
            pltpu.SemaphoreType.DMA((3,)),
        ],
        compiler_params=params(),
        cost_estimate=cost(8 * seq_len * width * width, 26 * seq_len * width),
    )(core, count, index, column, query_grad, key_grad, value_grad, mine, other, middle_grad, start, mod)


def swap_pairs(size, bit):
    return [(place, place ^ bit) for place in range(size)]


def swap_core(values):
    return lax.ppermute(values, "grp", swap_pairs(lax.axis_size("grp"), 1))


def add_low(*parts):
    total = parts[0].astype(f32)
    for part in parts[1:]:
        total = total + part.astype(f32)
    return total.astype(bf16)


def gather_blocks(shard):
    return lax.all_gather(shard, "tok", axis=1, tiled=True)


def scatter_blocks(mine, other):
    chip = add_low(mine, swap_core(other))
    shard = lax.psum_scatter(chip, "tok", scatter_dimension=1, tiled=True)
    bit = 2
    while bit < lax.axis_size("grp"):
        shard = add_low(shard, lax.ppermute(shard, "grp", swap_pairs(lax.axis_size("grp"), bit)))
        bit *= 2
    return shard


def on_device(
    kept_tokens,
    kept_index,
    kept_count,
    condition,
    mask_token,
    position_table,
    modulation_weight,
    modulation_bias,
    input_weight,
    query_bias,
    value_bias,
    output_weight,
    output_bias,
    up_weight,
    up_bias,
    down_weight,
    down_bias,
    cotangent,
):
    _, seq_len, width = cotangent.shape
    tok_count = lax.axis_size("tok")
    core = lax.axis_index("grp") % 2
    core_row = core.reshape(1)
    share = input_weight.shape[0]
    position_rows = position_table.shape[0]

    def by_core(first, second):
        return jnp.where(core == 0, first, second)

    condition_low = jax.nn.silu(condition).astype(bf16)
    condition_group = lax.all_gather(condition_low, "tok", axis=0, tiled=True)
    modulation_low = modulation_weight.astype(bf16)
    modulation_part = jnp.dot(
        condition_group, modulation_low, preferred_element_type=f32
    ) + modulation_bias.astype(bf16).astype(f32)
    modulation = lax.all_to_all(modulation_part, "tok", split_axis=0, concat_axis=1, tiled=True)
    mod = modulation.reshape(6, width)

    routed = lax.all_to_all(
        kept_tokens.astype(bf16), "tok", split_axis=0, concat_axis=1, tiled=True
    )[0]

    small_parts = [mask_token, query_bias, value_bias, output_bias, down_bias, up_bias]
    small_widths = [part.shape[0] for part in small_parts]
    cuts = [sum(small_widths[:number]) for number in range(len(small_widths) + 1)]
    small_rows = position_rows // 8
    table_rows = position_rows + small_rows
    table_half = table_rows // 2

    def as_rows(parts):
        flat = jnp.concatenate(parts, axis=-1)
        lead = flat.shape[:-1]
        flat = jnp.pad(flat, [(0, 0)] * len(lead) + [(0, small_rows * width - flat.shape[-1])])
        return flat.reshape(lead + (small_rows, width))

    table_shard = jnp.concatenate([position_table, as_rows(small_parts)]).astype(bf16)
    table_mine = gather_blocks(
        lax.dynamic_slice_in_dim(table_shard, core * table_half, table_half, 0)[None]
    )[0].reshape(tok_count, table_half, width)
    table_other = swap_core(table_mine)
    table = jnp.concatenate(
        [by_core(table_mine, table_other), by_core(table_other, table_mine)], axis=1
    )
    position = table[:, :position_rows].reshape(seq_len, width)
    small = table[:, position_rows:].reshape(tok_count, -1)
    mask_full, query_bias_full, value_bias_full, output_bias_full, down_bias_full = (
        small[:, cuts[number] : cuts[number + 1]].reshape(1, width).astype(f32)
        for number in range(5)
    )
    up_bias_full = (
        small[:, cuts[5] : cuts[6]].reshape(tok_count, 4, share).transpose(1, 0, 2).reshape(4, 1, width)
    ).astype(f32)
    up_bias_here = jnp.concatenate(
        [by_core(up_bias_full[:2], up_bias_full[2:]), by_core(up_bias_full[2:], up_bias_full[:2])]
    )

    input_low = input_weight.astype(bf16)
    input_blocks = [input_low[:, number * width : (number + 1) * width] for number in range(3)]
    attention_blocks = jnp.stack(input_blocks + [output_weight.astype(bf16)])
    up_blocks = up_weight.astype(bf16).reshape(share, tok_count, 4, share).transpose(2, 0, 1, 3)
    up_blocks = up_blocks.reshape(4, share, width)
    down_blocks = down_weight.astype(bf16).reshape(4, share, width)
    attention_mine = gather_blocks(by_core(attention_blocks[:2], attention_blocks[2:]))
    attention_other = swap_core(attention_mine)
    up_mine = gather_blocks(by_core(up_blocks[:2], up_blocks[2:]))
    up_other = swap_core(up_mine)
    down_mine = gather_blocks(by_core(down_blocks[:2], down_blocks[2:]))
    down_other = swap_core(down_mine)

    start, norm_one = start_call(kept_count, kept_index, routed, position, mask_full, mod)
    blank = jnp.zeros_like(query_bias_full)
    projected_bias = jnp.stack([query_bias_full, blank, value_bias_full])
    projected = project_call(core_row, norm_one, attention_mine, attention_other, projected_bias)
    mix, logs = attend_call(projected)
    joined, branch_one, middle, norm_two = mix_call(
        core_row, mix, start, attention_mine, attention_other, output_bias_full, mod
    )
    (
        block_output,
        hidden,
        pre_grad,
        grad_two,
        middle_grad,
        grad_one,
        feed_sums,
        up_bias_sum,
    ) = feed_call(
        norm_two, middle, cotangent[0], branch_one, mod, up_bias_here, down_bias_full, up_mine, up_other,
        down_mine, down_other,
    )
    feed_other = feed_weight_call(norm_two, pre_grad, hidden, grad_two, 2)
    feed_mine = feed_weight_call(norm_two, pre_grad, hidden, grad_two, 0)
    feed_shard = scatter_blocks(feed_mine, feed_other)
    mix_grad = mix_grad_call(core_row, grad_one, attention_mine, attention_other)
    query_grad, key_grad, value_grad = attend_back_call(projected, mix, logs, mix_grad)
    projected_grad, row_grad, slot_grad, start_sums = start_back_call(
        core_row, kept_count, kept_index, query_grad, key_grad, value_grad, attention_mine,
        attention_other, middle_grad, start, mod,
    )
    pair = jnp.arange(2, dtype=jnp.int32)
    attention_shard = scatter_blocks(
        attention_weight_call(pair + 2 * core, norm_one, joined, projected_grad, grad_one),
        attention_weight_call(pair + 2 * (1 - core), norm_one, joined, projected_grad, grad_one),
    )
    kept_grad = lax.all_to_all(
        slot_grad[None], "tok", split_axis=1, concat_axis=0, tiled=True
    ).astype(f32)

    up_sums = jnp.concatenate(
        [by_core(up_bias_sum[:2], up_bias_sum[2:]), by_core(up_bias_sum[2:], up_bias_sum[:2])]
    )
    up_sums = up_sums.reshape(4, tok_count, share).transpose(1, 0, 2).reshape(tok_count, -1)
    rows_of = lambda row: row.reshape(tok_count, -1)
    small_grads = as_rows(
        [
            rows_of(start_sums[4]),
            rows_of(start_sums[0]),
            rows_of(start_sums[1]),
            rows_of(feed_sums[5]),
            rows_of(feed_sums[1]),
            up_sums,
        ]
    ).astype(bf16)
    table_grad = jnp.concatenate(
        [row_grad.reshape(tok_count, position_rows, width), small_grads], axis=1
    )
    halves = [
        table_grad[:, :table_half].reshape(1, -1, width),
        table_grad[:, table_half:].reshape(1, -1, width),
    ]
    table_shard_grad = scatter_blocks(by_core(halves[0], halves[1]), by_core(halves[1], halves[0]))[0]

    def both_cores(shard):
        got = swap_core(shard)
        return by_core(shard, got).astype(f32), by_core(got, shard).astype(f32)

    table_total = jnp.concatenate(both_cores(table_shard_grad))
    position_total = table_total[:position_rows]
    small_total = table_total[position_rows:].reshape(-1)
    (
        mask_total,
        query_bias_total,
        value_bias_total,
        output_bias_total,
        down_bias_total,
        up_bias_total,
    ) = (small_total[cuts[number] : cuts[number + 1]] for number in range(6))
    first, second = both_cores(attention_shard)
    input_total = jnp.concatenate([first[0], first[1], second[0]], axis=1)
    output_total = second[1]
    first, second = both_cores(feed_shard)
    up_total = jnp.concatenate([first[:2], second[:2]]).reshape(4, share, tok_count, share)
    up_total = up_total.transpose(1, 2, 0, 3).reshape(share, -1)
    down_total = jnp.concatenate([first[2:], second[2:]]).reshape(-1, width)

    modulation_grad = jnp.concatenate(
        [start_sums[3], start_sums[2], feed_sums[4], feed_sums[3], feed_sums[2], feed_sums[0]]
    ).astype(bf16)[None]
    condition_all = lax.all_gather(condition_group, "grp", axis=0, tiled=True)
    modulation_grad_group = lax.all_to_all(
        modulation_grad, "tok", split_axis=1, concat_axis=0, tiled=True
    )
    modulation_grad_all = lax.all_gather(modulation_grad_group, "grp", axis=0, tiled=True)
    modulation_total = jnp.einsum(
        "id,ie->de", condition_all, modulation_grad_all, preferred_element_type=f32
    )
    modulation_bias_total = jnp.sum(modulation_grad_all.astype(f32), axis=0)
    condition_part = jnp.einsum(
        "ie,de->id", modulation_grad_group, modulation_low, preferred_element_type=f32
    )
    condition_low_grad = jnp.sum(
        lax.all_to_all(condition_part, "tok", split_axis=0, concat_axis=0, tiled=True),
        axis=0,
        keepdims=True,
    )
    _, silu_back = jax.vjp(jax.nn.silu, condition)
    condition_grad = silu_back(condition_low_grad)[0]
    return (
        block_output[None],
        kept_grad,
        condition_grad,
        mask_total,
        position_total,
        modulation_total,
        modulation_bias_total,
        input_total,
        query_bias_total,
        value_bias_total,
        output_total,
        output_bias_total,
        up_total,
        up_bias_total,
        down_total,
        down_bias_total,
    )


def solution(mesh):
    return jax.shard_map(
        on_device,
        mesh=mesh,
        in_specs=(
            P("grp", "tok", None),
            P(("grp", "tok"), None),
            P(("grp", "tok")),
            P(("grp", "tok"), None),
            P("tok"),
            P("tok", None),
            P(None, "tok"),
            P("tok"),
            P("tok", None),
            P("tok"),
            P("tok"),
            P("tok", None),
            P("tok"),
            P("tok", None),
            P("tok"),
            P("tok", None),
            P("tok"),
            P(("grp", "tok"), None, None),
        ),
        out_specs=(
            P(("grp", "tok"), None, None),
            P("grp", "tok", None),
            P(("grp", "tok"), None),
            P("tok"),
            P("tok", None),
            P(None, "tok"),
            P("tok"),
            P("tok", None),
            P("tok"),
            P("tok"),
            P("tok", None),
            P("tok"),
            P("tok", None),
            P("tok"),
            P("tok", None),
            P("tok"),
        ),
        check_vma=False,
    )
```

```python
import functools
import math

import jax
import jax.numpy as jnp
from jax import lax
from jax.experimental import pallas as pl
from jax.experimental.pallas import tpu as pltpu
from jax.sharding import PartitionSpec as P

H = 16
HD = 72
LANES = 128

epsilon = 1e-06
f32 = jnp.float32
bf16 = jnp.bfloat16
plain = (((1,), (0,)), ((), ()))
right_turned = (((1,), (1,)), ((), ()))
left_turned = (((0,), (0,)), ((), ()))
vmem_limit = 60 << 20


def product(left, right, dims=plain):
    return lax.dot_general(left, right, dims, preferred_element_type=f32)


def whole_block(array):
    zeros = (0,) * array.ndim
    return pl.BlockSpec(array.shape, lambda *_: zeros)


def row_block(rows, *rest):
    return pl.BlockSpec((rows,) + rest, lambda i: (i,) + (0,) * len(rest))


smem = pl.BlockSpec(memory_space=pltpu.SMEM)
anywhere = pl.BlockSpec(memory_space=pl.ANY)


def params():
    return pltpu.CompilerParams(vmem_limit_bytes=vmem_limit)


def cost(flops, moved, exps=0):
    return pl.CostEstimate(flops=int(flops), bytes_accessed=int(moved), transcendentals=int(exps))


def column_sum(values):
    return jnp.sum(values, axis=0, keepdims=True)


def normalize(values):
    center = values - jnp.mean(values, axis=-1, keepdims=True)
    spread = jnp.mean(center * center, axis=-1, keepdims=True)
    inverse = lax.rsqrt(spread + epsilon)
    return center * inverse, inverse


def normalize_back(grad, unit, inverse, scale):
    scaled = grad * (1.0 + scale)
    first = jnp.mean(scaled, axis=-1, keepdims=True)
    second = jnp.mean(scaled * unit, axis=-1, keepdims=True)
    return (scaled - first - unit * second) * inverse


def start_kernel(core_ref, places_ref, count_ref, index_ref, kept_ref, mask_ref, mod_ref, *rest, chunks, row, share):
    refs, (start_ref, norm_ref, table, sems) = rest[: len(chunks.arrays)], rest[len(chunks.arrays) :]
    rows, slots = start_ref.shape[0], kept_ref.shape[0]
    step = pl.program_id(0)
    low, high = table.at[:, :share], table.at[:, share:]

    @pl.when(step == 0)
    def _():
        @pl.when(core_ref[0] == 0)
        def _():
            chunks.load(refs, places_ref, True, row, low, sems.at[0])
            chunks.load(refs, places_ref, False, row, high, sems.at[1])

        @pl.when(core_ref[0] != 0)
        def _():
            chunks.load(refs, places_ref, False, row, low, sems.at[0])
            chunks.load(refs, places_ref, True, row, high, sems.at[1])

        wait_block(low, sems.at[0])
        wait_block(high, sems.at[1])

    base = step * rows
    here = lax.broadcasted_iota(jnp.int32, (rows, slots), 0) + base
    slot = lax.broadcasted_iota(jnp.int32, (rows, slots), 1)
    chosen = jnp.where((index_ref[...] == here) & (slot < count_ref[0]), 1.0, 0.0)
    filled = product(chosen.astype(bf16), kept_ref[...])
    empty = 1.0 - jnp.sum(chosen, axis=1, keepdims=True)
    groups_here = rows // table.shape[1]
    position = table[pl.ds(step * groups_here, groups_here)].reshape(rows, -1)
    start = filled + empty * mask_ref[...] + position.astype(f32)
    start_ref[...] = start
    unit, _ = normalize(start)
    norm_ref[...] = (unit * (1.0 + mod_ref[1:2]) + mod_ref[0:1]).astype(bf16)


def start_call(core, places, count, index, kept, mask, mod, chunks, row, share, seq_len):
    width = kept.shape[1]
    rows = seq_len // 4
    return pl.pallas_call(
        functools.partial(start_kernel, chunks=chunks, row=row, share=share),
        grid=(4,),
        in_specs=[
            smem,
            smem,
            smem,
            whole_block(index),
            whole_block(kept),
            whole_block(mask),
            whole_block(mod),
        ]
        + chunks.specs,
        out_specs=[row_block(rows, width)] * 2,
        out_shape=[
            jax.ShapeDtypeStruct((seq_len, width), f32),
            jax.ShapeDtypeStruct((seq_len, width), bf16),
        ],
        scratch_shapes=[
            pltpu.VMEM((8, seq_len // 8, width), bf16),
            pltpu.SemaphoreType.DMA((2,)),
        ],
        compiler_params=params(),
        cost_estimate=cost(2 * seq_len * width * kept.shape[0], 14 * seq_len * width),
    )(core, places, count, index, kept, mask, mod, *chunks.arrays)


class Chunks:
    def __init__(self, mine, other):
        self.arrays = list(mine) + list(other)
        self.counts = [array.shape[0] for array in mine]
        self.specs = [anywhere] * len(self.arrays)

    def load(self, refs, places_ref, from_mine, row, target, sem):
        count = len(self.counts)
        rows = pl.ds(row, target.shape[1])
        place = 0
        for ref, size in zip(refs[:count] if from_mine else refs[count:], self.counts):
            for index in range(size):
                pltpu.make_async_copy(
                    ref.at[index, rows], target.at[places_ref[place]], sem
                ).start()
                place += 1

    def load_block(self, refs, places_ref, core_ref, block, target, sem, first=0):
        owner, row = block // 2, (first + block % 2) * target.shape[1]

        @pl.when(core_ref[0] == owner)
        def _():
            self.load(refs, places_ref, True, row, target, sem)

        @pl.when(core_ref[0] != owner)
        def _():
            self.load(refs, places_ref, False, row, target, sem)


def wait_block(target, sem):
    pltpu.make_async_copy(target, target, sem).wait()


def square(weight):
    return weight.reshape(-1, weight.shape[-1])


def split_heads(values, store):
    rows = values.shape[0]
    blank = jnp.zeros((rows, LANES - HD), values.dtype)
    for head in range(H):
        store(head, jnp.concatenate([values[:, head * HD : (head + 1) * HD], blank], axis=1))


def project_kernel(core_ref, places_ref, norm_ref, bias_ref, *rest, chunks):
    refs, (out_ref, weight, sems) = rest[: len(chunks.arrays)], rest[len(chunks.arrays) :]
    step = pl.program_id(0)

    @pl.when(step == 0)
    def _():
        for block in range(3):
            chunks.load_block(refs, places_ref, core_ref, block, weight.at[block], sems.at[block])

    wait_block(weight.at[step], sems.at[step])
    half = norm_ref.shape[0] // 2
    for part in range(2):
        rows = slice(part * half, (part + 1) * half)
        result = product(norm_ref[rows], square(weight[step])) + bias_ref[0]

        def store(head, value):
            out_ref[0, head, rows] = value

        split_heads(result.astype(bf16), store)


def project_call(core, places, norm, bias, chunks):
    seq_len, width = norm.shape
    return pl.pallas_call(
        functools.partial(project_kernel, chunks=chunks),
        grid=(3,),
        in_specs=[
            smem,
            smem,
            whole_block(norm),
            pl.BlockSpec((1, 1, width), lambda i: (i, 0, 0)),
        ]
        + chunks.specs,
        out_specs=pl.BlockSpec((1, H, seq_len, LANES), lambda i: (i, 0, 0, 0)),
        out_shape=jax.ShapeDtypeStruct((3, H, seq_len, LANES), bf16),
        scratch_shapes=[
            pltpu.VMEM((3, 8, width // 8, width), bf16),
            pltpu.SemaphoreType.DMA((3,)),
        ],
        compiler_params=params(),
        cost_estimate=cost(6 * seq_len * width * width, 12 * seq_len * width + 6 * width * width),
    )(core, places, norm, bias, *chunks.arrays)


def attend_kernel(query_ref, key_ref, value_ref, mix_ref, log_ref, *, size, factor):
    turned_value = value_ref[0, 0].T
    for part in range(query_ref.shape[2] // size):
        rows = slice(part * size, (part + 1) * size)
        scores = product(key_ref[0, 0], query_ref[0, 0, rows], right_turned)
        top = jnp.max(scores, axis=0, keepdims=True)
        weights = jnp.exp2((scores - top) * factor)
        total = jnp.sum(weights, axis=0, keepdims=True)
        mix = product(turned_value, weights.astype(bf16))
        mix_ref[0, rows] = (mix / total).T.astype(bf16)
        log_ref[0, :, rows] = top * factor + jnp.log2(total)


groups = 4


def head_block(place, seq_len, group):
    first = group * (H // groups)
    return pl.BlockSpec((1, 1, seq_len, LANES), lambda h: (place, first + h, 0, 0))


def attend_call(projected, group):
    seq_len = projected.shape[2]
    heads = H // groups
    flat = pl.BlockSpec((1, seq_len, LANES), lambda h: (h, 0, 0))
    return pl.pallas_call(
        functools.partial(
            attend_kernel, size=seq_len, factor=math.log2(math.e) / math.sqrt(HD)
        ),
        grid=(heads,),
        in_specs=[head_block(place, seq_len, group) for place in range(3)],
        out_specs=[flat, pl.BlockSpec((1, 1, seq_len), lambda h: (h, 0, 0))],
        out_shape=[
            jax.ShapeDtypeStruct((heads, seq_len, LANES), bf16),
            jax.ShapeDtypeStruct((heads, 1, seq_len), f32),
        ],
        compiler_params=params(),
        cost_estimate=cost(4 * heads * seq_len * seq_len * 256, 8 * heads * seq_len * LANES, heads * seq_len * seq_len),
    )(projected, projected, projected)


def attend_back_kernel(
    query_ref, key_ref, value_ref, mix_ref, log_ref, grad_ref, query_grad_ref, key_grad_ref,
    value_grad_ref, key_sum, value_sum, *, size, factor
):
    key, value = key_ref[0, 0], value_ref[0, 0]
    turned_key = key.T
    base_two = factor * math.log2(math.e)
    for part in range(query_ref.shape[2] // size):
        rows = slice(part * size, (part + 1) * size)
        query, grad = query_ref[0, 0, rows], grad_ref[0, rows]
        scores = product(key, query, right_turned)
        weights = jnp.exp2(scores * base_two - log_ref[0, :, rows])
        value_part = product(weights.astype(bf16), grad)
        weight_grad = product(value, grad, right_turned)
        inner = column_sum((grad.astype(f32) * mix_ref[0, rows].astype(f32)).T)
        score_grad = (weights * (weight_grad - inner)).astype(bf16)
        key_part = product(score_grad, query)
        query_grad_ref[0, rows] = (product(turned_key, score_grad) * factor).T.astype(bf16)
        if part == 0:
            key_sum[...] = key_part
            value_sum[...] = value_part
        else:
            key_sum[...] += key_part
            value_sum[...] += value_part
    key_grad_ref[0] = (key_sum[...] * factor).astype(bf16)
    value_grad_ref[0] = value_sum[...].astype(bf16)


def attend_back_call(projected, mix, logs, grad, group):
    seq_len = projected.shape[2]
    heads = H // groups
    first = group * heads
    flat = pl.BlockSpec((1, seq_len, LANES), lambda h: (h, 0, 0))
    return pl.pallas_call(
        functools.partial(attend_back_kernel, size=seq_len // 2, factor=1.0 / math.sqrt(HD)),
        grid=(heads,),
        in_specs=[head_block(place, seq_len, group) for place in range(3)]
        + [
            flat,
            pl.BlockSpec((1, 1, seq_len), lambda h: (h, 0, 0)),
            pl.BlockSpec((1, seq_len, LANES), lambda h: (first + h, 0, 0)),
        ],
        out_specs=[flat] * 3,
        out_shape=[jax.ShapeDtypeStruct((heads, seq_len, LANES), bf16)] * 3,
        scratch_shapes=[pltpu.VMEM((seq_len, LANES), f32)] * 2,
        compiler_params=params(),
        cost_estimate=cost(10 * heads * seq_len * seq_len * 256, 16 * heads * seq_len * LANES, heads * seq_len * seq_len),
    )(projected, projected, projected, mix, logs, grad)


def join_heads(refs):
    return jnp.concatenate(
        [ref[head][:, :HD] for ref in refs for head in range(ref.shape[0])], axis=1
    )


def mix_kernel(core_ref, places_ref, start_ref, bias_ref, mod_ref, *rest, chunks):
    mix_refs, rest = rest[:groups], rest[groups:]
    refs, rest = rest[: len(chunks.arrays)], rest[len(chunks.arrays) :]
    joined_ref, branch_ref, middle_ref, norm_ref, weight, sem = rest

    @pl.when(pl.program_id(0) == 0)
    def _():
        chunks.load_block(refs, places_ref, core_ref, 3, weight, sem)
        wait_block(weight, sem)

    joined = join_heads(mix_refs)
    joined_ref[...] = joined
    branch = product(joined, square(weight[...])) + bias_ref[...]
    branch_ref[...] = branch
    middle = start_ref[...] + mod_ref[2:3] * branch
    middle_ref[...] = middle
    unit, _ = normalize(middle)
    norm_ref[...] = (unit * (1.0 + mod_ref[4:5]) + mod_ref[3:4]).astype(bf16)


def mix_call(core, places, mix, start, bias, mod, chunks):
    seq_len, width = start.shape
    rows = seq_len // 4
    block = row_block(rows, width)
    return pl.pallas_call(
        functools.partial(mix_kernel, chunks=chunks),
        grid=(4,),
        in_specs=[smem, smem, block, whole_block(bias), whole_block(mod)]
        + [pl.BlockSpec((H // groups, rows, LANES), lambda i: (0, i, 0))] * groups
        + chunks.specs,
        out_specs=[block] * 4,
        out_shape=[
            jax.ShapeDtypeStruct((seq_len, width), kind) for kind in (bf16, f32, f32, bf16)
        ],
        scratch_shapes=[pltpu.VMEM((8, width // 8, width), bf16), pltpu.SemaphoreType.DMA],
        compiler_params=params(),
        cost_estimate=cost(2 * seq_len * width * width, 18 * seq_len * width),
    )(core, places, start, bias, mod, *mix, *chunks.arrays)


def gelu_parts(values):
    inner = 0.7978845608028654 * (values + 0.044715 * values * values * values)
    turned = jnp.tanh(inner)
    half = 0.5 * (1.0 + turned)
    slope = half + 0.5 * values * (1.0 - turned * turned) * (
        0.7978845608028654 * (1.0 + 0.134145 * values * values)
    )
    return values * half, slope


def feed_kernel(
    core_ref, places_ref, norm_ref, middle_ref, cot_ref, branch_ref, mod_ref, up_bias_ref, down_bias_ref,
    *rest, source
):
    refs, rest = rest[: len(source.arrays)], rest[len(source.arrays) :]
    (
        out_ref, hidden_ref, pre_ref, grad_two_ref, middle_grad_ref, grad_one_ref, sums_ref,
        up_sums_ref, up, down, slopes, sems,
    ) = rest
    step = pl.program_id(0)
    chunks = 4

    @pl.when(step == 0)
    def _():
        for chunk in range(chunks):
            for side, target in enumerate((up, down)):
                source.load_block(
                    refs, places_ref, core_ref, chunk, target.at[chunk], sems.at[side, chunk], 2 * side
                )
        sums_ref[...] = jnp.zeros_like(sums_ref)
        up_sums_ref[...] = jnp.zeros_like(up_sums_ref)

    norm = norm_ref[...]
    total = None
    for chunk in range(chunks):

        @pl.when(step == 0)
        def _():
            wait_block(up.at[chunk], sems.at[0, chunk])
            wait_block(down.at[chunk], sems.at[1, chunk])

        before = product(norm, square(up[chunk])) + up_bias_ref[chunk]
        hidden, slope = gelu_parts(before)
        hidden = hidden.astype(bf16)
        hidden_ref[chunk] = hidden
        slopes[chunk] = slope.astype(slopes.dtype)
        part = product(hidden, square(down[chunk]))
        total = part if total is None else total + part
    branch_two = total + down_bias_ref[...]
    middle, cot = middle_ref[...], cot_ref[...]
    gate_two = mod_ref[5:6]
    out_ref[...] = middle + gate_two * branch_two
    grad_two = (gate_two * cot).astype(bf16)
    grad_two_ref[...] = grad_two
    sums_ref[0:1] += column_sum(cot * branch_two)
    sums_ref[1:2] += column_sum(grad_two.astype(f32))
    total = None
    for chunk in range(chunks):
        pre = (product(grad_two, square(down[chunk]), right_turned) * slopes[chunk].astype(f32)).astype(bf16)
        pre_ref[chunk] = pre
        up_sums_ref[chunk] += column_sum(pre.astype(f32))
        part = product(pre, square(up[chunk]), right_turned)
        total = part if total is None else total + part
    unit, inverse = normalize(middle)
    sums_ref[2:3] += column_sum(total * unit)
    sums_ref[3:4] += column_sum(total)
    middle_grad = cot + normalize_back(total, unit, inverse, mod_ref[4:5])
    middle_grad_ref[...] = middle_grad
    sums_ref[4:5] += column_sum(middle_grad * branch_ref[...])
    grad_one = (mod_ref[2:3] * middle_grad).astype(bf16)
    grad_one_ref[...] = grad_one
    sums_ref[5:6] += column_sum(grad_one.astype(f32))


def feed_call(core, places, norm, middle, cot, branch, mod, up_bias, down_bias, source):
    seq_len, width = middle.shape
    steps = 4
    rows = seq_len // steps
    block = row_block(rows, width)
    chunked = pl.BlockSpec((4, rows, width), lambda i: (0, i, 0))
    wide = jax.ShapeDtypeStruct((4, seq_len, width), bf16)
    return pl.pallas_call(
        functools.partial(feed_kernel, source=source),
        grid=(steps,),
        in_specs=[
            smem,
            smem,
            block,
            block,
            block,
            block,
            whole_block(mod),
            whole_block(up_bias),
            whole_block(down_bias),
        ]
        + source.specs,
        out_specs=[
            block,
            chunked,
            chunked,
            block,
            block,
            block,
            pl.BlockSpec((8, width), lambda i: (0, 0)),
            pl.BlockSpec((4, 1, width), lambda i: (0, 0, 0)),
        ],
        out_shape=[
            jax.ShapeDtypeStruct((seq_len, width), f32),
            wide,
            wide,
            jax.ShapeDtypeStruct((seq_len, width), bf16),
            jax.ShapeDtypeStruct((seq_len, width), f32),
            jax.ShapeDtypeStruct((seq_len, width), bf16),
            jax.ShapeDtypeStruct((8, width), f32),
            jax.ShapeDtypeStruct((4, 1, width), f32),
        ],
        scratch_shapes=[
            pltpu.VMEM((4, 8, width // 8, width), bf16),
            pltpu.VMEM((4, 8, width // 8, width), bf16),
            pltpu.VMEM((4, rows, width), f32),
            pltpu.SemaphoreType.DMA((2, 4)),
        ],
        compiler_params=params(),
        cost_estimate=cost(32 * seq_len * width * width, 60 * seq_len * width, 4 * seq_len * width),
    )(core, places, norm, middle, cot, branch, mod, up_bias, down_bias, *source.arrays)


def feed_weight_kernel(first_ref, norm_ref, pre_ref, hidden_ref, grad_ref, out_ref):
    step = pl.program_id(0)

    @pl.when(step < 2)
    def _():
        result = product(norm_ref[...], pre_ref[0], left_turned)
        out_ref[...] = result.astype(bf16).reshape(out_ref.shape)

    @pl.when(step >= 2)
    def _():
        result = product(hidden_ref[0], grad_ref[...], left_turned)
        out_ref[...] = result.astype(bf16).reshape(out_ref.shape)


def feed_weight_call(first, norm, pre, hidden, grad):
    seq_len, width = norm.shape
    block = (1, seq_len, width)
    full = pl.BlockSpec((seq_len, width), lambda i, f: (0, 0))
    return pl.pallas_call(
        feed_weight_kernel,
        grid_spec=pltpu.PrefetchScalarGridSpec(
            num_scalar_prefetch=1,
            grid=(4,),
            in_specs=[
                full,
                pl.BlockSpec(block, lambda i, f: (f[0] + jnp.minimum(i, 1), 0, 0)),
                pl.BlockSpec(block, lambda i, f: (f[0] + jnp.maximum(i - 2, 0), 0, 0)),
                full,
            ],
            out_specs=pl.BlockSpec((8, width // 8, width), lambda i, f: (0, i, 0)),
        ),
        out_shape=jax.ShapeDtypeStruct((8, width // 2, width), bf16),
        compiler_params=params(),
        cost_estimate=cost(8 * seq_len * width * width, 12 * seq_len * width + 8 * width * width),
    )(first, norm, pre, hidden, grad)


def attention_weight_kernel(owner_ref, norm_ref, joined_ref, grad_ref, *rest):
    head_refs = [rest[block * groups : (block + 1) * groups] for block in range(3)]
    out_ref, left, heads, right, sems = rest[3 * groups :]
    step = pl.program_id(0)
    size = heads.shape[1] // groups

    def copies(block, slot):
        if block == 3:
            return [(joined_ref, left.at[slot]), (grad_ref, right.at[slot])]
        return [(norm_ref, left.at[slot])] + [
            (ref, heads.at[slot, pl.ds(group * size, size)])
            for group, ref in enumerate(head_refs[block])
        ]

    @pl.when(step == 0)
    def _():
        for block in range(4):

            @pl.when(owner_ref[0] == block // 2)
            def _():
                for source, target in copies(block, block % 2):
                    pltpu.make_async_copy(source, target, sems.at[block % 2]).start()

    for block in range(4):

        @pl.when((owner_ref[0] == block // 2) & (step == block % 2))
        def _():
            slot = block % 2
            wait_block(left.at[slot], sems.at[slot])
            if block == 3:
                wait_block(right.at[slot], sems.at[slot])
            else:
                wait_block(heads.at[slot], sems.at[slot])
                right[slot] = jnp.concatenate(
                    [heads[slot, head][:, :HD] for head in range(H)], axis=1
                )

    result = product(left[step], right[step], left_turned)
    out_ref[...] = result.astype(bf16).reshape(out_ref.shape)


def attention_weight_call(owner, norm, joined, grad_one, grads):
    seq_len, width = norm.shape
    return pl.pallas_call(
        attention_weight_kernel,
        grid=(2,),
        in_specs=[smem] + [anywhere] * (3 + 3 * groups),
        out_specs=pl.BlockSpec((8, width // 8, width), lambda i: (0, i, 0)),
        out_shape=jax.ShapeDtypeStruct((8, width // 4, width), bf16),
        scratch_shapes=[
            pltpu.VMEM((2, seq_len, width), bf16),
            pltpu.VMEM((2, H, seq_len, LANES), bf16),
            pltpu.VMEM((2, seq_len, width), bf16),
            pltpu.SemaphoreType.DMA((2,)),
        ],
        compiler_params=params(),
        cost_estimate=cost(4 * seq_len * width * width, 10 * seq_len * width + 4 * width * width),
    )(owner, norm, joined, grad_one, *grads)


def mix_grad_kernel(core_ref, places_ref, grad_ref, *rest, chunks):
    refs, (out_ref, weight, sem) = rest[: len(chunks.arrays)], rest[len(chunks.arrays) :]

    @pl.when(pl.program_id(0) == 0)
    def _():
        chunks.load_block(refs, places_ref, core_ref, 3, weight, sem)
        wait_block(weight, sem)

    def store(head, value):
        out_ref[head] = value

    split_heads(product(grad_ref[...], square(weight[...]), right_turned).astype(bf16), store)


def mix_grad_call(core, places, grad_one, chunks):
    seq_len, width = grad_one.shape
    rows = seq_len // 2
    return pl.pallas_call(
        functools.partial(mix_grad_kernel, chunks=chunks),
        grid=(2,),
        in_specs=[smem, smem, row_block(rows, width)] + chunks.specs,
        out_specs=pl.BlockSpec((H, rows, LANES), lambda i: (0, i, 0)),
        out_shape=jax.ShapeDtypeStruct((H, seq_len, LANES), bf16),
        scratch_shapes=[pltpu.VMEM((8, width // 8, width), bf16), pltpu.SemaphoreType.DMA],
        compiler_params=params(),
        cost_estimate=cost(2 * seq_len * width * width, 8 * seq_len * width),
    )(core, places, grad_one, *chunks.arrays)


def start_back_kernel(
    core_ref, places_ref, count_ref, index_row_ref, index_ref, middle_grad_ref, start_ref, mod_ref,
    *rest, chunks, first
):
    grad_refs = [rest[block * groups : (block + 1) * groups] for block in range(3)]
    rest = rest[3 * groups :]
    refs, rest = rest[: len(chunks.arrays)], rest[len(chunks.arrays) :]
    row_grad_ref, slot_ref, sums_ref, weight, slots, sems = rest
    step = pl.program_id(0)
    rows, width = start_ref.shape
    slot_count = slots.shape[0]

    @pl.when(step == 0)
    def _():
        for block in range(3):
            chunks.load_block(refs, places_ref, core_ref, block, weight.at[block], sems.at[block])
        sums_ref[...] = jnp.zeros_like(sums_ref)

    total = None
    for block, refs in enumerate(grad_refs):
        joined = join_heads(refs)
        if block != 1:
            place = block // 2
            sums_ref[place : place + 1] += column_sum(joined.astype(f32))

        @pl.when(step == 0)
        def _():
            wait_block(weight.at[block], sems.at[block])

        part = product(joined, square(weight[block]), right_turned)
        total = part if total is None else total + part
    unit, inverse = normalize(start_ref[...])
    sums_ref[2:3] += column_sum(total * unit)
    sums_ref[3:4] += column_sum(total)
    row_grad = middle_grad_ref[...] + normalize_back(total, unit, inverse, mod_ref[1:2])
    row_low = row_grad.astype(bf16)
    row_grad_ref[...] = row_low
    base = (first + step) * rows
    place = lax.broadcasted_iota(jnp.int32, (slot_count, rows), 1) + base
    slot = lax.broadcasted_iota(jnp.int32, (slot_count, rows), 0)
    chosen = jnp.where((index_ref[...] == place) & (slot < count_ref[0]), 1.0, 0.0)
    part = product(chosen.astype(bf16), row_low)

    @pl.when(step == 0)
    def _():
        slots[...] = part

    @pl.when(step > 0)
    def _():
        slots[...] += part

    here = lax.broadcasted_iota(jnp.int32, (rows, slot_count), 0) + base
    lane = lax.broadcasted_iota(jnp.int32, (rows, slot_count), 1)
    taken = jnp.where((index_row_ref[...] == here) & (lane < count_ref[0]), 1.0, 0.0)
    empty = 1.0 - jnp.sum(taken, axis=1, keepdims=True)
    sums_ref[4:5] += column_sum(row_grad * empty)

    @pl.when(step == pl.num_programs(0) - 1)
    def _():
        slot_ref[...] = slots[...].astype(bf16)


def start_back_call(half, core, places, count, index, grads, middle_grad, start, mod, chunks):
    seq_len, width = start.shape
    slot_count = index.shape[1]
    steps = 2
    rows = seq_len // 4
    first = half * steps
    heads = pl.BlockSpec((H // groups, rows, LANES), lambda i: (0, first + i, 0))
    block = pl.BlockSpec((rows, width), lambda i: (first + i, 0))
    column = index.reshape(slot_count, 1)
    return pl.pallas_call(
        functools.partial(start_back_kernel, chunks=chunks, first=first),
        grid=(steps,),
        in_specs=[
            smem,
            smem,
            smem,
            whole_block(index),
            whole_block(column),
            block,
            block,
            whole_block(mod),
        ]
        + [heads] * (3 * groups)
        + chunks.specs,
        out_specs=[
            row_block(rows, width),
            pl.BlockSpec((slot_count, width), lambda i: (0, 0)),
            pl.BlockSpec((8, width), lambda i: (0, 0)),
        ],
        out_shape=[
            jax.ShapeDtypeStruct((seq_len // 2, width), bf16),
            jax.ShapeDtypeStruct((slot_count, width), bf16),
            jax.ShapeDtypeStruct((8, width), f32),
        ],
        scratch_shapes=[
            pltpu.VMEM((3, 8, width // 8, width), bf16),
            pltpu.VMEM((slot_count, width), f32),
            pltpu.SemaphoreType.DMA((3,)),
        ],
        compiler_params=params(),
        cost_estimate=cost(4 * seq_len * width * width, 13 * seq_len * width),
    )(core, places, count, index, column, middle_grad, start, mod, *grads, *chunks.arrays)


def swap_pairs(size, bit):
    return [(place, place ^ bit) for place in range(size)]


def swap_core(values):
    return lax.ppermute(values, "grp", swap_pairs(lax.axis_size("grp"), 1))


def add_low(*parts):
    total = parts[0].astype(f32)
    for part in parts[1:]:
        total = total + part.astype(f32)
    return total.astype(bf16)


def swap_x(values):
    return lax.ppermute(values, "grp", swap_pairs(lax.axis_size("grp"), 2))


class Ring:
    def __init__(self):
        size = lax.axis_size("tok")
        self.size = size
        order = list(range(0, size, 2)) + list(range(1, size, 2))[::-1]
        self.ahead = [(order[i], order[(i + 1) % size]) for i in range(size)]
        self.behind = [(after, before) for before, after in self.ahead]
        tok = lax.axis_index("tok")
        self.place = jnp.where(tok % 2 == 0, tok // 2, size - 1 - tok // 2)
        self.x_bit = (lax.axis_index("grp") // 2) % 2

    def tok_at(self, distance):
        place = (self.place + distance) % self.size
        return jnp.where(place < self.size // 2, 2 * place, 2 * (self.size - 1 - place) + 1)

    def forward(self, values):
        return lax.ppermute(values, "tok", self.ahead)

    def backward(self, values):
        return lax.ppermute(values, "tok", self.behind)


def sync(*values):
    return lax.optimization_barrier(values)


class Gather:
    def __init__(self, ring, mine, other, part, middle):
        self.ring, self.part, self.middle = ring, part, middle
        self.mine, self.other = [mine[None]], [other[None]]
        payload = lax.dynamic_slice_in_dim(mine, part * ring.x_bit, part + middle, 0)
        self.pieces = [payload, payload]
        self.distance = 0
        self.arrived = self.whole = None

    def issue(self):
        ring, flight = self.ring, {}
        bit, half = ring.x_bit, self.ring.size // 2
        if self.distance < half:
            self.distance += 1
            ahead, behind = self.pieces
            if self.distance == half:
                split = ahead.shape[0] // 2
                ahead, behind = ahead[:split], behind[split:]
            flight["ring"] = [ring.forward(ahead), ring.backward(behind)]
        if self.arrived is not None:
            own = lax.dynamic_slice_in_dim(self.arrived, self.middle * bit, self.part, 1)
            flight["x"] = swap_x(own)
        if self.whole is not None:
            flight["core"] = swap_core(self.whole)
        return flight

    def land(self, flight):
        bit, waiting = self.ring.x_bit, self.arrived
        self.arrived = self.whole = None
        if "ring" in flight:
            self.pieces = flight["ring"]
            if self.distance == self.ring.size // 2:
                self.arrived = jnp.concatenate(self.pieces)[None]
            else:
                self.arrived = jnp.stack(self.pieces)
        if "x" in flight:
            got = flight["x"]
            self.whole = jnp.where(
                bit == 0,
                jnp.concatenate([waiting, got], axis=1),
                jnp.concatenate([got, waiting], axis=1),
            )
            self.mine.append(self.whole)
        if "core" in flight:
            self.other.append(flight["core"])


class Scatter:
    def __init__(self, ring, mine, got):
        self.ring, self.values = ring, (mine, got)
        self.distance = ring.size // 2
        self.split = mine.shape[1] // 2

    def piece(self, place, row, count):
        tok, width = self.ring.tok_at(place), self.values[0].shape[2]
        mine, got = (
            lax.dynamic_slice(values, (tok, row, 0), (1, count, width))[0].astype(f32)
            for values in self.values
        )
        return mine + got

    def hop(self):
        ring, distance, split = self.ring, self.distance, self.split
        rows = self.values[0].shape[1]
        if distance == ring.size // 2:
            ahead = self.piece(distance, 0, split)
            behind = self.piece(distance, split, rows - split)
        else:
            ahead, behind = self.ahead.astype(f32), self.behind.astype(f32)
            if distance == ring.size // 2 - 1:
                ahead = jnp.pad(ahead, ((0, rows - split), (0, 0)))
                behind = jnp.pad(behind, ((split, 0), (0, 0)))
            ahead = self.piece(distance, 0, rows) + ahead
            behind = self.piece(-distance, 0, rows) + behind
        self.distance -= 1
        return ring.forward(ahead.astype(bf16)), ring.backward(behind.astype(bf16))

    def land(self, flight):
        self.ahead, self.behind = flight

    def total(self):
        rows = self.values[0].shape[1]
        total = self.piece(0, 0, rows) + self.ahead.astype(f32) + self.behind.astype(f32)
        return total.astype(bf16)


def gather_plain(shard, share):
    size, width = lax.axis_size("tok"), shard.shape[1]
    full = lax.all_gather(shard, "tok", axis=0)
    blocks = [
        full[:, row : row + share].reshape(8, -1, width) for row in range(0, shard.shape[0], share)
    ]
    return jnp.concatenate(blocks, axis=1)


def by_tok(values, share):
    size = lax.axis_size("tok")
    if size == 8:
        return values
    rows = share * size // 8
    blocks = [
        values[:, row : row + rows].reshape(size, share, -1)
        for row in range(0, values.shape[1], rows)
    ]
    return jnp.concatenate(blocks, axis=1)


def scatter_plain(chip):
    return lax.psum_scatter(chip, "tok", scatter_dimension=0, tiled=True)[0]


def add_x(shard):
    step = 2
    while step < lax.axis_size("grp"):
        shard = add_low(shard, lax.ppermute(shard, "grp", swap_pairs(lax.axis_size("grp"), step)))
        step *= 2
    return shard


def spread_kernel(weight_ref, out_ref, *, count):
    share = weight_ref.shape[0]
    for block in range(4):
        pieces = [
            weight_ref[:, (4 * tok + block) * share : (4 * tok + block + 1) * share]
            for tok in range(count)
        ]
        out_ref[block] = jnp.concatenate(pieces, axis=1).astype(bf16)


def spread_call(weight, count):
    share = weight.shape[0]
    return pl.pallas_call(
        functools.partial(spread_kernel, count=count),
        out_shape=jax.ShapeDtypeStruct((4, share, weight.shape[1] // 4), bf16),
        compiler_params=params(),
    )(weight)


def unspread_kernel(core_ref, mine_ref, other_ref, out_ref, *, count):
    share = mine_ref.shape[1]

    def write(refs):
        pieces = [
            refs[block // 2][block % 2, :, tok * share : (tok + 1) * share].astype(f32)
            for tok in range(count)
            for block in range(4)
        ]
        out_ref[...] = jnp.concatenate(pieces, axis=1)

    @pl.when(core_ref[0] == 0)
    def _():
        write((mine_ref, other_ref))

    @pl.when(core_ref[0] != 0)
    def _():
        write((other_ref, mine_ref))


def unspread_call(core, mine, other, count):
    share, width = mine.shape[1:]
    return pl.pallas_call(
        functools.partial(unspread_kernel, count=count),
        in_specs=[smem, whole_block(mine), whole_block(other)],
        out_shape=jax.ShapeDtypeStruct((share, 4 * width), f32),
        compiler_params=params(),
    )(core, mine, other)


def on_device(
    kept_tokens,
    kept_index,
    kept_count,
    condition,
    mask_token,
    position_table,
    modulation_weight,
    modulation_bias,
    input_weight,
    query_bias,
    value_bias,
    output_weight,
    output_bias,
    up_weight,
    up_bias,
    down_weight,
    down_bias,
    cotangent,
):
    _, seq_len, width = cotangent.shape
    tok_count = lax.axis_size("tok")
    core = lax.axis_index("grp") % 2
    core_row = core.reshape(1)
    share = input_weight.shape[0]
    position_rows = position_table.shape[0]

    def by_core(first, second):
        return jnp.where(core == 0, first, second)

    def exchange(values):
        return lax.all_to_all(values, "tok", split_axis=0, concat_axis=0, tiled=True)

    ring = Ring()

    condition_low = jax.nn.silu(condition).astype(bf16)
    slots_here = kept_tokens.shape[1]
    condition_rows = jnp.broadcast_to(condition_low, (tok_count, 8, width))
    arrived = exchange(jnp.concatenate([kept_tokens.astype(bf16), condition_rows], axis=1))
    routed = arrived[:, :slots_here].reshape(-1, width)
    condition_group = arrived[:, slots_here]

    modulation_low = modulation_weight.astype(bf16)

    def modulate_all(conditions):
        modulation_part = jnp.dot(
            conditions, modulation_low, preferred_element_type=f32
        ) + modulation_bias.astype(bf16).astype(f32)
        return exchange(modulation_part).reshape(6, width)

    condition_all = lax.all_gather(condition_group, "grp", axis=0, tiled=True)

    ringed = share % 16 == 0 and lax.axis_size("grp") == 4
    small_parts = [mask_token, query_bias, value_bias, output_bias, down_bias, up_bias]
    small_widths = [part.shape[0] for part in small_parts]
    cuts = [sum(small_widths[:number]) for number in range(len(small_widths) + 1)]
    small_rows = position_rows // 8
    table_rows = position_rows * 5 // 8
    tail_rows = position_rows - table_rows

    def as_rows(parts):
        flat = jnp.concatenate(parts, axis=-1)
        lead = flat.shape[:-1]
        flat = jnp.pad(flat, [(0, 0)] * len(lead) + [(0, small_rows * width - flat.shape[-1])])
        return flat.reshape(lead + (small_rows, width))

    def table_parts(table, small):
        lead = table.shape[:-2]
        blank = jnp.zeros(lead + (table_rows - tail_rows - small_rows, width), table.dtype)
        return table[..., :table_rows, :], jnp.concatenate(
            [table[..., table_rows:, :], small, blank], axis=-2
        )

    input_low = input_weight.astype(bf16)
    input_blocks = [input_low[:, number * width : (number + 1) * width] for number in range(3)]
    table_low = table_parts(position_table.astype(bf16), as_rows(small_parts).astype(bf16))
    attention_low = (
        jnp.concatenate(input_blocks[:2] + [table_low[0]]),
        jnp.concatenate([input_blocks[2], output_weight.astype(bf16), table_low[1]]),
    )
    up_low = spread_call(up_weight, tok_count)
    down_low = down_weight.astype(bf16).reshape(4, share, width)
    feed_low = tuple(
        jnp.concatenate([up_low[half : half + 2], down_low[half : half + 2]]).reshape(-1, width)
        for half in (0, 2)
    )

    attention_cut, feed_cut = (8 * share // 9, 7 * share // 9), (4 * share // 3, 4 * share // 3)
    if ringed:
        mine, other = by_core(*attention_low), by_core(*attention_low[::-1])
        gather = Gather(ring, mine, other, *attention_cut)
        mine, other = by_core(*feed_low), by_core(*feed_low[::-1])
        feed_gather = Gather(ring, mine, other, *feed_cut)
        for _ in range(2):
            (flight,) = sync(gather.issue())
            gather.land(flight)
        flight, condition_group, routed = sync(gather.issue(), condition_group, routed)
        gather.land(flight)
    mod = modulate_all(condition_group)
    if ringed:
        flight, mod = sync(gather.issue(), mod)
        gather.land(flight)
        feed_gather.pieces, gather.arrived = sync(feed_gather.pieces, gather.arrived)
        feed_flight = feed_gather.issue()
        (flight,) = sync(gather.issue())
        gather.land(flight)
        flight, feed_flight = sync(gather.issue(), feed_flight)
        gather.land(flight)
        feed_gather.land(feed_flight)
        attention_chunks = Chunks(gather.mine, gather.other)
        distances = [0]
        for distance in range(1, ring.size // 2):
            distances += [-distance, distance]
        places = ring.tok_at(jnp.array(distances + [ring.size // 2], jnp.int32))
        small_rel = jnp.concatenate(
            [
                by_core(other, mine)[:, 2 * share + tail_rows : 2 * share + tail_rows + small_rows]
                for mine, other in zip(gather.mine, gather.other)
            ]
        )
        small = jnp.zeros_like(small_rel).at[places].set(small_rel).reshape(tok_count, -1)
    else:
        places = jnp.arange(8, dtype=jnp.int32)
        mine = gather_plain(by_core(*attention_low)[: 2 * share], share)
        attention_chunks = Chunks([mine], [swap_core(mine)])
        mine = gather_plain(by_core(*feed_low), share)
        feed_chunks = Chunks([mine], [swap_core(mine)])
        table = lax.all_gather(
            jnp.concatenate([position_table.astype(bf16), as_rows(small_parts).astype(bf16)]), "tok"
        )
        small = table[:, position_rows:].reshape(tok_count, -1)
        table = table[:, :position_rows].reshape(8, -1, width)
    mask_full, query_bias_full, value_bias_full, output_bias_full, down_bias_full = (
        small[:, cuts[number] : cuts[number + 1]].reshape(1, width).astype(f32)
        for number in range(5)
    )
    up_bias_full = (
        small[:, cuts[5] : cuts[6]].reshape(tok_count, 4, share).transpose(1, 0, 2).reshape(4, 1, width)
    ).astype(f32)

    if ringed:
        table_chunks, table_row, table_share = attention_chunks, 2 * share, table_rows
    else:
        table_share = table.shape[1] // 2
        halves = table[:, :table_share], table[:, table_share:]
        table_chunks, table_row = Chunks([by_core(*halves)], [by_core(*halves[::-1])]), 0
    start, norm_one = start_call(
        core_row, places, kept_count, kept_index, routed, mask_full, mod, table_chunks, table_row,
        table_share, seq_len,
    )
    blank = jnp.zeros_like(query_bias_full)
    projected_bias = jnp.stack([query_bias_full, blank, value_bias_full])
    projected = project_call(core_row, places, norm_one, projected_bias, attention_chunks)
    if ringed:
        flight, projected, start = sync(feed_gather.issue(), projected, start)
        feed_gather.land(flight)
    attended = []
    for group in range(groups):
        attended.append(attend_call(projected, group))
        if ringed and group % 2:
            flight, attended, projected = sync(feed_gather.issue(), attended, projected)
            feed_gather.land(flight)
    joined, branch_one, middle, norm_two = mix_call(
        core_row, places, [pair[0] for pair in attended], start, output_bias_full, mod, attention_chunks
    )
    if ringed:
        flight, norm_two = sync(feed_gather.issue(), norm_two)
        feed_gather.land(flight)
        (flight,) = sync(feed_gather.issue())
        feed_gather.land(flight)
        feed_chunks = Chunks(feed_gather.mine, feed_gather.other)
    (
        block_output,
        hidden,
        pre_grad,
        grad_two,
        middle_grad,
        grad_one,
        feed_sums,
        up_bias_sum,
    ) = feed_call(
        core_row, places, norm_two, middle, cotangent[0], branch_one, mod, up_bias_full, down_bias_full,
        feed_chunks,
    )
    feed_other = feed_weight_call(2 - 2 * core_row, norm_two, pre_grad, hidden, grad_two)
    feed_other, norm_two, grad_one = sync(feed_other, norm_two, grad_one)
    feed_mine = feed_weight_call(2 * core_row, norm_two, pre_grad, hidden, grad_two)
    feed_got, feed_mine, grad_one = sync(swap_core(feed_other), feed_mine, grad_one)
    mix_grad = mix_grad_call(core_row, places, grad_one, attention_chunks)
    if ringed:
        feed_scatter = Scatter(ring, feed_mine, feed_got)
    grads = []
    for group in range(groups):
        grads.append(attend_back_call(projected, *attended[group], mix_grad, group))
        if ringed and group in (0, 2):
            flight, grads, mix_grad = sync(feed_scatter.hop(), grads, mix_grad)
            feed_scatter.land(flight)
    grads = [triple[block] for block in range(3) for triple in grads]

    def attention_weights(owner, norm):
        return attention_weight_call(owner, norm, joined, grad_one, grads)

    def start_back(half, grads):
        return start_back_call(
            half, core_row, places, kept_count, kept_index, grads, middle_grad, start, mod, attention_chunks
        )

    attention_other = attention_weights(1 - core_row, norm_one)
    if ringed:
        flight, attention_other, norm_one, grads = sync(
            feed_scatter.hop(), attention_other, norm_one, grads
        )
        feed_scatter.land(flight)
    attention_mine = attention_weights(core_row, norm_one)
    attention_got = swap_core(attention_other)
    first_half = start_back(0, grads)
    if ringed:
        flight, attention_mine, attention_got, first_half, grads = sync(
            feed_scatter.hop(), attention_mine, attention_got, first_half, grads
        )
        feed_scatter.land(flight)
        feed_shard = feed_scatter.total()
        scatter = Scatter(ring, attention_mine, attention_got)
        second_half = start_back(1, grads)
        flight, second_half = sync(scatter.hop(), second_half)
        scatter.land(flight)
    else:
        second_half = start_back(1, grads)
    row_grad = jnp.concatenate([first_half[0], second_half[0]])
    slot_grad = first_half[1] + second_half[1]
    start_sums = first_half[2] + second_half[2]
    kept_grad = exchange(slot_grad.reshape(tok_count, -1, width)).astype(f32)

    up_sums = up_bias_sum.reshape(4, tok_count, share).transpose(1, 0, 2).reshape(tok_count, -1)
    rows_of = lambda row: row.reshape(tok_count, -1)
    small_grads = as_rows(
        [
            rows_of(start_sums[4]),
            rows_of(start_sums[0]),
            rows_of(start_sums[1]),
            rows_of(feed_sums[5]),
            rows_of(feed_sums[1]),
            up_sums,
        ]
    ).astype(bf16)
    position_grad = row_grad.reshape(tok_count, position_rows, width)
    tables = table_parts(position_grad, small_grads)
    table_got = swap_core(by_core(tables[1], tables[0]))
    table_chip = add_low(by_core(tables[0], tables[1]), table_got)
    table_shard = jnp.sum(exchange(table_chip).astype(f32), axis=0).astype(bf16)
    table_shard = add_x(table_shard)
    table_far = swap_core(table_shard)
    first, second = by_core(table_shard, table_far), by_core(table_far, table_shard)
    position_total = jnp.concatenate([first, second[:tail_rows]]).astype(f32)
    small_total = second[tail_rows : tail_rows + small_rows].astype(f32).reshape(-1)
    if ringed:
        while scatter.distance > 0:
            (flight,) = sync(scatter.hop())
            scatter.land(flight)
        attention_shard = add_x(scatter.total())
    else:
        attention_chip = by_tok(add_low(attention_mine, attention_got), share)
        attention_shard = add_x(scatter_plain(attention_chip))
        feed_shard = scatter_plain(by_tok(add_low(feed_mine, feed_got), share))
    feed_shard = add_x(feed_shard)

    (
        mask_total,
        query_bias_total,
        value_bias_total,
        output_bias_total,
        down_bias_total,
        up_bias_total,
    ) = (small_total[cuts[number] : cuts[number + 1]] for number in range(6))
    far = swap_core(attention_shard)
    first, second = by_core(attention_shard, far).astype(f32), by_core(far, attention_shard).astype(f32)
    input_total = jnp.concatenate([first[:share], first[share:], second[:share]], axis=1)
    output_total = second[share:]
    feed_shard = feed_shard.reshape(4, share, width)
    feed_far = swap_core(feed_shard)
    up_total = unspread_call(core_row, feed_shard[:2], feed_far[:2], tok_count)
    down_total = jnp.concatenate(
        [by_core(feed_shard[2:], feed_far[2:]), by_core(feed_far[2:], feed_shard[2:])]
    ).reshape(-1, width).astype(f32)

    modulation_grad = jnp.concatenate(
        [start_sums[3], start_sums[2], feed_sums[4], feed_sums[3], feed_sums[2], feed_sums[0]]
    ).astype(bf16)
    modulation_grad_group = exchange(modulation_grad.reshape(tok_count, -1))
    modulation_grad_all = lax.all_gather(modulation_grad_group, "grp", axis=0, tiled=True)
    modulation_total = jnp.einsum(
        "id,ie->de", condition_all, modulation_grad_all, preferred_element_type=f32
    )
    modulation_bias_total = jnp.sum(modulation_grad_all.astype(f32), axis=0)
    condition_part = jnp.einsum(
        "ie,de->id", modulation_grad_group, modulation_low, preferred_element_type=f32
    )
    condition_low_grad = jnp.sum(exchange(condition_part), axis=0, keepdims=True)
    _, silu_back = jax.vjp(jax.nn.silu, condition)
    condition_grad = silu_back(condition_low_grad)[0]
    return (
        block_output[None],
        kept_grad,
        condition_grad,
        mask_total,
        position_total,
        modulation_total,
        modulation_bias_total,
        input_total,
        query_bias_total,
        value_bias_total,
        output_total,
        output_bias_total,
        up_total,
        up_bias_total,
        down_total,
        down_bias_total,
    )


def solution(mesh):
    return jax.shard_map(
        on_device,
        mesh=mesh,
        in_specs=(
            P("grp", "tok", None),
            P(("grp", "tok"), None),
            P(("grp", "tok")),
            P(("grp", "tok"), None),
            P("tok"),
            P("tok", None),
            P(None, "tok"),
            P("tok"),
            P("tok", None),
            P("tok"),
            P("tok"),
            P("tok", None),
            P("tok"),
            P("tok", None),
            P("tok"),
            P("tok", None),
            P("tok"),
            P(("grp", "tok"), None, None),
        ),
        out_specs=(
            P(("grp", "tok"), None, None),
            P("grp", "tok", None),
            P(("grp", "tok"), None),
            P("tok"),
            P("tok", None),
            P(None, "tok"),
            P("tok"),
            P("tok", None),
            P("tok"),
            P("tok"),
            P("tok", None),
            P("tok"),
            P("tok", None),
            P("tok"),
            P("tok", None),
            P("tok"),
        ),
        check_vma=False,
    )
```

```python
import functools
import math

import jax
import jax.numpy as jnp
from jax import lax
from jax.experimental import pallas as pl
from jax.experimental.pallas import tpu as pltpu
from jax.sharding import PartitionSpec as P

H = 16
HD = 72
LANES = 128

epsilon = 1e-06
f32 = jnp.float32
bf16 = jnp.bfloat16
plain = (((1,), (0,)), ((), ()))
right_turned = (((1,), (1,)), ((), ()))
left_turned = (((0,), (0,)), ((), ()))
vmem_limit = 60 << 20


def product(left, right, dims=plain):
    return lax.dot_general(left, right, dims, preferred_element_type=f32)


def whole_block(array):
    zeros = (0,) * array.ndim
    return pl.BlockSpec(array.shape, lambda *_: zeros)


def row_block(rows, *rest):
    return pl.BlockSpec((rows,) + rest, lambda i: (i,) + (0,) * len(rest))


smem = pl.BlockSpec(memory_space=pltpu.SMEM)
anywhere = pl.BlockSpec(memory_space=pl.ANY)


def params():
    return pltpu.CompilerParams(vmem_limit_bytes=vmem_limit)


def cost(flops, moved, exps=0):
    return pl.CostEstimate(flops=int(flops), bytes_accessed=int(moved), transcendentals=int(exps))


def column_sum(values):
    return jnp.sum(values, axis=0, keepdims=True)


def normalize(values):
    center = values - jnp.mean(values, axis=-1, keepdims=True)
    spread = jnp.mean(center * center, axis=-1, keepdims=True)
    inverse = lax.rsqrt(spread + epsilon)
    return center * inverse, inverse


def normalize_back(grad, unit, inverse, scale):
    scaled = grad * (1.0 + scale)
    first = jnp.mean(scaled, axis=-1, keepdims=True)
    second = jnp.mean(scaled * unit, axis=-1, keepdims=True)
    return (scaled - first - unit * second) * inverse


def start_kernel(core_ref, places_ref, count_ref, index_ref, kept_ref, small_ref, mod_ref, *rest, chunks, row, share):
    refs, (start_ref, norm_ref, table, sems) = rest[: len(chunks.arrays)], rest[len(chunks.arrays) :]
    rows, slots = start_ref.shape[0], kept_ref.shape[0]
    step = pl.program_id(0)
    low, high = table.at[:, :share], table.at[:, share:]

    @pl.when(step == 0)
    def _():
        @pl.when(core_ref[0] == 0)
        def _():
            chunks.load(refs, places_ref, core_ref, True, row, low, sems.at[0])
            chunks.load(refs, places_ref, core_ref, False, row, high, sems.at[1])

        @pl.when(core_ref[0] != 0)
        def _():
            chunks.load(refs, places_ref, core_ref, False, row, low, sems.at[0])
            chunks.load(refs, places_ref, core_ref, True, row, high, sems.at[1])

        wait_block(low, sems.at[0])
        wait_block(high, sems.at[1])

    base = step * rows
    here = lax.broadcasted_iota(jnp.int32, (rows, slots), 0) + base
    slot = lax.broadcasted_iota(jnp.int32, (rows, slots), 1)
    chosen = jnp.where((index_ref[...] == here) & (slot < count_ref[0]), 1.0, 0.0)
    filled = product(chosen.astype(bf16), kept_ref[...])
    empty = 1.0 - jnp.sum(chosen, axis=1, keepdims=True)
    groups_here = rows // table.shape[1]
    position = table[pl.ds(step * groups_here, groups_here)].reshape(rows, -1)
    start = filled + empty * small_ref[0:1] + position.astype(f32)
    start_ref[...] = start
    unit, _ = normalize(start)
    norm_ref[...] = (unit * (1.0 + mod_ref[1:2]) + mod_ref[0:1]).astype(bf16)


def start_call(core, places, count, index, kept, small, mod, chunks, row, share, seq_len):
    width = kept.shape[1]
    rows = seq_len // 4
    return pl.pallas_call(
        functools.partial(start_kernel, chunks=chunks, row=row, share=share),
        grid=(4,),
        in_specs=[
            smem,
            smem,
            smem,
            whole_block(index),
            whole_block(kept),
            whole_block(small),
            whole_block(mod),
        ]
        + chunks.specs,
        out_specs=[row_block(rows, width)] * 2,
        out_shape=[
            jax.ShapeDtypeStruct((seq_len, width), f32),
            jax.ShapeDtypeStruct((seq_len, width), bf16),
        ],
        scratch_shapes=[
            pltpu.VMEM((8, seq_len // 8, width), bf16),
            pltpu.SemaphoreType.DMA((2,)),
        ],
        compiler_params=params(),
        cost_estimate=cost(2 * seq_len * width * kept.shape[0], 14 * seq_len * width),
    )(core, places, count, index, kept, small, mod, *chunks.arrays)


class Chunks:
    def __init__(self, mine, other, part=0, middle=0):
        self.sources = list(mine), list(other)
        self.part, self.middle = part, middle
        self.arrays = [entry[0] for source in self.sources for entry in source]
        self.specs = [anywhere] * len(self.arrays)

    def span(self, kind, bit):
        part, middle = self.part, self.middle
        start = part * bit
        return {
            "piece": (start, start + part + middle),
            "first": (start, start + middle),
            "second": (start + middle, start + part + middle),
            "got": ((0, part) if bit else (part + middle, 2 * part + middle)),
            "all": (0, 1 << 20),
        }[kind]

    def spans(self, kind, bit):
        if kind == "pair":
            return [self.span("piece", bit) + (0,), self.span("got", bit) + (self.part + self.middle,)]
        return [self.span(kind, bit) + (0,)]

    def load(self, refs, places_ref, spot_ref, from_mine, row, target, sem):
        source = self.sources[0 if from_mine else 1]
        refs = refs[: len(source)] if from_mine else refs[len(self.sources[0]) :]

        def start(ref, kind, places, bit):
            for low, high, base in self.spans(kind, bit):
                begin, end = max(row, low), min(row + target.shape[1], high)
                for index, place in enumerate(places if begin < end else []):
                    pltpu.make_async_copy(
                        ref.at[index, pl.ds(base + begin - low, end - begin)],
                        target.at[places_ref[place], pl.ds(begin - row, end - begin)],
                        sem,
                    ).start()

        for ref, (_, kind, places) in zip(refs, source):
            if kind == "all":
                start(ref, kind, places, 0)
        if any(kind != "all" for _, kind, _ in source):
            for bit in (0, 1):

                @pl.when(spot_ref[1] == bit)
                def _():
                    for ref, (_, kind, places) in zip(refs, source):
                        if kind != "all":
                            start(ref, kind, places, bit)

    def load_block(self, refs, places_ref, spot_ref, block, target, sem, first=0):
        owner, row = block // 2, (first + block % 2) * target.shape[1]

        @pl.when(spot_ref[0] == owner)
        def _():
            self.load(refs, places_ref, spot_ref, True, row, target, sem)

        @pl.when(spot_ref[0] != owner)
        def _():
            self.load(refs, places_ref, spot_ref, False, row, target, sem)


def wait_block(target, sem):
    pltpu.make_async_copy(target, target, sem).wait()


def square(weight):
    return weight.reshape(-1, weight.shape[-1])


def split_heads(values, store):
    rows = values.shape[0]
    blank = jnp.zeros((rows, LANES - HD), values.dtype)
    for head in range(H):
        store(head, jnp.concatenate([values[:, head * HD : (head + 1) * HD], blank], axis=1))


def project_kernel(core_ref, places_ref, norm_ref, small_ref, *rest, chunks):
    refs, (out_ref, weight, sems) = rest[: len(chunks.arrays)], rest[len(chunks.arrays) :]
    step = pl.program_id(0)

    @pl.when(step == 0)
    def _():
        for block in range(3):
            chunks.load_block(refs, places_ref, core_ref, block, weight.at[block], sems.at[block])

    wait_block(weight.at[step], sems.at[step])
    key_free = jnp.where(step == 1, 0.0, 1.0)
    bias = jnp.where(step == 0, small_ref[1:2], small_ref[2:3]) * key_free
    half = norm_ref.shape[0] // 2
    for part in range(2):
        rows = slice(part * half, (part + 1) * half)
        result = product(norm_ref[rows], square(weight[step])) + bias

        def store(head, value):
            out_ref[0, head, rows] = value

        split_heads(result.astype(bf16), store)


def project_call(core, places, norm, small, chunks):
    seq_len, width = norm.shape
    return pl.pallas_call(
        functools.partial(project_kernel, chunks=chunks),
        grid=(3,),
        in_specs=[
            smem,
            smem,
            whole_block(norm),
            whole_block(small),
        ]
        + chunks.specs,
        out_specs=pl.BlockSpec((1, H, seq_len, LANES), lambda i: (i, 0, 0, 0)),
        out_shape=jax.ShapeDtypeStruct((3, H, seq_len, LANES), bf16),
        scratch_shapes=[
            pltpu.VMEM((3, 8, width // 8, width), bf16),
            pltpu.SemaphoreType.DMA((3,)),
        ],
        compiler_params=params(),
        cost_estimate=cost(6 * seq_len * width * width, 12 * seq_len * width + 6 * width * width),
    )(core, places, norm, small, *chunks.arrays)


def attend_kernel(query_ref, key_ref, value_ref, mix_ref, log_ref, *, size, factor):
    turned_value = value_ref[0, 0].T
    for part in range(query_ref.shape[2] // size):
        rows = slice(part * size, (part + 1) * size)
        scores = product(key_ref[0, 0], query_ref[0, 0, rows], right_turned)
        top = jnp.max(scores, axis=0, keepdims=True)
        weights = jnp.exp2((scores - top) * factor)
        total = jnp.sum(weights, axis=0, keepdims=True)
        mix = product(turned_value, weights.astype(bf16))
        mix_ref[0, rows] = (mix / total).T.astype(bf16)
        log_ref[0, :, rows] = top * factor + jnp.log2(total)


groups = 4


def head_block(place, seq_len, group):
    first = group * (H // groups)
    return pl.BlockSpec((1, 1, seq_len, LANES), lambda h: (place, first + h, 0, 0))


def attend_call(projected, group):
    seq_len = projected.shape[2]
    heads = H // groups
    flat = pl.BlockSpec((1, seq_len, LANES), lambda h: (h, 0, 0))
    return pl.pallas_call(
        functools.partial(
            attend_kernel, size=seq_len, factor=math.log2(math.e) / math.sqrt(HD)
        ),
        grid=(heads,),
        in_specs=[head_block(place, seq_len, group) for place in range(3)],
        out_specs=[flat, pl.BlockSpec((1, 1, seq_len), lambda h: (h, 0, 0))],
        out_shape=[
            jax.ShapeDtypeStruct((heads, seq_len, LANES), bf16),
            jax.ShapeDtypeStruct((heads, 1, seq_len), f32),
        ],
        compiler_params=params(),
        cost_estimate=cost(4 * heads * seq_len * seq_len * 256, 8 * heads * seq_len * LANES, heads * seq_len * seq_len),
    )(projected, projected, projected)


def attend_back_kernel(
    query_ref, key_ref, value_ref, mix_ref, log_ref, grad_ref, query_grad_ref, key_grad_ref,
    value_grad_ref, key_sum, value_sum, *, size, factor
):
    key, value = key_ref[0, 0], value_ref[0, 0]
    turned_key = key.T
    base_two = factor * math.log2(math.e)
    for part in range(query_ref.shape[2] // size):
        rows = slice(part * size, (part + 1) * size)
        query, grad = query_ref[0, 0, rows], grad_ref[0, rows]
        scores = product(key, query, right_turned)
        weights = jnp.exp2(scores * base_two - log_ref[0, :, rows])
        value_part = product(weights.astype(bf16), grad)
        weight_grad = product(value, grad, right_turned)
        inner = column_sum((grad.astype(f32) * mix_ref[0, rows].astype(f32)).T)
        score_grad = (weights * (weight_grad - inner)).astype(bf16)
        key_part = product(score_grad, query)
        query_grad_ref[0, rows] = (product(turned_key, score_grad) * factor).T.astype(bf16)
        if part == 0:
            key_sum[...] = key_part
            value_sum[...] = value_part
        else:
            key_sum[...] += key_part
            value_sum[...] += value_part
    key_grad_ref[0] = (key_sum[...] * factor).astype(bf16)
    value_grad_ref[0] = value_sum[...].astype(bf16)


def attend_back_call(projected, mix, logs, grad, group):
    seq_len = projected.shape[2]
    heads = H // groups
    first = group * heads
    flat = pl.BlockSpec((1, seq_len, LANES), lambda h: (h, 0, 0))
    return pl.pallas_call(
        functools.partial(attend_back_kernel, size=seq_len // 2, factor=1.0 / math.sqrt(HD)),
        grid=(heads,),
        in_specs=[head_block(place, seq_len, group) for place in range(3)]
        + [
            flat,
            pl.BlockSpec((1, 1, seq_len), lambda h: (h, 0, 0)),
            pl.BlockSpec((1, seq_len, LANES), lambda h: (first + h, 0, 0)),
        ],
        out_specs=[flat] * 3,
        out_shape=[jax.ShapeDtypeStruct((heads, seq_len, LANES), bf16)] * 3,
        scratch_shapes=[pltpu.VMEM((seq_len, LANES), f32)] * 2,
        compiler_params=params(),
        cost_estimate=cost(10 * heads * seq_len * seq_len * 256, 16 * heads * seq_len * LANES, heads * seq_len * seq_len),
    )(projected, projected, projected, mix, logs, grad)


def join_heads(refs):
    return jnp.concatenate(
        [ref[head][:, :HD] for ref in refs for head in range(ref.shape[0])], axis=1
    )


def mix_kernel(core_ref, places_ref, start_ref, small_ref, mod_ref, *rest, chunks):
    mix_refs, rest = rest[:groups], rest[groups:]
    refs, rest = rest[: len(chunks.arrays)], rest[len(chunks.arrays) :]
    joined_ref, branch_ref, middle_ref, norm_ref, weight, sem = rest

    @pl.when(pl.program_id(0) == 0)
    def _():
        chunks.load_block(refs, places_ref, core_ref, 3, weight, sem)
        wait_block(weight, sem)

    joined = join_heads(mix_refs)
    joined_ref[...] = joined
    branch = product(joined, square(weight[...])) + small_ref[3:4]
    branch_ref[...] = branch
    middle = start_ref[...] + mod_ref[2:3] * branch
    middle_ref[...] = middle
    unit, _ = normalize(middle)
    norm_ref[...] = (unit * (1.0 + mod_ref[4:5]) + mod_ref[3:4]).astype(bf16)


def mix_call(core, places, mix, start, small, mod, chunks):
    seq_len, width = start.shape
    rows = seq_len // 4
    block = row_block(rows, width)
    return pl.pallas_call(
        functools.partial(mix_kernel, chunks=chunks),
        grid=(4,),
        in_specs=[smem, smem, block, whole_block(small), whole_block(mod)]
        + [pl.BlockSpec((H // groups, rows, LANES), lambda i: (0, i, 0))] * groups
        + chunks.specs,
        out_specs=[block] * 4,
        out_shape=[
            jax.ShapeDtypeStruct((seq_len, width), kind) for kind in (bf16, f32, f32, bf16)
        ],
        scratch_shapes=[pltpu.VMEM((8, width // 8, width), bf16), pltpu.SemaphoreType.DMA],
        compiler_params=params(),
        cost_estimate=cost(2 * seq_len * width * width, 18 * seq_len * width),
    )(core, places, start, small, mod, *mix, *chunks.arrays)


def gelu_parts(values):
    inner = 0.7978845608028654 * (values + 0.044715 * values * values * values)
    turned = jnp.tanh(inner)
    half = 0.5 * (1.0 + turned)
    slope = half + 0.5 * values * (1.0 - turned * turned) * (
        0.7978845608028654 * (1.0 + 0.134145 * values * values)
    )
    return values * half, slope


def feed_kernel(
    core_ref, places_ref, norm_ref, middle_ref, cot_ref, branch_ref, mod_ref, small_ref, *rest, source
):
    refs, rest = rest[: len(source.arrays)], rest[len(source.arrays) :]
    (
        out_ref, hidden_ref, pre_ref, grad_two_ref, middle_grad_ref, grad_one_ref, sums_ref,
        up_sums_ref, up, down, slopes, sems,
    ) = rest
    step = pl.program_id(0)
    chunks = 4

    @pl.when(step == 0)
    def _():
        for chunk in range(chunks):
            for side, target in enumerate((up, down)):
                source.load_block(
                    refs, places_ref, core_ref, chunk, target.at[chunk], sems.at[side, chunk], 2 * side
                )
        sums_ref[...] = jnp.zeros_like(sums_ref)
        up_sums_ref[...] = jnp.zeros_like(up_sums_ref)

    norm = norm_ref[...]
    total = None
    for chunk in range(chunks):

        @pl.when(step == 0)
        def _():
            wait_block(up.at[chunk], sems.at[0, chunk])
            wait_block(down.at[chunk], sems.at[1, chunk])

        before = product(norm, square(up[chunk])) + small_ref[5 + chunk : 6 + chunk]
        hidden, slope = gelu_parts(before)
        hidden = hidden.astype(bf16)
        hidden_ref[chunk] = hidden
        slopes[chunk] = slope.astype(slopes.dtype)
        part = product(hidden, square(down[chunk]))
        total = part if total is None else total + part
    branch_two = total + small_ref[4:5]
    middle, cot = middle_ref[...], cot_ref[...]
    gate_two = mod_ref[5:6]
    out_ref[...] = middle + gate_two * branch_two
    grad_two = (gate_two * cot).astype(bf16)
    grad_two_ref[...] = grad_two
    sums_ref[0:1] += column_sum(cot * branch_two)
    sums_ref[1:2] += column_sum(grad_two.astype(f32))
    total = None
    for chunk in range(chunks):
        pre = (product(grad_two, square(down[chunk]), right_turned) * slopes[chunk].astype(f32)).astype(bf16)
        pre_ref[chunk] = pre
        up_sums_ref[chunk] += column_sum(pre.astype(f32))
        part = product(pre, square(up[chunk]), right_turned)
        total = part if total is None else total + part
    unit, inverse = normalize(middle)
    sums_ref[2:3] += column_sum(total * unit)
    sums_ref[3:4] += column_sum(total)
    middle_grad = cot + normalize_back(total, unit, inverse, mod_ref[4:5])
    middle_grad_ref[...] = middle_grad
    sums_ref[4:5] += column_sum(middle_grad * branch_ref[...])
    grad_one = (mod_ref[2:3] * middle_grad).astype(bf16)
    grad_one_ref[...] = grad_one
    sums_ref[5:6] += column_sum(grad_one.astype(f32))


def feed_call(core, places, norm, middle, cot, branch, mod, small, source):
    seq_len, width = middle.shape
    steps = 4
    rows = seq_len // steps
    block = row_block(rows, width)
    chunked = pl.BlockSpec((4, rows, width), lambda i: (0, i, 0))
    wide = jax.ShapeDtypeStruct((4, seq_len, width), bf16)
    return pl.pallas_call(
        functools.partial(feed_kernel, source=source),
        grid=(steps,),
        in_specs=[
            smem,
            smem,
            block,
            block,
            block,
            block,
            whole_block(mod),
            whole_block(small),
        ]
        + source.specs,
        out_specs=[
            block,
            chunked,
            chunked,
            block,
            block,
            block,
            pl.BlockSpec((8, width), lambda i: (0, 0)),
            pl.BlockSpec((4, 1, width), lambda i: (0, 0, 0)),
        ],
        out_shape=[
            jax.ShapeDtypeStruct((seq_len, width), f32),
            wide,
            wide,
            jax.ShapeDtypeStruct((seq_len, width), bf16),
            jax.ShapeDtypeStruct((seq_len, width), f32),
            jax.ShapeDtypeStruct((seq_len, width), bf16),
            jax.ShapeDtypeStruct((8, width), f32),
            jax.ShapeDtypeStruct((4, 1, width), f32),
        ],
        scratch_shapes=[
            pltpu.VMEM((4, 8, width // 8, width), bf16),
            pltpu.VMEM((4, 8, width // 8, width), bf16),
            pltpu.VMEM((4, rows, width), f32),
            pltpu.SemaphoreType.DMA((2, 4)),
        ],
        compiler_params=params(),
        cost_estimate=cost(32 * seq_len * width * width, 60 * seq_len * width, 4 * seq_len * width),
    )(core, places, norm, middle, cot, branch, mod, small, *source.arrays)


def feed_weight_kernel(first_ref, norm_ref, pre_ref, hidden_ref, grad_ref, out_ref):
    step = pl.program_id(0)

    @pl.when(step < 2)
    def _():
        result = product(norm_ref[...], pre_ref[0], left_turned)
        out_ref[...] = result.astype(bf16).reshape(out_ref.shape)

    @pl.when(step >= 2)
    def _():
        result = product(hidden_ref[0], grad_ref[...], left_turned)
        out_ref[...] = result.astype(bf16).reshape(out_ref.shape)


def feed_weight_call(first, norm, pre, hidden, grad):
    seq_len, width = norm.shape
    block = (1, seq_len, width)
    full = pl.BlockSpec((seq_len, width), lambda i, f: (0, 0))
    return pl.pallas_call(
        feed_weight_kernel,
        grid_spec=pltpu.PrefetchScalarGridSpec(
            num_scalar_prefetch=1,
            grid=(4,),
            in_specs=[
                full,
                pl.BlockSpec(block, lambda i, f: (f[0] + jnp.minimum(i, 1), 0, 0)),
                pl.BlockSpec(block, lambda i, f: (f[0] + jnp.maximum(i - 2, 0), 0, 0)),
                full,
            ],
            out_specs=pl.BlockSpec((8, width // 8, width), lambda i, f: (0, i, 0)),
        ),
        out_shape=jax.ShapeDtypeStruct((8, width // 2, width), bf16),
        compiler_params=params(),
        cost_estimate=cost(8 * seq_len * width * width, 12 * seq_len * width + 8 * width * width),
    )(first, norm, pre, hidden, grad)


def attention_weight_kernel(owner_ref, norm_ref, joined_ref, grad_ref, *rest):
    head_refs = [rest[block * groups : (block + 1) * groups] for block in range(3)]
    out_ref, left, heads, right, sems = rest[3 * groups :]
    step = pl.program_id(0)
    size = heads.shape[1] // groups

    def copies(block, slot):
        if block == 3:
            return [(joined_ref, left.at[slot]), (grad_ref, right.at[slot])]
        return [(norm_ref, left.at[slot])] + [
            (ref, heads.at[slot, pl.ds(group * size, size)])
            for group, ref in enumerate(head_refs[block])
        ]

    @pl.when(step == 0)
    def _():
        for block in range(4):

            @pl.when(owner_ref[0] == block // 2)
            def _():
                for source, target in copies(block, block % 2):
                    pltpu.make_async_copy(source, target, sems.at[block % 2]).start()

    for block in range(4):

        @pl.when((owner_ref[0] == block // 2) & (step == block % 2))
        def _():
            slot = block % 2
            wait_block(left.at[slot], sems.at[slot])
            if block == 3:
                wait_block(right.at[slot], sems.at[slot])
            else:
                wait_block(heads.at[slot], sems.at[slot])
                right[slot] = jnp.concatenate(
                    [heads[slot, head][:, :HD] for head in range(H)], axis=1
                )

    result = product(left[step], right[step], left_turned)
    out_ref[...] = result.astype(bf16).reshape(out_ref.shape)


def attention_weight_call(owner, norm, joined, grad_one, grads):
    seq_len, width = norm.shape
    return pl.pallas_call(
        attention_weight_kernel,
        grid=(2,),
        in_specs=[smem] + [anywhere] * (3 + 3 * groups),
        out_specs=pl.BlockSpec((8, width // 8, width), lambda i: (0, i, 0)),
        out_shape=jax.ShapeDtypeStruct((8, width // 4, width), bf16),
        scratch_shapes=[
            pltpu.VMEM((2, seq_len, width), bf16),
            pltpu.VMEM((2, H, seq_len, LANES), bf16),
            pltpu.VMEM((2, seq_len, width), bf16),
            pltpu.SemaphoreType.DMA((2,)),
        ],
        compiler_params=params(),
        cost_estimate=cost(4 * seq_len * width * width, 10 * seq_len * width + 4 * width * width),
    )(owner, norm, joined, grad_one, *grads)


def mix_grad_kernel(core_ref, places_ref, grad_ref, *rest, chunks):
    refs, (out_ref, weight, sem) = rest[: len(chunks.arrays)], rest[len(chunks.arrays) :]

    @pl.when(pl.program_id(0) == 0)
    def _():
        chunks.load_block(refs, places_ref, core_ref, 3, weight, sem)
        wait_block(weight, sem)

    def store(head, value):
        out_ref[head] = value

    split_heads(product(grad_ref[...], square(weight[...]), right_turned).astype(bf16), store)


def mix_grad_call(core, places, grad_one, chunks):
    seq_len, width = grad_one.shape
    rows = seq_len // 2
    return pl.pallas_call(
        functools.partial(mix_grad_kernel, chunks=chunks),
        grid=(2,),
        in_specs=[smem, smem, row_block(rows, width)] + chunks.specs,
        out_specs=pl.BlockSpec((H, rows, LANES), lambda i: (0, i, 0)),
        out_shape=jax.ShapeDtypeStruct((H, seq_len, LANES), bf16),
        scratch_shapes=[pltpu.VMEM((8, width // 8, width), bf16), pltpu.SemaphoreType.DMA],
        compiler_params=params(),
        cost_estimate=cost(2 * seq_len * width * width, 8 * seq_len * width),
    )(core, places, grad_one, *chunks.arrays)


def start_back_kernel(
    core_ref, places_ref, count_ref, index_row_ref, index_ref, middle_grad_ref, start_ref, mod_ref,
    *rest, chunks, first
):
    grad_refs = [rest[block * groups : (block + 1) * groups] for block in range(3)]
    rest = rest[3 * groups :]
    refs, rest = rest[: len(chunks.arrays)], rest[len(chunks.arrays) :]
    row_grad_ref, slot_ref, sums_ref, weight, slots, sems = rest
    step = pl.program_id(0)
    rows, width = start_ref.shape
    slot_count = slots.shape[0]

    @pl.when(step == 0)
    def _():
        for block in range(3):
            chunks.load_block(refs, places_ref, core_ref, block, weight.at[block], sems.at[block])
        sums_ref[...] = jnp.zeros_like(sums_ref)

    total = None
    for block, refs in enumerate(grad_refs):
        joined = join_heads(refs)
        if block != 1:
            place = block // 2
            sums_ref[place : place + 1] += column_sum(joined.astype(f32))

        @pl.when(step == 0)
        def _():
            wait_block(weight.at[block], sems.at[block])

        part = product(joined, square(weight[block]), right_turned)
        total = part if total is None else total + part
    unit, inverse = normalize(start_ref[...])
    sums_ref[2:3] += column_sum(total * unit)
    sums_ref[3:4] += column_sum(total)
    row_grad = middle_grad_ref[...] + normalize_back(total, unit, inverse, mod_ref[1:2])
    row_low = row_grad.astype(bf16)
    row_grad_ref[...] = row_low
    base = (first + step) * rows
    place = lax.broadcasted_iota(jnp.int32, (slot_count, rows), 1) + base
    slot = lax.broadcasted_iota(jnp.int32, (slot_count, rows), 0)
    chosen = jnp.where((index_ref[...] == place) & (slot < count_ref[0]), 1.0, 0.0)
    part = product(chosen.astype(bf16), row_low)

    @pl.when(step == 0)
    def _():
        slots[...] = part

    @pl.when(step > 0)
    def _():
        slots[...] += part

    here = lax.broadcasted_iota(jnp.int32, (rows, slot_count), 0) + base
    lane = lax.broadcasted_iota(jnp.int32, (rows, slot_count), 1)
    taken = jnp.where((index_row_ref[...] == here) & (lane < count_ref[0]), 1.0, 0.0)
    empty = 1.0 - jnp.sum(taken, axis=1, keepdims=True)
    sums_ref[4:5] += column_sum(row_grad * empty)

    @pl.when(step == pl.num_programs(0) - 1)
    def _():
        slot_ref[...] = slots[...].astype(bf16)


def start_back_call(half, core, places, count, index, grads, middle_grad, start, mod, chunks):
    seq_len, width = start.shape
    slot_count = index.shape[1]
    steps = 2
    rows = seq_len // 4
    first = half * steps
    heads = pl.BlockSpec((H // groups, rows, LANES), lambda i: (0, first + i, 0))
    block = pl.BlockSpec((rows, width), lambda i: (first + i, 0))
    column = index.reshape(slot_count, 1)
    return pl.pallas_call(
        functools.partial(start_back_kernel, chunks=chunks, first=first),
        grid=(steps,),
        in_specs=[
            smem,
            smem,
            smem,
            whole_block(index),
            whole_block(column),
            block,
            block,
            whole_block(mod),
        ]
        + [heads] * (3 * groups)
        + chunks.specs,
        out_specs=[
            row_block(rows, width),
            pl.BlockSpec((slot_count, width), lambda i: (0, 0)),
            pl.BlockSpec((8, width), lambda i: (0, 0)),
        ],
        out_shape=[
            jax.ShapeDtypeStruct((seq_len // 2, width), bf16),
            jax.ShapeDtypeStruct((slot_count, width), bf16),
            jax.ShapeDtypeStruct((8, width), f32),
        ],
        scratch_shapes=[
            pltpu.VMEM((3, 8, width // 8, width), bf16),
            pltpu.VMEM((slot_count, width), f32),
            pltpu.SemaphoreType.DMA((3,)),
        ],
        compiler_params=params(),
        cost_estimate=cost(4 * seq_len * width * width, 13 * seq_len * width),
    )(core, places, count, index, column, middle_grad, start, mod, *grads, *chunks.arrays)


def collect_kernel(first_ref, second_ref, feed_ref, up_ref, mod_ref, small_ref):
    start = first_ref[...] + second_ref[...]
    feed = feed_ref[...]
    row = lambda values, number: values[number : number + 1]
    blank = jnp.zeros((7, start.shape[1]), f32)
    mod_ref[...] = jnp.concatenate(
        [row(start, 3), row(start, 2), row(feed, 4), row(feed, 3), row(feed, 2), row(feed, 0)]
    ).astype(bf16)
    small_ref[...] = jnp.concatenate(
        [row(start, 4), row(start, 0), row(start, 1), row(feed, 5), row(feed, 1)]
        + [up_ref[block] for block in range(4)]
        + [blank]
    ).astype(bf16)


def collect_call(first, second, feed, up):
    width = first.shape[1]
    return pl.pallas_call(
        collect_kernel,
        out_shape=[
            jax.ShapeDtypeStruct((6, width), bf16),
            jax.ShapeDtypeStruct((16, width), bf16),
        ],
        compiler_params=params(),
    )(first, second, feed, up)


def swap_pairs(size, bit):
    return [(place, place ^ bit) for place in range(size)]


def swap_core(values):
    return lax.ppermute(values, "grp", swap_pairs(lax.axis_size("grp"), 1))


def add_low(*parts):
    total = parts[0].astype(f32)
    for part in parts[1:]:
        total = total + part.astype(f32)
    return total.astype(bf16)


def swap_x(values):
    return lax.ppermute(values, "grp", swap_pairs(lax.axis_size("grp"), 2))


class Ring:
    def __init__(self):
        size = lax.axis_size("tok")
        self.size = size
        order = list(range(0, size, 2)) + list(range(1, size, 2))[::-1]
        self.ahead = [(order[i], order[(i + 1) % size]) for i in range(size)]
        self.behind = [(after, before) for before, after in self.ahead]
        tok = lax.axis_index("tok")
        self.place = jnp.where(tok % 2 == 0, tok // 2, size - 1 - tok // 2)
        self.x_bit = (lax.axis_index("grp") // 2) % 2

    def tok_at(self, distance):
        place = (self.place + distance) % self.size
        return jnp.where(place < self.size // 2, 2 * place, 2 * (self.size - 1 - place) + 1)

    def forward(self, values):
        return lax.ppermute(values, "tok", self.ahead)

    def backward(self, values):
        return lax.ppermute(values, "tok", self.behind)


def sync(*values):
    return lax.optimization_barrier(values)


class Gather:
    def __init__(self, ring, mine, other, part, middle):
        self.ring, self.part, self.middle = ring, part, middle
        self.mine, self.other = [(mine[None], "all", [0])], [(other[None], "all", [0])]
        payload = lax.dynamic_slice_in_dim(mine, part * ring.x_bit, part + middle, 0)
        self.pieces = [payload, payload]
        self.distance = 0
        self.own = self.pair = None

    def issue(self):
        ring, flight = self.ring, {}
        middle, half = self.middle, ring.size // 2
        if self.distance < half:
            self.distance += 1
            ahead, behind = self.pieces
            if self.distance == half:
                ahead, behind = ahead[:middle], behind[middle:]
            flight["ring"] = [ring.forward(ahead), ring.backward(behind)]
        if self.own is not None:
            flight["x"] = swap_x(self.own)
        if self.pair is not None:
            flight["core"] = swap_core(self.pair)
        return flight

    def land(self, flight):
        bit, part, middle = self.ring.x_bit, self.part, self.middle
        if "core" in flight:
            self.other.append((flight["core"], "pair", self.pair_places))
        self.pair = self.own = None
        if "x" in flight:
            got = flight["x"]
            self.mine.append((got, "got", self.places))
            if len(self.places) == 1:
                ahead, behind = self.pieces
                self.pair = jnp.concatenate([ahead, behind, got[0]])[None]
            else:
                self.pair = jnp.concatenate([jnp.stack(self.pieces), got], axis=1)
            self.pair_places = self.places
        if "ring" in flight:
            ahead, behind = self.pieces = flight["ring"]
            place = 2 * self.distance - 1
            if self.distance == self.ring.size // 2:
                self.places = [place]
                self.mine += [(ahead[None], "first", [place]), (behind[None], "second", [place])]
                self.own = jnp.where(bit == 0, ahead[:part], behind)[None]
            else:
                self.places = [place, place + 1]
                self.mine += [(ahead[None], "piece", [place]), (behind[None], "piece", [place + 1])]
                self.own = jnp.stack(
                    [
                        lax.dynamic_slice_in_dim(piece, middle * bit, part, 0)
                        for piece in self.pieces
                    ]
                )

    def chunks(self):
        return Chunks(self.mine, self.other, self.part, self.middle)


class Scatter:
    def __init__(self, ring, mine, got):
        self.ring, self.values = ring, (mine, got)
        self.distance = ring.size // 2
        self.split = mine.shape[1] // 2

    def piece(self, place, row, count):
        tok, width = self.ring.tok_at(place), self.values[0].shape[2]
        mine, got = (
            lax.dynamic_slice(values, (tok, row, 0), (1, count, width))[0].astype(f32)
            for values in self.values
        )
        return mine + got

    def hop(self):
        ring, distance, split = self.ring, self.distance, self.split
        rows = self.values[0].shape[1]
        if distance == ring.size // 2:
            ahead = self.piece(distance, 0, split)
            behind = self.piece(distance, split, rows - split)
        else:
            ahead, behind = self.ahead.astype(f32), self.behind.astype(f32)
            if distance == ring.size // 2 - 1:
                ahead = jnp.pad(ahead, ((0, rows - split), (0, 0)))
                behind = jnp.pad(behind, ((split, 0), (0, 0)))
            ahead = self.piece(distance, 0, rows) + ahead
            behind = self.piece(-distance, 0, rows) + behind
        self.distance -= 1
        return ring.forward(ahead.astype(bf16)), ring.backward(behind.astype(bf16))

    def land(self, flight):
        self.ahead, self.behind = flight

    def total(self):
        rows = self.values[0].shape[1]
        total = self.piece(0, 0, rows) + self.ahead.astype(f32) + self.behind.astype(f32)
        return total.astype(bf16)


def gather_plain(shard, share):
    size, width = lax.axis_size("tok"), shard.shape[1]
    full = lax.all_gather(shard, "tok", axis=0)
    blocks = [
        full[:, row : row + share].reshape(8, -1, width) for row in range(0, shard.shape[0], share)
    ]
    return jnp.concatenate(blocks, axis=1)


def by_tok(values, share):
    size = lax.axis_size("tok")
    if size == 8:
        return values
    rows = share * size // 8
    blocks = [
        values[:, row : row + rows].reshape(size, share, -1)
        for row in range(0, values.shape[1], rows)
    ]
    return jnp.concatenate(blocks, axis=1)


def scatter_plain(chip):
    return lax.psum_scatter(chip, "tok", scatter_dimension=0, tiled=True)[0]


def gather_grp(values):
    step = 1
    while step < lax.axis_size("grp"):
        got = lax.ppermute(values, "grp", swap_pairs(lax.axis_size("grp"), step))
        values = jnp.concatenate([values, got])
        step *= 2
    return values


def add_x(shard):
    step = 2
    while step < lax.axis_size("grp"):
        shard = add_low(shard, lax.ppermute(shard, "grp", swap_pairs(lax.axis_size("grp"), step)))
        step *= 2
    return shard


def spread_kernel(weight_ref, out_ref, *, count):
    share = weight_ref.shape[0]
    for block in range(4):
        pieces = [
            weight_ref[:, (4 * tok + block) * share : (4 * tok + block + 1) * share]
            for tok in range(count)
        ]
        out_ref[block] = jnp.concatenate(pieces, axis=1).astype(bf16)


def spread_call(weight, count):
    share = weight.shape[0]
    return pl.pallas_call(
        functools.partial(spread_kernel, count=count),
        out_shape=jax.ShapeDtypeStruct((4, share, weight.shape[1] // 4), bf16),
        compiler_params=params(),
    )(weight)


def unspread_kernel(core_ref, mine_ref, other_ref, out_ref, *, count):
    share = mine_ref.shape[1]

    def write(refs):
        pieces = [
            refs[block // 2][block % 2, :, tok * share : (tok + 1) * share].astype(f32)
            for tok in range(count)
            for block in range(4)
        ]
        out_ref[...] = jnp.concatenate(pieces, axis=1)

    @pl.when(core_ref[0] == 0)
    def _():
        write((mine_ref, other_ref))

    @pl.when(core_ref[0] != 0)
    def _():
        write((other_ref, mine_ref))


def unspread_call(core, mine, other, count):
    share, width = mine.shape[1:]
    return pl.pallas_call(
        functools.partial(unspread_kernel, count=count),
        in_specs=[smem, whole_block(mine), whole_block(other)],
        out_shape=jax.ShapeDtypeStruct((share, 4 * width), f32),
        compiler_params=params(),
    )(core, mine, other)


def on_device(
    kept_tokens,
    kept_index,
    kept_count,
    condition,
    mask_token,
    position_table,
    modulation_weight,
    modulation_bias,
    input_weight,
    query_bias,
    value_bias,
    output_weight,
    output_bias,
    up_weight,
    up_bias,
    down_weight,
    down_bias,
    cotangent,
):
    _, seq_len, width = cotangent.shape
    tok_count = lax.axis_size("tok")
    core = lax.axis_index("grp") % 2
    share = input_weight.shape[0]
    position_rows = position_table.shape[0]

    def by_core(first, second):
        return jnp.where(core == 0, first, second)

    def exchange(values):
        return lax.all_to_all(values, "tok", split_axis=0, concat_axis=0, tiled=True)

    ring = Ring()

    core_row = jnp.stack([core, ring.x_bit])
    condition_low = jax.nn.silu(condition).astype(bf16)
    slots_here = kept_tokens.shape[1]
    small_here = jnp.concatenate(
        [
            jnp.stack([mask_token, query_bias, value_bias, output_bias, down_bias]),
            up_bias.reshape(4, share),
        ]
    ).astype(bf16)
    extra = lax.dynamic_update_slice(
        jnp.zeros((16, width), bf16), small_here, (0, share * lax.axis_index("tok"))
    )
    extra = jnp.concatenate([extra[:9], condition_low, extra[10:]])
    arrived = exchange(
        jnp.concatenate(
            [kept_tokens.astype(bf16), jnp.broadcast_to(extra, (tok_count, 16, width))], axis=1
        )
    )
    routed = arrived[:, :slots_here].reshape(-1, width)
    condition_group = arrived[:, slots_here + 9]
    small = jnp.sum(arrived[:, slots_here:].astype(f32), axis=0)

    modulation_low = modulation_weight.astype(bf16)

    def modulate_all(conditions, weight):
        modulation_part = jnp.dot(
            conditions, weight, preferred_element_type=f32
        ) + modulation_bias.astype(bf16).astype(f32)
        return exchange(modulation_part).reshape(6, width)

    condition_all = gather_grp(condition_group)

    ringed = share % 16 == 0 and lax.axis_size("grp") == 4
    table_rows = position_rows // 2

    input_low = input_weight.astype(bf16)
    input_blocks = [input_low[:, number * width : (number + 1) * width] for number in range(3)]
    position_low = position_table.astype(bf16)
    attention_low = (
        jnp.concatenate(input_blocks[:2] + [position_low[:table_rows]]),
        jnp.concatenate([input_blocks[2], output_weight.astype(bf16), position_low[table_rows:]]),
    )
    up_low = spread_call(up_weight, tok_count)
    down_low = down_weight.astype(bf16).reshape(4, share, width)
    feed_low = tuple(
        jnp.concatenate([up_low[half : half + 2], down_low[half : half + 2]]).reshape(-1, width)
        for half in (0, 2)
    )

    attention_cut, feed_cut = (7 * share // 9, 8 * share // 9), (4 * share // 3, 4 * share // 3)
    if ringed:
        mine, other = by_core(*attention_low), by_core(*attention_low[::-1])
        gather = Gather(ring, mine, other, *attention_cut)
        (flight,) = sync(gather.issue())
        gather.land(flight)
        mine, other = by_core(*feed_low), by_core(*feed_low[::-1])
        flight, mine, other, modulation_low = sync(gather.issue(), mine, other, modulation_low)
        gather.land(flight)
        feed_gather = Gather(ring, mine, other, *feed_cut)
        flight, condition_group, routed, small = sync(
            gather.issue(), condition_group, routed, small
        )
        gather.land(flight)
    mod = modulate_all(condition_group, modulation_low)
    if ringed:
        (flight,) = sync(gather.issue())
        gather.land(flight)
        feed_flight = feed_gather.issue()
        flight, mod = sync(gather.issue(), mod)
        gather.land(flight)
        (flight,) = sync(gather.issue())
        gather.land(flight)
        attention_chunks = gather.chunks()
        distances = [0]
        for distance in range(1, ring.size // 2):
            distances += [-distance, distance]
        places = ring.tok_at(jnp.array(distances + [ring.size // 2], jnp.int32))
    else:
        places = jnp.arange(8, dtype=jnp.int32)
        mine = gather_plain(by_core(*attention_low)[: 2 * share], share)
        everywhere = list(range(8))
        plain_chunks = lambda mine: Chunks(
            [(mine, "all", everywhere)], [(swap_core(mine), "all", everywhere)]
        )
        attention_chunks = plain_chunks(mine)
        feed_chunks = plain_chunks(gather_plain(by_core(*feed_low), share))
        table = lax.all_gather(position_low, "tok").reshape(8, -1, width)

    if ringed:
        table_chunks, table_row, table_share = attention_chunks, 2 * share, table_rows
    else:
        table_share = table.shape[1] // 2
        halves = table[:, :table_share], table[:, table_share:]
        table_chunks, table_row = (
            Chunks(
                [(by_core(*halves), "all", everywhere)], [(by_core(*halves[::-1]), "all", everywhere)]
            ),
            0,
        )
    start, norm_one = start_call(
        core_row, places, kept_count, kept_index, routed, small, mod, table_chunks, table_row,
        table_share, seq_len,
    )
    if ringed:
        feed_flight, start, norm_one = sync(feed_flight, start, norm_one)
        feed_gather.land(feed_flight)
    projected = project_call(core_row, places, norm_one, small, attention_chunks)
    if ringed:
        flight, projected, start = sync(feed_gather.issue(), projected, start)
        feed_gather.land(flight)
    attended = []
    for group in range(groups):
        attended.append(attend_call(projected, group))
        if ringed and group % 2:
            flight, attended, projected = sync(feed_gather.issue(), attended, projected)
            feed_gather.land(flight)
    joined, branch_one, middle, norm_two = mix_call(
        core_row, places, [pair[0] for pair in attended], start, small, mod, attention_chunks
    )
    if ringed:
        flight, norm_two = sync(feed_gather.issue(), norm_two)
        feed_gather.land(flight)
        (flight,) = sync(feed_gather.issue())
        feed_gather.land(flight)
        feed_chunks = feed_gather.chunks()
    (
        block_output,
        hidden,
        pre_grad,
        grad_two,
        middle_grad,
        grad_one,
        feed_sums,
        up_bias_sum,
    ) = feed_call(
        core_row, places, norm_two, middle, cotangent[0], branch_one, mod, small, feed_chunks
    )
    feed_other = feed_weight_call(2 - 2 * core_row[:1], norm_two, pre_grad, hidden, grad_two)
    feed_other, norm_two, grad_one = sync(feed_other, norm_two, grad_one)
    feed_mine = feed_weight_call(2 * core_row[:1], norm_two, pre_grad, hidden, grad_two)
    feed_got, feed_mine, grad_one = sync(swap_core(feed_other), feed_mine, grad_one)
    mix_grad = mix_grad_call(core_row, places, grad_one, attention_chunks)
    if ringed:
        feed_scatter = Scatter(ring, feed_mine, feed_got)
    grads = []
    for group in range(groups):
        grads.append(attend_back_call(projected, *attended[group], mix_grad, group))
        if ringed and group in (0, 2):
            flight, grads, mix_grad = sync(feed_scatter.hop(), grads, mix_grad)
            feed_scatter.land(flight)
    grads = [triple[block] for block in range(3) for triple in grads]

    def attention_weights(owner, norm):
        return attention_weight_call(owner, norm, joined, grad_one, grads)

    def start_back(half, grads):
        return start_back_call(
            half, core_row, places, kept_count, kept_index, grads, middle_grad, start, mod, attention_chunks
        )

    attention_other = attention_weights(1 - core_row[:1], norm_one)
    if ringed:
        flight, attention_other, norm_one, grads = sync(
            feed_scatter.hop(), attention_other, norm_one, grads
        )
        feed_scatter.land(flight)
        feed_flight = feed_scatter.hop()
    attention_mine = attention_weights(core_row[:1], norm_one)
    attention_got = swap_core(attention_other)
    if ringed:
        attention_mine, attention_got, grads = sync(attention_mine, attention_got, grads)
        scatter = Scatter(ring, attention_mine, attention_got)
        flight = scatter.hop()
    first_half = start_back(0, grads)
    if ringed:
        flight, feed_flight, first_half, grads = sync(flight, feed_flight, first_half, grads)
        scatter.land(flight)
        feed_scatter.land(feed_flight)
        feed_shard = feed_scatter.total()
        feed_cross = swap_x(feed_shard)
        second_half = start_back(1, grads)
        flight, second_half, feed_cross = sync(scatter.hop(), second_half, feed_cross)
        scatter.land(flight)
    else:
        second_half = start_back(1, grads)
    row_grad = jnp.concatenate([first_half[0], second_half[0]])
    slot_grad = first_half[1] + second_half[1]
    modulation_grad, small_grad = collect_call(
        first_half[2], second_half[2], feed_sums, up_bias_sum
    )

    position_grad = row_grad.reshape(tok_count, position_rows, width)
    halves = [
        half.reshape(-1, width)
        for half in (position_grad[:, :table_rows], position_grad[:, table_rows:])
    ]
    table_got = swap_core(jnp.concatenate([by_core(halves[1], halves[0]), small_grad]))
    modulation_grad_group = exchange(modulation_grad.reshape(tok_count, -1))
    if ringed:
        flight, table_got, modulation_grad_group = sync(
            scatter.hop(), table_got, modulation_grad_group
        )
        scatter.land(flight)
    table_chip = add_low(jnp.concatenate([by_core(halves[0], halves[1]), small_grad]), table_got)
    arrived = exchange(
        jnp.concatenate(
            [
                slot_grad.reshape(tok_count, -1, width),
                table_chip[:-16].reshape(tok_count, table_rows, width),
                jnp.broadcast_to(table_chip[-16:], (tok_count, 16, width)),
            ],
            axis=1,
        )
    )
    modulation_grad_all = gather_grp(modulation_grad_group)
    condition_part = jnp.einsum(
        "ie,de->id", modulation_grad_group, modulation_low, preferred_element_type=f32
    )
    modulation_total = jnp.einsum(
        "id,ie->de", condition_all, modulation_grad_all, preferred_element_type=f32
    )
    modulation_bias_total = jnp.sum(modulation_grad_all.astype(f32), axis=0)
    if ringed:
        flight, condition_part, modulation_total, modulation_bias_total = sync(
            scatter.hop(), condition_part, modulation_total, modulation_bias_total
        )
        scatter.land(flight)
    condition_part, arrived = sync(condition_part, arrived)
    condition_parts = exchange(condition_part)
    kept_low = arrived[:, :slots_here]
    table_shard = add_x(jnp.sum(arrived[:, slots_here:].astype(f32), axis=0).astype(bf16))
    if ringed:
        attention_shard = add_x(scatter.total())
        feed_shard = add_low(feed_shard, feed_cross)
    else:
        attention_chip = by_tok(add_low(attention_mine, attention_got), share)
        attention_shard = add_x(scatter_plain(attention_chip))
        feed_shard = add_x(scatter_plain(by_tok(add_low(feed_mine, feed_got), share)))
    table_far = swap_core(table_shard[:table_rows])
    first, second = by_core(table_shard[:table_rows], table_far), by_core(table_far, table_shard[:table_rows])
    position_total = jnp.concatenate([first, second]).astype(f32)
    small_total = lax.dynamic_slice_in_dim(
        table_shard[table_rows:], share * lax.axis_index("tok"), share, 1
    ).astype(f32)
    mask_total, query_bias_total, value_bias_total, output_bias_total, down_bias_total = (
        small_total[number] for number in range(5)
    )
    up_bias_total = small_total[5:9].reshape(-1)
    kept_grad = kept_low.astype(f32)
    far = swap_core(attention_shard)
    first, second = by_core(attention_shard, far).astype(f32), by_core(far, attention_shard).astype(f32)
    input_total = jnp.concatenate([first[:share], first[share:], second[:share]], axis=1)
    output_total = second[share:]
    feed_shard = feed_shard.reshape(4, share, width)
    feed_far = swap_core(feed_shard)
    up_total = unspread_call(core_row, feed_shard[:2], feed_far[:2], tok_count)
    down_total = jnp.concatenate(
        [by_core(feed_shard[2:], feed_far[2:]), by_core(feed_far[2:], feed_shard[2:])]
    ).reshape(-1, width).astype(f32)

    condition_low_grad = jnp.sum(condition_parts, axis=0, keepdims=True)
    _, silu_back = jax.vjp(jax.nn.silu, condition)
    condition_grad = silu_back(condition_low_grad)[0]
    return (
        block_output[None],
        kept_grad,
        condition_grad,
        mask_total,
        position_total,
        modulation_total,
        modulation_bias_total,
        input_total,
        query_bias_total,
        value_bias_total,
        output_total,
        output_bias_total,
        up_total,
        up_bias_total,
        down_total,
        down_bias_total,
    )


def solution(mesh):
    return jax.shard_map(
        on_device,
        mesh=mesh,
        in_specs=(
            P("grp", "tok", None),
            P(("grp", "tok"), None),
            P(("grp", "tok")),
            P(("grp", "tok"), None),
            P("tok"),
            P("tok", None),
            P(None, "tok"),
            P("tok"),
            P("tok", None),
            P("tok"),
            P("tok"),
            P("tok", None),
            P("tok"),
            P("tok", None),
            P("tok"),
            P("tok", None),
            P("tok"),
            P(("grp", "tok"), None, None),
        ),
        out_specs=(
            P(("grp", "tok"), None, None),
            P("grp", "tok", None),
            P(("grp", "tok"), None),
            P("tok"),
            P("tok", None),
            P(None, "tok"),
            P("tok"),
            P("tok", None),
            P("tok"),
            P("tok"),
            P("tok", None),
            P("tok"),
            P("tok", None),
            P("tok"),
            P("tok", None),
            P("tok"),
        ),
        check_vma=False,
    )
```

```python
import functools
import math

import jax
import jax.numpy as jnp
from jax import lax
from jax.experimental import pallas as pl
from jax.experimental.pallas import tpu as pltpu
from jax.sharding import PartitionSpec as P

H = 16
HD = 72
LANES = 128

epsilon = 1e-06
f32 = jnp.float32
bf16 = jnp.bfloat16
plain = (((1,), (0,)), ((), ()))
right_turned = (((1,), (1,)), ((), ()))
left_turned = (((0,), (0,)), ((), ()))
vmem_limit = 60 << 20


def product(left, right, dims=plain):
    return lax.dot_general(left, right, dims, preferred_element_type=f32)


def whole_block(array):
    zeros = (0,) * array.ndim
    return pl.BlockSpec(array.shape, lambda *_: zeros)


def row_block(rows, *rest):
    return pl.BlockSpec((rows,) + rest, lambda i: (i,) + (0,) * len(rest))


smem = pl.BlockSpec(memory_space=pltpu.SMEM)
anywhere = pl.BlockSpec(memory_space=pl.ANY)


def params():
    return pltpu.CompilerParams(vmem_limit_bytes=vmem_limit)


def cost(flops, moved, exps=0):
    return pl.CostEstimate(flops=int(flops), bytes_accessed=int(moved), transcendentals=int(exps))


def column_sum(values):
    return jnp.sum(values, axis=0, keepdims=True)


def normalize(values):
    center = values - jnp.mean(values, axis=-1, keepdims=True)
    spread = jnp.mean(center * center, axis=-1, keepdims=True)
    inverse = lax.rsqrt(spread + epsilon)
    return center * inverse, inverse


def normalize_back(grad, unit, inverse, scale):
    scaled = grad * (1.0 + scale)
    first = jnp.mean(scaled, axis=-1, keepdims=True)
    second = jnp.mean(scaled * unit, axis=-1, keepdims=True)
    return (scaled - first - unit * second) * inverse


def start_kernel(core_ref, places_ref, count_ref, index_ref, kept_ref, small_ref, mod_ref, *rest, chunks, row, share):
    refs, (start_ref, norm_ref, table, sems) = rest[: len(chunks.arrays)], rest[len(chunks.arrays) :]
    rows, slots = start_ref.shape[0], index_ref.shape[1]
    step = pl.program_id(0)
    low, high = table.at[:, :share], table.at[:, share:]

    @pl.when(step == 0)
    def _():
        @pl.when(core_ref[0] == 0)
        def _():
            chunks.load(refs, places_ref, core_ref, True, row, low, sems.at[0])
            chunks.load(refs, places_ref, core_ref, False, row, high, sems.at[1])

        @pl.when(core_ref[0] != 0)
        def _():
            chunks.load(refs, places_ref, core_ref, False, row, low, sems.at[0])
            chunks.load(refs, places_ref, core_ref, True, row, high, sems.at[1])

        wait_block(low, sems.at[0])
        wait_block(high, sems.at[1])

    base = step * rows
    here = lax.broadcasted_iota(jnp.int32, (rows, slots), 0) + base
    slot = lax.broadcasted_iota(jnp.int32, (rows, slots), 1)
    chosen = jnp.where((index_ref[...] == here) & (slot < count_ref[0]), 1.0, 0.0)
    kept = kept_ref[:, : slots // kept_ref.shape[0]].reshape(slots, -1)
    filled = product(chosen.astype(bf16), kept)
    empty = 1.0 - jnp.sum(chosen, axis=1, keepdims=True)
    groups_here = rows // table.shape[1]
    position = table[pl.ds(step * groups_here, groups_here)].reshape(rows, -1)
    start = filled + empty * small_ref[0:1] + position.astype(f32)
    start_ref[...] = start
    unit, _ = normalize(start)
    norm_ref[...] = (unit * (1.0 + mod_ref[1:2]) + mod_ref[0:1]).astype(bf16)


def start_call(core, places, count, index, kept, small, mod, chunks, row, share, seq_len):
    width = kept.shape[2]
    rows = seq_len // 4
    return pl.pallas_call(
        functools.partial(start_kernel, chunks=chunks, row=row, share=share),
        grid=(4,),
        in_specs=[
            smem,
            smem,
            smem,
            whole_block(index),
            whole_block(kept),
            whole_block(small),
            whole_block(mod),
        ]
        + chunks.specs,
        out_specs=[row_block(rows, width)] * 2,
        out_shape=[
            jax.ShapeDtypeStruct((seq_len, width), f32),
            jax.ShapeDtypeStruct((seq_len, width), bf16),
        ],
        scratch_shapes=[
            pltpu.VMEM((8, seq_len // 8, width), bf16),
            pltpu.SemaphoreType.DMA((2,)),
        ],
        compiler_params=params(),
        cost_estimate=cost(2 * seq_len * width * index.shape[1], 14 * seq_len * width),
    )(core, places, count, index, kept, small, mod, *chunks.arrays)


class Chunks:
    def __init__(self, mine, other, part=0, middle=0, stride=0):
        self.sources = list(mine), list(other)
        self.part, self.middle, self.stride = part, middle, stride
        self.arrays = [entry[0] for source in self.sources for entry in source]
        self.specs = [anywhere] * len(self.arrays)

    def span(self, kind, bit):
        part, middle = self.part, self.middle
        start = part * bit
        return {
            "piece": (start, start + part + middle),
            "first": (start, start + middle),
            "second": (start + middle, start + part + middle),
            "got": ((0, part) if bit else (part + middle, 2 * part + middle)),
            "all": (0, 1 << 20),
        }[kind]

    def spans(self, kind, bit):
        if kind == "pair":
            return [self.span("piece", bit) + (0,), self.span("got", bit) + (self.part + self.middle,)]
        return [self.span(kind, bit) + (0,)]

    def load(self, refs, places_ref, spot_ref, from_mine, row, target, sem):
        source = self.sources[0 if from_mine else 1]
        refs = refs[: len(source)] if from_mine else refs[len(self.sources[0]) :]

        def start(ref, kind, places, bit):
            for low, high, base in self.spans(kind, bit):
                begin, end = max(row, low), min(row + target.shape[1], high)
                for index, place in enumerate(places if begin < end else []):
                    pltpu.make_async_copy(
                        ref.at[index, pl.ds(base + begin - low, end - begin)],
                        target.at[places_ref[place], pl.ds(begin - row, end - begin)],
                        sem,
                    ).start()

        for ref, (_, kind, places) in zip(refs, source):
            if kind == "all":
                start(ref, kind, places, 0)
        if any(kind != "all" for _, kind, _ in source):
            for bit in (0, 1):

                @pl.when(spot_ref[1] == bit)
                def _():
                    for ref, (_, kind, places) in zip(refs, source):
                        if kind != "all":
                            start(ref, kind, places, bit)

    def load_block(self, refs, places_ref, spot_ref, block, target, sem, first=0):
        rows = target.shape[1]
        owner, row = block // 2, first * rows + (block % 2) * (self.stride or rows)

        @pl.when(spot_ref[0] == owner)
        def _():
            self.load(refs, places_ref, spot_ref, True, row, target, sem)

        @pl.when(spot_ref[0] != owner)
        def _():
            self.load(refs, places_ref, spot_ref, False, row, target, sem)


def wait_block(target, sem):
    pltpu.make_async_copy(target, target, sem).wait()


def square(weight):
    return weight.reshape(-1, weight.shape[-1])


def split_heads(values, store):
    rows = values.shape[0]
    blank = jnp.zeros((rows, LANES - HD), values.dtype)
    for head in range(H):
        store(head, jnp.concatenate([values[:, head * HD : (head + 1) * HD], blank], axis=1))


def project_kernel(core_ref, places_ref, norm_ref, small_ref, *rest, chunks):
    refs, (out_ref, weight, sems) = rest[: len(chunks.arrays)], rest[len(chunks.arrays) :]
    step = pl.program_id(0)

    @pl.when(step == 0)
    def _():
        for block in range(3):
            chunks.load_block(refs, places_ref, core_ref, block, weight.at[block], sems.at[block])

    wait_block(weight.at[step], sems.at[step])
    key_free = jnp.where(step == 1, 0.0, 1.0)
    bias = jnp.where(step == 0, small_ref[1:2], small_ref[2:3]) * key_free
    half = norm_ref.shape[0] // 2
    for part in range(2):
        rows = slice(part * half, (part + 1) * half)
        result = product(norm_ref[rows], square(weight[step])) + bias

        def store(head, value):
            out_ref[0, head, rows] = value

        split_heads(result.astype(bf16), store)


def project_call(core, places, norm, small, chunks):
    seq_len, width = norm.shape
    return pl.pallas_call(
        functools.partial(project_kernel, chunks=chunks),
        grid=(3,),
        in_specs=[
            smem,
            smem,
            whole_block(norm),
            whole_block(small),
        ]
        + chunks.specs,
        out_specs=pl.BlockSpec((1, H, seq_len, LANES), lambda i: (i, 0, 0, 0)),
        out_shape=jax.ShapeDtypeStruct((3, H, seq_len, LANES), bf16),
        scratch_shapes=[
            pltpu.VMEM((3, 8, width // 8, width), bf16),
            pltpu.SemaphoreType.DMA((3,)),
        ],
        compiler_params=params(),
        cost_estimate=cost(6 * seq_len * width * width, 12 * seq_len * width + 6 * width * width),
    )(core, places, norm, small, *chunks.arrays)


def attend_kernel(query_ref, key_ref, value_ref, *rest, size, factor):
    mix_ref, log_ref = rest[-2:]
    turned_value = value_ref[0, 0].T
    for part in range(query_ref.shape[2] // size):
        rows = slice(part * size, (part + 1) * size)
        scores = product(key_ref[0, 0], query_ref[0, 0, rows], right_turned)
        top = jnp.max(scores, axis=0, keepdims=True)
        weights = jnp.exp2((scores - top) * factor)
        total = jnp.sum(weights, axis=0, keepdims=True)
        mix = product(turned_value, weights.astype(bf16))
        mix_ref[0, rows] = (mix / total).T.astype(bf16)
        log_ref[0, :, rows] = top * factor + jnp.log2(total)


forward_groups = ((0, 8), (8, 8))
back_groups = ((0, 4), (4, 8), (12, 4))
groups = len(back_groups)


def head_block(place, seq_len, first):
    return pl.BlockSpec((1, 1, seq_len, LANES), lambda h: (place, first + h, 0, 0))


def attend_call(projected, first, heads, earlier=None):
    seq_len = projected.shape[2]
    kept = [] if earlier is None else list(earlier)
    return pl.pallas_call(
        functools.partial(
            attend_kernel, size=seq_len, factor=math.log2(math.e) / math.sqrt(HD)
        ),
        grid=(heads,),
        in_specs=[head_block(place, seq_len, first) for place in range(3)] + [anywhere] * len(kept),
        out_specs=[
            pl.BlockSpec((1, seq_len, LANES), lambda h: (first + h, 0, 0)),
            pl.BlockSpec((1, 1, seq_len), lambda h: (first + h, 0, 0)),
        ],
        out_shape=[
            jax.ShapeDtypeStruct((H, seq_len, LANES), bf16),
            jax.ShapeDtypeStruct((H, 1, seq_len), f32),
        ],
        input_output_aliases={3: 0, 4: 1} if kept else {},
        compiler_params=params(),
        cost_estimate=cost(4 * heads * seq_len * seq_len * 256, 8 * heads * seq_len * LANES, heads * seq_len * seq_len),
    )(projected, projected, projected, *kept)


def attend_back_kernel(
    query_ref, key_ref, value_ref, mix_ref, log_ref, grad_ref, query_grad_ref, key_grad_ref,
    value_grad_ref, key_sum, value_sum, *, size, factor
):
    key, value = key_ref[0, 0], value_ref[0, 0]
    turned_key = key.T
    base_two = factor * math.log2(math.e)
    for part in range(query_ref.shape[2] // size):
        rows = slice(part * size, (part + 1) * size)
        query, grad = query_ref[0, 0, rows], grad_ref[0, rows]
        scores = product(key, query, right_turned)
        weights = jnp.exp2(scores * base_two - log_ref[0, :, rows])
        value_part = product(weights.astype(bf16), grad)
        weight_grad = product(value, grad, right_turned)
        inner = column_sum((grad.astype(f32) * mix_ref[0, rows].astype(f32)).T)
        score_grad = (weights * (weight_grad - inner)).astype(bf16)
        key_part = product(score_grad, query)
        query_grad_ref[0, rows] = (product(turned_key, score_grad) * factor).T.astype(bf16)
        if part == 0:
            key_sum[...] = key_part
            value_sum[...] = value_part
        else:
            key_sum[...] += key_part
            value_sum[...] += value_part
    key_grad_ref[0] = (key_sum[...] * factor).astype(bf16)
    value_grad_ref[0] = value_sum[...].astype(bf16)


def attend_back_call(projected, attended, grad, first, heads):
    seq_len = projected.shape[2]
    mix, logs = attended
    flat = pl.BlockSpec((1, seq_len, LANES), lambda h: (h, 0, 0))
    return pl.pallas_call(
        functools.partial(attend_back_kernel, size=seq_len // 2, factor=1.0 / math.sqrt(HD)),
        grid=(heads,),
        in_specs=[head_block(place, seq_len, first) for place in range(3)]
        + [
            pl.BlockSpec((1, seq_len, LANES), lambda h: (first + h, 0, 0)),
            pl.BlockSpec((1, 1, seq_len), lambda h: (first + h, 0, 0)),
            pl.BlockSpec((1, seq_len, LANES), lambda h: (first + h, 0, 0)),
        ],
        out_specs=[flat] * 3,
        out_shape=[jax.ShapeDtypeStruct((heads, seq_len, LANES), bf16)] * 3,
        scratch_shapes=[pltpu.VMEM((seq_len, LANES), f32)] * 2,
        compiler_params=params(),
        cost_estimate=cost(10 * heads * seq_len * seq_len * 256, 16 * heads * seq_len * LANES, heads * seq_len * seq_len),
    )(projected, projected, projected, mix, logs, grad)


def join_heads(refs):
    return jnp.concatenate(
        [ref[head][:, :HD] for ref in refs for head in range(ref.shape[0])], axis=1
    )


def mix_kernel(core_ref, places_ref, start_ref, small_ref, mod_ref, *rest, chunks):
    mix_refs, rest = rest[:1], rest[1:]
    refs, rest = rest[: len(chunks.arrays)], rest[len(chunks.arrays) :]
    joined_ref, branch_ref, middle_ref, norm_ref, weight, sem = rest

    @pl.when(pl.program_id(0) == 0)
    def _():
        chunks.load_block(refs, places_ref, core_ref, 3, weight, sem)
        wait_block(weight, sem)

    joined = join_heads(mix_refs)
    joined_ref[...] = joined
    branch = product(joined, square(weight[...])) + small_ref[3:4]
    branch_ref[...] = branch
    middle = start_ref[...] + mod_ref[2:3] * branch
    middle_ref[...] = middle
    unit, _ = normalize(middle)
    norm_ref[...] = (unit * (1.0 + mod_ref[4:5]) + mod_ref[3:4]).astype(bf16)


def mix_call(core, places, mix, start, small, mod, chunks):
    seq_len, width = start.shape
    rows = seq_len // 4
    block = row_block(rows, width)
    return pl.pallas_call(
        functools.partial(mix_kernel, chunks=chunks),
        grid=(4,),
        in_specs=[smem, smem, block, whole_block(small), whole_block(mod)]
        + [pl.BlockSpec((H, rows, LANES), lambda i: (0, i, 0))]
        + chunks.specs,
        out_specs=[block] * 4,
        out_shape=[
            jax.ShapeDtypeStruct((seq_len, width), kind) for kind in (bf16, f32, f32, bf16)
        ],
        scratch_shapes=[pltpu.VMEM((8, width // 8, width), bf16), pltpu.SemaphoreType.DMA],
        compiler_params=params(),
        cost_estimate=cost(2 * seq_len * width * width, 18 * seq_len * width),
    )(core, places, start, small, mod, mix, *chunks.arrays)


def gelu_parts(values):
    inner = 0.7978845608028654 * (values + 0.044715 * values * values * values)
    turned = jnp.tanh(inner)
    half = 0.5 * (1.0 + turned)
    slope = half + 0.5 * values * (1.0 - turned * turned) * (
        0.7978845608028654 * (1.0 + 0.134145 * values * values)
    )
    return values * half, slope


def feed_kernel(
    core_ref, places_ref, norm_ref, middle_ref, cot_ref, branch_ref, mod_ref, small_ref, *rest, source
):
    refs, rest = rest[: len(source.arrays)], rest[len(source.arrays) :]
    (
        out_ref, hidden_ref, pre_ref, grad_two_ref, middle_grad_ref, grad_one_ref, sums_ref,
        up_sums_ref, up, down, slopes, sems,
    ) = rest
    step = pl.program_id(0)
    chunks = 4

    @pl.when(step == 0)
    def _():
        for chunk in range(chunks):
            for side, target in enumerate((up, down)):
                source.load_block(
                    refs, places_ref, core_ref, chunk, target.at[chunk], sems.at[side, chunk], 2 * side
                )
        sums_ref[...] = jnp.zeros_like(sums_ref)
        up_sums_ref[...] = jnp.zeros_like(up_sums_ref)

    norm = norm_ref[...]
    total = None
    for chunk in range(chunks):

        @pl.when(step == 0)
        def _():
            wait_block(up.at[chunk], sems.at[0, chunk])
            wait_block(down.at[chunk], sems.at[1, chunk])

        before = product(norm, square(up[chunk])) + small_ref[5 + chunk : 6 + chunk]
        hidden, slope = gelu_parts(before)
        hidden = hidden.astype(bf16)
        hidden_ref[chunk] = hidden
        slopes[chunk] = slope.astype(slopes.dtype)
        part = product(hidden, square(down[chunk]))
        total = part if total is None else total + part
    branch_two = total + small_ref[4:5]
    middle, cot = middle_ref[...], cot_ref[...]
    gate_two = mod_ref[5:6]
    out_ref[...] = middle + gate_two * branch_two
    grad_two = (gate_two * cot).astype(bf16)
    grad_two_ref[...] = grad_two
    sums_ref[0:1] += column_sum(cot * branch_two)
    sums_ref[1:2] += column_sum(grad_two.astype(f32))
    total = None
    for chunk in range(chunks):
        pre = (product(grad_two, square(down[chunk]), right_turned) * slopes[chunk].astype(f32)).astype(bf16)
        pre_ref[chunk] = pre
        up_sums_ref[chunk] += column_sum(pre.astype(f32))
        part = product(pre, square(up[chunk]), right_turned)
        total = part if total is None else total + part
    unit, inverse = normalize(middle)
    sums_ref[2:3] += column_sum(total * unit)
    sums_ref[3:4] += column_sum(total)
    middle_grad = cot + normalize_back(total, unit, inverse, mod_ref[4:5])
    middle_grad_ref[...] = middle_grad
    sums_ref[4:5] += column_sum(middle_grad * branch_ref[...])
    grad_one = (mod_ref[2:3] * middle_grad).astype(bf16)
    grad_one_ref[...] = grad_one
    sums_ref[5:6] += column_sum(grad_one.astype(f32))


def feed_call(core, places, norm, middle, cot, branch, mod, small, source):
    seq_len, width = middle.shape
    steps = 4
    rows = seq_len // steps
    block = row_block(rows, width)
    chunked = pl.BlockSpec((4, rows, width), lambda i: (0, i, 0))
    wide = jax.ShapeDtypeStruct((4, seq_len, width), bf16)
    return pl.pallas_call(
        functools.partial(feed_kernel, source=source),
        grid=(steps,),
        in_specs=[
            smem,
            smem,
            block,
            block,
            block,
            block,
            whole_block(mod),
            whole_block(small),
        ]
        + source.specs,
        out_specs=[
            block,
            chunked,
            chunked,
            block,
            block,
            block,
            pl.BlockSpec((8, width), lambda i: (0, 0)),
            pl.BlockSpec((4, 1, width), lambda i: (0, 0, 0)),
        ],
        out_shape=[
            jax.ShapeDtypeStruct((seq_len, width), f32),
            wide,
            wide,
            jax.ShapeDtypeStruct((seq_len, width), bf16),
            jax.ShapeDtypeStruct((seq_len, width), f32),
            jax.ShapeDtypeStruct((seq_len, width), bf16),
            jax.ShapeDtypeStruct((8, width), f32),
            jax.ShapeDtypeStruct((4, 1, width), f32),
        ],
        scratch_shapes=[
            pltpu.VMEM((4, 8, width // 8, width), bf16),
            pltpu.VMEM((4, 8, width // 8, width), bf16),
            pltpu.VMEM((4, rows, width), f32),
            pltpu.SemaphoreType.DMA((2, 4)),
        ],
        compiler_params=params(),
        cost_estimate=cost(32 * seq_len * width * width, 60 * seq_len * width, 4 * seq_len * width),
    )(core, places, norm, middle, cot, branch, mod, small, *source.arrays)


def feed_weight_kernel(first_ref, left_ref, right_ref, *rest):
    out_ref = rest[-1]
    left = left_ref[0] if left_ref.ndim == 3 else left_ref[...]
    right = right_ref[0] if right_ref.ndim == 3 else right_ref[...]
    result = product(left, right, left_turned).reshape(out_ref.shape)
    if len(rest) > 1:
        result = result + rest[0][...].astype(f32)
    out_ref[...] = result.astype(bf16)


def feed_weight_call(first, left, right, got=None, base=None, row=0, rows=2):
    width = left.shape[-1]
    seq_len = left.shape[-2]
    out_block = (8, width // 8, width)

    def spec(array):
        if array.ndim == 2:
            return pl.BlockSpec(array.shape, lambda i, f: (0, 0))
        return pl.BlockSpec((1, seq_len, width), lambda i, f: (f[0] + i, 0, 0))

    more, specs, aliases = [], [], {}
    if got is not None:
        more, specs = [got], [pl.BlockSpec(out_block, lambda i, f: (0, i, 0))]
    if base is not None:
        aliases = {3 + len(more): 0}
        more, specs = more + [base], specs + [anywhere]
    return pl.pallas_call(
        feed_weight_kernel,
        grid_spec=pltpu.PrefetchScalarGridSpec(
            num_scalar_prefetch=1,
            grid=(2,),
            in_specs=[spec(left), spec(right)] + specs,
            out_specs=pl.BlockSpec(out_block, lambda i, f: (0, row + i, 0)),
        ),
        out_shape=jax.ShapeDtypeStruct((8, rows * width // 8, width), bf16),
        input_output_aliases=aliases,
        compiler_params=params(),
        cost_estimate=cost(4 * seq_len * width * width, 8 * seq_len * width + 4 * width * width),
    )(first, left, right, *more)


def attention_weight_kernel(owner_ref, norm_ref, joined_ref, grad_ref, *rest):
    head_refs = [rest[block * groups : (block + 1) * groups] for block in range(3)]
    out_ref, left, heads, right, sems = rest[3 * groups :]
    step = pl.program_id(0)

    def copies(block, slot):
        if block == 3:
            return [(joined_ref, left.at[slot]), (grad_ref, right.at[slot])]
        return [(norm_ref, left.at[slot])] + [
            (ref, heads.at[slot, pl.ds(first, count)])
            for (first, count), ref in zip(back_groups, head_refs[block])
        ]

    @pl.when(step == 0)
    def _():
        for block in range(4):

            @pl.when(owner_ref[0] == block // 2)
            def _():
                for source, target in copies(block, block % 2):
                    pltpu.make_async_copy(source, target, sems.at[block % 2]).start()

    for block in range(4):

        @pl.when((owner_ref[0] == block // 2) & (step == block % 2))
        def _():
            slot = block % 2
            wait_block(left.at[slot], sems.at[slot])
            if block == 3:
                wait_block(right.at[slot], sems.at[slot])
            else:
                wait_block(heads.at[slot], sems.at[slot])
                right[slot] = jnp.concatenate(
                    [heads[slot, head][:, :HD] for head in range(H)], axis=1
                )

    result = product(left[step], right[step], left_turned)
    out_ref[...] = result.astype(bf16).reshape(out_ref.shape)


def attention_weight_call(owner, norm, joined, grad_one, grads):
    seq_len, width = norm.shape
    return pl.pallas_call(
        attention_weight_kernel,
        grid=(2,),
        in_specs=[smem] + [anywhere] * (3 + 3 * groups),
        out_specs=pl.BlockSpec((8, width // 8, width), lambda i: (0, i, 0)),
        out_shape=jax.ShapeDtypeStruct((8, width // 4, width), bf16),
        scratch_shapes=[
            pltpu.VMEM((2, seq_len, width), bf16),
            pltpu.VMEM((2, H, seq_len, LANES), bf16),
            pltpu.VMEM((2, seq_len, width), bf16),
            pltpu.SemaphoreType.DMA((2,)),
        ],
        compiler_params=params(),
        cost_estimate=cost(4 * seq_len * width * width, 10 * seq_len * width + 4 * width * width),
    )(owner, norm, joined, grad_one, *grads)


def mix_grad_kernel(core_ref, places_ref, grad_ref, *rest, chunks):
    refs, (out_ref, weight, sem) = rest[: len(chunks.arrays)], rest[len(chunks.arrays) :]

    @pl.when(pl.program_id(0) == 0)
    def _():
        chunks.load_block(refs, places_ref, core_ref, 3, weight, sem)
        wait_block(weight, sem)

    def store(head, value):
        out_ref[head] = value

    split_heads(product(grad_ref[...], square(weight[...]), right_turned).astype(bf16), store)


def mix_grad_call(core, places, grad_one, chunks):
    seq_len, width = grad_one.shape
    rows = seq_len // 2
    return pl.pallas_call(
        functools.partial(mix_grad_kernel, chunks=chunks),
        grid=(2,),
        in_specs=[smem, smem, row_block(rows, width)] + chunks.specs,
        out_specs=pl.BlockSpec((H, rows, LANES), lambda i: (0, i, 0)),
        out_shape=jax.ShapeDtypeStruct((H, seq_len, LANES), bf16),
        scratch_shapes=[pltpu.VMEM((8, width // 8, width), bf16), pltpu.SemaphoreType.DMA],
        compiler_params=params(),
        cost_estimate=cost(2 * seq_len * width * width, 8 * seq_len * width),
    )(core, places, grad_one, *chunks.arrays)


def start_back_kernel(
    core_ref, places_ref, count_ref, index_row_ref, index_ref, middle_grad_ref, start_ref, mod_ref,
    *rest, chunks, first
):
    grad_refs = [rest[block * groups : (block + 1) * groups] for block in range(3)]
    rest = rest[3 * groups :]
    refs, rest = rest[: len(chunks.arrays)], rest[len(chunks.arrays) :]
    row_grad_ref, slot_ref, sums_ref, weight, sems = rest[-5:]
    earlier = rest[:-5]
    rows, width = start_ref.shape
    toks, per_tok = slot_ref.shape[0], index_ref.shape[0] // slot_ref.shape[0]
    slot_count = index_ref.shape[0]

    for block in range(3):
        chunks.load_block(refs, places_ref, core_ref, block, weight.at[block], sems.at[block])
    sums = {}
    total = None
    for block, refs in enumerate(grad_refs):
        joined = join_heads(refs)
        if block != 1:
            sums[block // 2] = column_sum(joined.astype(f32))
        wait_block(weight.at[block], sems.at[block])
        part = product(joined, square(weight[block]), right_turned)
        total = part if total is None else total + part
    unit, inverse = normalize(start_ref[...])
    sums[2] = column_sum(total * unit)
    sums[3] = column_sum(total)
    row_grad = middle_grad_ref[...] + normalize_back(total, unit, inverse, mod_ref[1:2])
    row_low = row_grad.astype(bf16)
    row_grad_ref[...] = row_low
    base = first * rows
    place = lax.broadcasted_iota(jnp.int32, (slot_count, rows), 1) + base
    slot = lax.broadcasted_iota(jnp.int32, (slot_count, rows), 0)
    chosen = jnp.where((index_ref[...] == place) & (slot < count_ref[0]), 1.0, 0.0)
    part = product(chosen.astype(bf16), row_low)

    part = part.astype(bf16).reshape(toks, per_tok, width)
    if earlier:
        part = part + earlier[0][:, :per_tok]
    slot_ref[:, :per_tok] = part
    here = lax.broadcasted_iota(jnp.int32, (rows, slot_count), 0) + base
    lane = lax.broadcasted_iota(jnp.int32, (rows, slot_count), 1)
    taken = jnp.where((index_row_ref[...] == here) & (lane < count_ref[0]), 1.0, 0.0)
    empty = 1.0 - jnp.sum(taken, axis=1, keepdims=True)
    sums[4] = column_sum(row_grad * empty)
    sums_ref[...] = jnp.concatenate(
        [sums[number] for number in range(5)] + [jnp.zeros((3, width), f32)]
    )


def start_back_call(quarter, earlier, core, places, count, index, grads, middle_grad, start, mod, chunks):
    seq_len, width = start.shape
    slot_count = index.shape[1]
    toks = lax.axis_size("tok")
    rows = seq_len // 4
    heads = [
        pl.BlockSpec((array.shape[0], rows, LANES), lambda i: (0, quarter, 0)) for array in grads
    ]
    block = pl.BlockSpec((rows, width), lambda i: (quarter, 0))
    kept = [] if earlier is None else [earlier]
    column = index.reshape(slot_count, 1)
    return pl.pallas_call(
        functools.partial(start_back_kernel, chunks=chunks, first=quarter),
        grid=(1,),
        in_specs=[
            smem,
            smem,
            smem,
            whole_block(index),
            whole_block(column),
            block,
            block,
            whole_block(mod),
        ]
        + heads
        + chunks.specs
        + [whole_block(array) for array in kept],
        out_specs=[
            row_block(rows, width),
            pl.BlockSpec((toks, slot_count // toks + 8, width), lambda i: (0, 0, 0)),
            pl.BlockSpec((8, width), lambda i: (0, 0)),
        ],
        out_shape=[
            jax.ShapeDtypeStruct((rows, width), bf16),
            jax.ShapeDtypeStruct((toks, slot_count // toks + 8, width), bf16),
            jax.ShapeDtypeStruct((8, width), f32),
        ],
        scratch_shapes=[
            pltpu.VMEM((3, 8, width // 8, width), bf16),
            pltpu.SemaphoreType.DMA((3,)),
        ],
        compiler_params=params(),
        cost_estimate=cost(2 * seq_len * width * width, 7 * seq_len * width),
    )(core, places, count, index, column, middle_grad, start, mod, *grads, *chunks.arrays, *kept)


def collect_kernel(feed_ref, up_ref, *rest):
    *start_refs, _, mod_ref, small_ref = rest
    start = start_refs[0][...]
    for ref in start_refs[1:]:
        start = start + ref[...]
    feed = feed_ref[...]
    row = lambda values, number: values[number : number + 1]
    blank = jnp.zeros((7, start.shape[1]), f32)
    width = start.shape[1]
    rows = [row(start, 3), row(start, 2), row(feed, 4), row(feed, 3), row(feed, 2), row(feed, 0)]
    share = 6 * width // mod_ref.shape[0]
    for tok in range(mod_ref.shape[0]):
        place, left, pieces = tok * share, share, []
        while left:
            within = place % width
            count = min(left, width - within)
            pieces.append(rows[place // width][:, within : within + count])
            place, left = place + count, left - count
        pieces.append(jnp.zeros((1, width - share), f32))
        line = jnp.concatenate(pieces, axis=1)
        mod_ref[tok] = jnp.broadcast_to(line, (8, width)).astype(bf16)
    small_ref[...] = jnp.concatenate(
        [row(start, 4), row(start, 0), row(start, 1), row(feed, 5), row(feed, 1)]
        + [up_ref[block] for block in range(4)]
        + [blank]
    ).astype(bf16)


def collect_call(feed, up, slots, *starts):
    toks, rows, width = slots.shape
    return pl.pallas_call(
        collect_kernel,
        grid=(1,),
        in_specs=[whole_block(feed), whole_block(up)]
        + [whole_block(start) for start in starts]
        + [anywhere],
        out_specs=[
            pl.BlockSpec((toks, 8, width), lambda i: (0, rows // 8 - 1, 0)),
            pl.BlockSpec((16, width), lambda i: (0, 0)),
        ],
        out_shape=[
            jax.ShapeDtypeStruct(slots.shape, bf16),
            jax.ShapeDtypeStruct((16, width), bf16),
        ],
        input_output_aliases={2 + len(starts): 0},
        compiler_params=params(),
    )(feed, up, *starts, slots)


def swap_pairs(size, bit):
    return [(place, place ^ bit) for place in range(size)]


def swap_core(values):
    return lax.ppermute(values, "grp", swap_pairs(lax.axis_size("grp"), 1))


def add_low(*parts):
    total = parts[0].astype(f32)
    for part in parts[1:]:
        total = total + part.astype(f32)
    return total.astype(bf16)


def swap_x(values):
    return lax.ppermute(values, "grp", swap_pairs(lax.axis_size("grp"), 2))


class Ring:
    def __init__(self):
        size = lax.axis_size("tok")
        self.size = size
        order = list(range(0, size, 2)) + list(range(1, size, 2))[::-1]
        self.ahead = [(order[i], order[(i + 1) % size]) for i in range(size)]
        self.behind = [(after, before) for before, after in self.ahead]
        tok = lax.axis_index("tok")
        self.place = jnp.where(tok % 2 == 0, tok // 2, size - 1 - tok // 2)
        self.x_bit = (lax.axis_index("grp") // 2) % 2

    def tok_at(self, distance):
        place = (self.place + distance) % self.size
        return jnp.where(place < self.size // 2, 2 * place, 2 * (self.size - 1 - place) + 1)

    def forward(self, values):
        return lax.ppermute(values, "tok", self.ahead)

    def backward(self, values):
        return lax.ppermute(values, "tok", self.behind)


def sync(*values):
    return lax.optimization_barrier(values)


class Gather:
    def __init__(self, ring, mine, other, part, middle):
        self.ring, self.part, self.middle = ring, part, middle
        self.mine, self.other = [(mine[None], "all", [0])], [(other[None], "all", [0])]
        payload = lax.dynamic_slice_in_dim(mine, part * ring.x_bit, part + middle, 0)
        self.pieces = [payload, payload]
        self.distance = 0
        self.own = None
        self.making, self.ready = [], []

    def issue(self):
        ring, flight = self.ring, {}
        middle, half = self.middle, ring.size // 2
        if self.distance == half:
            self.ready, self.making = self.ready + self.making, []
        flight["pair"] = [array for array, _ in self.making]
        self.made = [places for _, places in self.making]
        self.making = []
        flight["core"] = [swap_core(array) for array, _ in self.ready]
        self.sent = [places for _, places in self.ready]
        if self.distance < half:
            self.distance += 1
            ahead, behind = self.pieces
            if self.distance == half:
                ahead, behind = ahead[:middle], behind[middle:]
            flight["ring"] = [ring.forward(ahead), ring.backward(behind)]
        if self.own is not None:
            flight["x"] = swap_x(self.own)
        return flight

    def land(self, flight):
        bit, part, middle = self.ring.x_bit, self.part, self.middle
        self.other += [(array, "pair", places) for array, places in zip(flight["core"], self.sent)]
        self.ready = list(zip(flight["pair"], self.made))
        self.own = None
        if "x" in flight:
            got = flight["x"]
            self.mine.append((got, "got", self.places))
            if len(self.places) == 1:
                ahead, behind = self.pieces
                pair = jnp.concatenate([ahead, behind, got[0]])[None]
            else:
                pair = jnp.concatenate([jnp.stack(self.pieces), got], axis=1)
            self.making = [(pair, self.places)]
        if "ring" in flight:
            ahead, behind = self.pieces = flight["ring"]
            place = 2 * self.distance - 1
            if self.distance == self.ring.size // 2:
                self.places = [place]
                self.mine += [(ahead[None], "first", [place]), (behind[None], "second", [place])]
                self.own = jnp.where(bit == 0, ahead[:part], behind)[None]
            else:
                self.places = [place, place + 1]
                self.mine += [(ahead[None], "piece", [place]), (behind[None], "piece", [place + 1])]
                self.own = jnp.stack(
                    [
                        lax.dynamic_slice_in_dim(piece, middle * bit, part, 0)
                        for piece in self.pieces
                    ]
                )

    def chunks(self, stride=0):
        return Chunks(self.mine, self.other, self.part, self.middle, stride)

    def rows(self, first, count):
        bit, part, middle = self.ring.x_bit, self.part, self.middle
        low = first - part
        ahead, behind = self.pieces
        parts = [self.mine[0][0][0, first : first + count]]
        for array, kind, _ in self.mine:
            if kind == "piece":
                parts.append(lax.dynamic_slice_in_dim(array[0], first - part * bit, count, 0))
        parts.append(jnp.where(bit == 0, behind[first - middle :][:count], ahead[low:][:count]))
        return jnp.stack(parts)


class Scatter:
    def __init__(self, ring, *values):
        self.ring, self.values = ring, values
        self.distance = ring.size // 2
        self.split = values[0].shape[1] // 2

    def piece(self, place, row, count):
        tok, width = self.ring.tok_at(place), self.values[0].shape[2]
        return sum(
            lax.dynamic_slice(values, (tok, row, 0), (1, count, width))[0].astype(f32)
            for values in self.values
        )

    def hop(self):
        ring, distance, split = self.ring, self.distance, self.split
        rows = self.values[0].shape[1]
        if distance == ring.size // 2:
            ahead = self.piece(distance, 0, split)
            behind = self.piece(distance, split, rows - split)
        else:
            ahead, behind = self.ahead.astype(f32), self.behind.astype(f32)
            if distance == ring.size // 2 - 1:
                ahead = jnp.pad(ahead, ((0, rows - split), (0, 0)))
                behind = jnp.pad(behind, ((split, 0), (0, 0)))
            ahead = self.piece(distance, 0, rows) + ahead
            behind = self.piece(-distance, 0, rows) + behind
        self.distance -= 1
        return ring.forward(ahead.astype(bf16)), ring.backward(behind.astype(bf16))

    def land(self, flight):
        self.ahead, self.behind = flight

    def total(self):
        rows = self.values[0].shape[1]
        total = self.piece(0, 0, rows) + self.ahead.astype(f32) + self.behind.astype(f32)
        return total.astype(bf16)


def gather_plain(shard, share):
    size, width = lax.axis_size("tok"), shard.shape[1]
    full = lax.all_gather(shard, "tok", axis=0)
    blocks = [
        full[:, row : row + share].reshape(8, -1, width) for row in range(0, shard.shape[0], share)
    ]
    return jnp.concatenate(blocks, axis=1)


def by_tok(values, share):
    size = lax.axis_size("tok")
    if size == 8:
        return values
    rows = share * size // 8
    blocks = [
        values[:, row : row + rows].reshape(size, share, -1)
        for row in range(0, values.shape[1], rows)
    ]
    return jnp.concatenate(blocks, axis=1)


def scatter_plain(chip):
    return lax.psum_scatter(chip, "tok", scatter_dimension=0, tiled=True)[0]


def gather_grp(values):
    step = 1
    while step < lax.axis_size("grp"):
        got = lax.ppermute(values, "grp", swap_pairs(lax.axis_size("grp"), step))
        values = jnp.concatenate([values, got])
        step *= 2
    return values


def add_x(shard):
    step = 2
    while step < lax.axis_size("grp"):
        shard = add_low(shard, lax.ppermute(shard, "grp", swap_pairs(lax.axis_size("grp"), step)))
        step *= 2
    return shard


def spread_kernel(weight_ref, out_ref, *, count):
    share = weight_ref.shape[0]
    for block in range(4):
        pieces = [
            weight_ref[:, (4 * tok + block) * share : (4 * tok + block + 1) * share]
            for tok in range(count)
        ]
        out_ref[block] = jnp.concatenate(pieces, axis=1).astype(bf16)


def spread_call(weight, count):
    share = weight.shape[0]
    return pl.pallas_call(
        functools.partial(spread_kernel, count=count),
        out_shape=jax.ShapeDtypeStruct((4, share, weight.shape[1] // 4), bf16),
        compiler_params=params(),
    )(weight)


def unspread_kernel(core_ref, mine_ref, other_ref, out_ref, *, count):
    share = mine_ref.shape[1]

    def write(refs):
        pieces = [
            refs[block // 2][block % 2, :, tok * share : (tok + 1) * share].astype(f32)
            for tok in range(count)
            for block in range(4)
        ]
        out_ref[...] = jnp.concatenate(pieces, axis=1)

    @pl.when(core_ref[0] == 0)
    def _():
        write((mine_ref, other_ref))

    @pl.when(core_ref[0] != 0)
    def _():
        write((other_ref, mine_ref))


def unspread_call(core, mine, other, count):
    share, width = mine.shape[1:]
    return pl.pallas_call(
        functools.partial(unspread_kernel, count=count),
        in_specs=[smem, whole_block(mine), whole_block(other)],
        out_shape=jax.ShapeDtypeStruct((share, 4 * width), f32),
        compiler_params=params(),
    )(core, mine, other)


def on_device(
    kept_tokens,
    kept_index,
    kept_count,
    condition,
    mask_token,
    position_table,
    modulation_weight,
    modulation_bias,
    input_weight,
    query_bias,
    value_bias,
    output_weight,
    output_bias,
    up_weight,
    up_bias,
    down_weight,
    down_bias,
    cotangent,
):
    _, seq_len, width = cotangent.shape
    tok_count = lax.axis_size("tok")
    core = lax.axis_index("grp") % 2
    share = input_weight.shape[0]
    position_rows = position_table.shape[0]

    def by_core(first, second):
        return jnp.where(core == 0, first, second)

    def by_core_pair(pairs):
        return [by_core(first, second) for first, second in zip(*pairs)]

    def exchange(values):
        return lax.all_to_all(values, "tok", split_axis=0, concat_axis=0, tiled=True)

    ring = Ring()

    core_row = jnp.stack([core, ring.x_bit])
    condition_low = jax.nn.silu(condition).astype(bf16)
    slots_here = kept_tokens.shape[1]
    small_here = jnp.concatenate(
        [
            jnp.stack([mask_token, query_bias, value_bias, output_bias, down_bias]),
            up_bias.reshape(4, share),
        ]
    ).astype(bf16)
    extra = lax.dynamic_update_slice(
        jnp.zeros((16, width), bf16), small_here, (0, share * lax.axis_index("tok"))
    )
    extra = jnp.concatenate([extra[:9], condition_low, extra[10:]])
    arrived = exchange(
        jnp.concatenate(
            [kept_tokens.astype(bf16), jnp.broadcast_to(extra, (tok_count, 16, width))], axis=1
        )
    )
    condition_group = arrived[:, slots_here + 9]
    small = jnp.sum(arrived[:, slots_here:].astype(f32), axis=0)

    def modulate_all(conditions, weight):
        modulation_part = jnp.dot(
            conditions, weight, preferred_element_type=f32
        ) + modulation_bias.astype(bf16).astype(f32)
        return exchange(modulation_part).reshape(6, width)

    condition_all = gather_grp(condition_group)

    ringed = share % 16 == 0 and lax.axis_size("grp") == 4
    table_rows = position_rows // 2

    input_low = input_weight.astype(bf16)
    input_blocks = [input_low[:, number * width : (number + 1) * width] for number in range(3)]
    position_low = position_table.astype(bf16)
    attention_pairs = input_blocks[:2], [input_blocks[2], output_weight.astype(bf16)]
    attention_low = tuple(
        jnp.concatenate([pair[0], position_low[half * table_rows : (half + 1) * table_rows], pair[1]])
        for half, pair in enumerate(attention_pairs)
    )
    attention_cut, feed_cut = (7 * share // 9, 8 * share // 9), (4 * share // 3, 4 * share // 3)
    if ringed:
        mine, other = by_core(*attention_low), by_core(*attention_low[::-1])
        gather = Gather(ring, mine, other, *attention_cut)
        flight, up_weight, down_weight, modulation_weight = sync(
            gather.issue(), up_weight, down_weight, modulation_weight
        )
        gather.land(flight)
        (flight,) = sync(gather.issue())
        gather.land(flight)
    modulation_low = modulation_weight.astype(bf16)
    up_low = spread_call(up_weight, tok_count)
    down_low = down_weight.astype(bf16).reshape(4, share, width)
    feed_low = tuple(
        jnp.concatenate([up_low[half : half + 2], down_low[half : half + 2]]).reshape(-1, width)
        for half in (0, 2)
    )
    if ringed:
        mine, other = by_core(*feed_low), by_core(*feed_low[::-1])
        flight, condition_group, arrived, small, mine, other, modulation_low = sync(
            gather.issue(), condition_group, arrived, small, mine, other, modulation_low
        )
        gather.land(flight)
        feed_gather = Gather(ring, mine, other, *feed_cut)
        flight, condition_group = sync(gather.issue(), condition_group)
        gather.land(flight)
    mod = modulate_all(condition_group, modulation_low)
    if ringed:
        table_mine = gather.rows(share, table_rows)
        feed_flight = feed_gather.issue()
        flight, table_mine, table_other, mod = sync(
            gather.issue(), table_mine, swap_core(table_mine), mod
        )
        gather.land(flight)
        flight = gather.issue()
        distances = [0]
        for distance in range(1, ring.size // 2):
            distances += [-distance, distance]
        places = ring.tok_at(jnp.array(distances + [ring.size // 2], jnp.int32))
    else:
        places = jnp.arange(8, dtype=jnp.int32)
        mine = gather_plain(jnp.concatenate(by_core_pair(attention_pairs)), share)
        everywhere = list(range(8))
        plain_chunks = lambda mine: Chunks(
            [(mine, "all", everywhere)], [(swap_core(mine), "all", everywhere)]
        )
        attention_chunks = plain_chunks(mine)
        feed_chunks = plain_chunks(gather_plain(by_core(*feed_low), share))
        table = lax.all_gather(position_low, "tok").reshape(8, -1, width)

        halves = jnp.split(table, 2, axis=1)
        table_mine, table_other = by_core(*halves), by_core(*halves[::-1])
    table_chunks = Chunks(
        [(table_mine, "all", list(range(8)))], [(table_other, "all", list(range(8)))]
    )
    start, norm_one = start_call(
        core_row, places, kept_count, kept_index, arrived, small, mod, table_chunks, 0,
        table_mine.shape[1], seq_len,
    )
    if ringed:
        flight, feed_flight, start, norm_one = sync(flight, feed_flight, start, norm_one)
        gather.land(flight)
        attention_chunks = gather.chunks(share + table_rows)
        feed_gather.land(feed_flight)
    projected = project_call(core_row, places, norm_one, small, attention_chunks)
    if ringed:
        flight, projected, start = sync(feed_gather.issue(), projected, start)
        feed_gather.land(flight)
    attended = None
    for first, heads in forward_groups:
        attended = attend_call(projected, first, heads, attended)
        if ringed:
            flight, attended, projected = sync(feed_gather.issue(), attended, projected)
            feed_gather.land(flight)
    joined, branch_one, middle, norm_two = mix_call(
        core_row, places, attended[0], start, small, mod, attention_chunks
    )
    if ringed:
        flight, norm_two = sync(feed_gather.issue(), norm_two)
        feed_gather.land(flight)
        (flight,) = sync(feed_gather.issue())
        feed_gather.land(flight)
        feed_chunks = feed_gather.chunks()
    (
        block_output,
        hidden,
        pre_grad,
        grad_two,
        middle_grad,
        grad_one,
        feed_sums,
        up_bias_sum,
    ) = feed_call(
        core_row, places, norm_two, middle, cotangent[0], branch_one, mod, small, feed_chunks
    )
    far, near = 2 - 2 * core_row[:1], 2 * core_row[:1]
    other_up = feed_weight_call(far, norm_two, pre_grad)
    other_up, hidden, grad_one = sync(other_up, hidden, grad_one)
    other_down = feed_weight_call(far, hidden, grad_two)
    got_up, other_down, norm_two = sync(swap_core(other_up), other_down, norm_two)
    feed_chip = feed_weight_call(near, norm_two, pre_grad, got_up, rows=4)
    got_down, feed_chip, hidden = sync(swap_core(other_down), feed_chip, hidden)
    feed_chip = feed_weight_call(near, hidden, grad_two, got_down, feed_chip, 2, 4)
    feed_chip, grad_one = sync(feed_chip, grad_one)
    mix_grad = mix_grad_call(core_row, places, grad_one, attention_chunks)
    if ringed:
        feed_scatter = Scatter(ring, feed_chip)
    grads = []
    for group, (first, heads) in enumerate(back_groups):
        grads.append(attend_back_call(projected, attended, mix_grad, first, heads))
        if ringed and group < 2:
            flight, grads, mix_grad = sync(feed_scatter.hop(), grads, mix_grad)
            feed_scatter.land(flight)
    grads = [triple[block] for block in range(3) for triple in grads]

    def attention_weights(owner, norm):
        return attention_weight_call(owner, norm, joined, grad_one, grads)

    def start_back(quarter, earlier, grads):
        return start_back_call(
            quarter, earlier, core_row, places, kept_count, kept_index, grads, middle_grad, start, mod,
            attention_chunks,
        )

    attention_other = attention_weights(1 - core_row[:1], norm_one)
    if ringed:
        flight, attention_other, norm_one, grads = sync(
            feed_scatter.hop(), attention_other, norm_one, grads
        )
        feed_scatter.land(flight)
        feed_flight = feed_scatter.hop()
    attention_mine = attention_weights(core_row[:1], norm_one)
    attention_got = swap_core(attention_other)
    if ringed:
        attention_mine, attention_got, grads = sync(attention_mine, attention_got, grads)
        scatter = Scatter(ring, attention_mine, attention_got)
    quarters = []
    slot_grad = None
    for quarter in range(4):
        part = start_back(quarter, slot_grad, grads)
        if ringed:
            if quarter in (0, 3):
                flight, part, grads, feed_flight = sync(scatter.hop(), part, grads, feed_flight)
            else:
                flight, part, grads = sync(scatter.hop(), part, grads)
            scatter.land(flight)
            if quarter == 0:
                feed_scatter.land(feed_flight)
                feed_shard = feed_scatter.total()
                feed_flight = feed_cross = swap_x(feed_shard)
            else:
                feed_cross = feed_flight
        quarters.append(part)
        slot_grad = part[1]
    row_grad = jnp.concatenate([part[0] for part in quarters])
    slot_grad, small_grad = collect_call(
        feed_sums, up_bias_sum, slot_grad, *[part[2] for part in quarters]
    )

    position_grad = row_grad.reshape(tok_count, position_rows, width)
    halves = [
        half.reshape(-1, width)
        for half in (position_grad[:, :table_rows], position_grad[:, table_rows:])
    ]
    table_got = swap_core(jnp.concatenate([by_core(halves[1], halves[0]), small_grad]))
    arrived = exchange(slot_grad)
    table_chip = add_low(jnp.concatenate([by_core(halves[0], halves[1]), small_grad]), table_got)
    small_chip = table_chip[-16:]
    table_chip = table_chip[:-16].reshape(tok_count, table_rows, width)
    half_rows = table_rows // 2
    table_near, table_away = (
        jnp.concatenate(
            [
                lax.dynamic_slice_in_dim(table_chip, half_rows * place, half_rows, 1).reshape(-1, width),
                small_chip,
            ]
        )
        for place in (ring.x_bit, 1 - ring.x_bit)
    )
    table_got = swap_x(table_away)
    if ringed:
        attention_shard = scatter.total()
        attention_cross = swap_x(attention_shard)
    table_pair = add_low(table_near, table_got)
    table_pair, small_grad, arrived = sync(table_pair[:-16], table_pair[-16:], arrived)
    kept_low = arrived[:, :slots_here]
    modulation_grad_group = arrived[:, slots_here, : modulation_bias.shape[0]]
    condition_part = jnp.einsum(
        "ie,de->id", modulation_grad_group, modulation_low, preferred_element_type=f32
    )
    condition_high = condition_part.astype(bf16)
    condition_rest = (condition_part - condition_high.astype(f32)).astype(bf16)
    table_parts = exchange(
        jnp.concatenate(
            [
                table_pair.reshape(tok_count, half_rows, width),
                jnp.broadcast_to(small_grad[:14], (tok_count, 14, width)),
                condition_high[:, None],
                condition_rest[:, None],
            ],
            axis=1,
        )
    )
    modulation_grad_all = gather_grp(modulation_grad_group)
    modulation_total = jnp.einsum(
        "id,ie->de", condition_all, modulation_grad_all, preferred_element_type=f32
    )
    modulation_bias_total = jnp.sum(modulation_grad_all.astype(f32), axis=0)
    table_sum = jnp.sum(table_parts.astype(f32), axis=0)
    table_shard = table_sum.astype(bf16)
    condition_low_grad = table_sum[-2:-1] + table_sum[-1:]
    step = 4
    while step < lax.axis_size("grp"):
        table_shard = add_low(
            table_shard, lax.ppermute(table_shard, "grp", swap_pairs(lax.axis_size("grp"), step))
        )
        step *= 2
    table_cross = swap_x(table_shard[:half_rows])
    table_half = jnp.concatenate(
        [
            jnp.where(ring.x_bit == 0, table_shard[:half_rows], table_cross),
            jnp.where(ring.x_bit == 0, table_cross, table_shard[:half_rows]),
        ]
    )
    if ringed:
        attention_shard = add_low(attention_shard, attention_cross)
        feed_shard = add_low(feed_shard, feed_cross)
    else:
        attention_chip = by_tok(add_low(attention_mine, attention_got), share)
        attention_shard = add_x(scatter_plain(attention_chip))
        feed_shard = add_x(scatter_plain(by_tok(feed_chip, share)))
    table_far = swap_core(table_half)
    position_total = jnp.concatenate(
        [by_core(table_half, table_far), by_core(table_far, table_half)]
    ).astype(f32)
    small_total = lax.dynamic_slice_in_dim(
        table_shard[half_rows:], share * lax.axis_index("tok"), share, 1
    ).astype(f32)
    mask_total, query_bias_total, value_bias_total, output_bias_total, down_bias_total = (
        small_total[number] for number in range(5)
    )
    up_bias_total = small_total[5:9].reshape(-1)
    kept_grad = kept_low.astype(f32)
    far = swap_core(attention_shard)
    first, second = by_core(attention_shard, far).astype(f32), by_core(far, attention_shard).astype(f32)
    input_total = jnp.concatenate([first[:share], first[share:], second[:share]], axis=1)
    output_total = second[share:]
    feed_shard = feed_shard.reshape(4, share, width)
    feed_far = swap_core(feed_shard)
    up_total = unspread_call(core_row, feed_shard[:2], feed_far[:2], tok_count)
    down_total = jnp.concatenate(
        [by_core(feed_shard[2:], feed_far[2:]), by_core(feed_far[2:], feed_shard[2:])]
    ).reshape(-1, width).astype(f32)

    _, silu_back = jax.vjp(jax.nn.silu, condition)
    condition_grad = silu_back(condition_low_grad)[0]
    return (
        block_output[None],
        kept_grad,
        condition_grad,
        mask_total,
        position_total,
        modulation_total,
        modulation_bias_total,
        input_total,
        query_bias_total,
        value_bias_total,
        output_total,
        output_bias_total,
        up_total,
        up_bias_total,
        down_total,
        down_bias_total,
    )


def solution(mesh):
    return jax.shard_map(
        on_device,
        mesh=mesh,
        in_specs=(
            P("grp", "tok", None),
            P(("grp", "tok"), None),
            P(("grp", "tok")),
            P(("grp", "tok"), None),
            P("tok"),
            P("tok", None),
            P(None, "tok"),
            P("tok"),
            P("tok", None),
            P("tok"),
            P("tok"),
            P("tok", None),
            P("tok"),
            P("tok", None),
            P("tok"),
            P("tok", None),
            P("tok"),
            P(("grp", "tok"), None, None),
        ),
        out_specs=(
            P(("grp", "tok"), None, None),
            P("grp", "tok", None),
            P(("grp", "tok"), None),
            P("tok"),
            P("tok", None),
            P(None, "tok"),
            P("tok"),
            P("tok", None),
            P("tok"),
            P("tok"),
            P("tok", None),
            P("tok"),
            P("tok", None),
            P("tok"),
            P("tok", None),
            P("tok"),
        ),
        check_vma=False,
    )
```

```python
import functools
import math

import jax
import jax.numpy as jnp
from jax import lax
from jax.experimental import pallas as pl
from jax.experimental.pallas import tpu as pltpu
from jax.sharding import PartitionSpec as P

H = 16
HD = 72
LANES = 128

epsilon = 1e-06
f32 = jnp.float32
bf16 = jnp.bfloat16
plain = (((1,), (0,)), ((), ()))
right_turned = (((1,), (1,)), ((), ()))
left_turned = (((0,), (0,)), ((), ()))
vmem_limit = 60 << 20


def product(left, right, dims=plain):
    return lax.dot_general(left, right, dims, preferred_element_type=f32)


def whole_block(array):
    zeros = (0,) * array.ndim
    return pl.BlockSpec(array.shape, lambda *_: zeros)


def row_block(rows, *rest):
    return pl.BlockSpec((rows,) + rest, lambda i: (i,) + (0,) * len(rest))


smem = pl.BlockSpec(memory_space=pltpu.SMEM)
anywhere = pl.BlockSpec(memory_space=pl.ANY)


def params():
    return pltpu.CompilerParams(vmem_limit_bytes=vmem_limit)


def cost(flops, moved, exps=0):
    return pl.CostEstimate(flops=int(flops), bytes_accessed=int(moved), transcendentals=int(exps))


def column_sum(values):
    return jnp.sum(values, axis=0, keepdims=True)


def normalize(values):
    center = values - jnp.mean(values, axis=-1, keepdims=True)
    spread = jnp.mean(center * center, axis=-1, keepdims=True)
    inverse = lax.rsqrt(spread + epsilon)
    return center * inverse, inverse


def normalize_back(grad, unit, inverse, scale):
    scaled = grad * (1.0 + scale)
    first = jnp.mean(scaled, axis=-1, keepdims=True)
    second = jnp.mean(scaled * unit, axis=-1, keepdims=True)
    return (scaled - first - unit * second) * inverse


def start_kernel(core_ref, places_ref, count_ref, index_ref, kept_ref, small_ref, mod_ref, *rest, chunks, row, share):
    refs, (start_ref, norm_ref, table, sems) = rest[: len(chunks.arrays)], rest[len(chunks.arrays) :]
    rows, slots = start_ref.shape[0], index_ref.shape[1]
    step = pl.program_id(0)
    low, high = table.at[:, :share], table.at[:, share:]

    @pl.when(step == 0)
    def _():
        @pl.when(core_ref[0] == 0)
        def _():
            chunks.load(refs, places_ref, core_ref, True, row, low, sems.at[0])
            chunks.load(refs, places_ref, core_ref, False, row, high, sems.at[1])

        @pl.when(core_ref[0] != 0)
        def _():
            chunks.load(refs, places_ref, core_ref, False, row, low, sems.at[0])
            chunks.load(refs, places_ref, core_ref, True, row, high, sems.at[1])

        wait_block(low, sems.at[0])
        wait_block(high, sems.at[1])

    base = step * rows
    here = lax.broadcasted_iota(jnp.int32, (rows, slots), 0) + base
    slot = lax.broadcasted_iota(jnp.int32, (rows, slots), 1)
    chosen = jnp.where((index_ref[...] == here) & (slot < count_ref[0]), 1.0, 0.0)
    kept = kept_ref[:, : slots // kept_ref.shape[0]].reshape(slots, -1)
    filled = product(chosen.astype(bf16), kept)
    empty = 1.0 - jnp.sum(chosen, axis=1, keepdims=True)
    groups_here = rows // table.shape[1]
    position = table[pl.ds(step * groups_here, groups_here)].reshape(rows, -1)
    start = filled + empty * small_ref[0:1] + position.astype(f32)
    start_ref[...] = start
    unit, _ = normalize(start)
    norm_ref[...] = (unit * (1.0 + mod_ref[1:2]) + mod_ref[0:1]).astype(bf16)


def start_call(core, places, count, index, kept, small, mod, chunks, row, share, seq_len):
    width = kept.shape[2]
    rows = seq_len // 4
    return pl.pallas_call(
        functools.partial(start_kernel, chunks=chunks, row=row, share=share),
        grid=(4,),
        in_specs=[
            smem,
            smem,
            smem,
            whole_block(index),
            whole_block(kept),
            whole_block(small),
            whole_block(mod),
        ]
        + chunks.specs,
        out_specs=[row_block(rows, width)] * 2,
        out_shape=[
            jax.ShapeDtypeStruct((seq_len, width), f32),
            jax.ShapeDtypeStruct((seq_len, width), bf16),
        ],
        scratch_shapes=[
            pltpu.VMEM((8, seq_len // 8, width), bf16),
            pltpu.SemaphoreType.DMA((2,)),
        ],
        compiler_params=params(),
        cost_estimate=cost(2 * seq_len * width * index.shape[1], 14 * seq_len * width),
    )(core, places, count, index, kept, small, mod, *chunks.arrays)


class Chunks:
    def __init__(self, mine, other, part=0, middle=0, stride=0):
        self.sources = list(mine), list(other)
        self.part, self.middle, self.stride = part, middle, stride
        self.arrays = [entry[0] for source in self.sources for entry in source]
        self.specs = [anywhere] * len(self.arrays)

    def span(self, kind, bit):
        part, middle = self.part, self.middle
        start = part * bit
        return {
            "piece": (start, start + part + middle),
            "first": (start, start + middle),
            "second": (start + middle, start + part + middle),
            "got": ((0, part) if bit else (part + middle, 2 * part + middle)),
            "all": (0, 1 << 20),
        }[kind]

    def spans(self, kind, bit):
        if kind == "pair":
            return [self.span("piece", bit) + (0,), self.span("got", bit) + (self.part + self.middle,)]
        return [self.span(kind, bit) + (0,)]

    def load(self, refs, places_ref, spot_ref, from_mine, row, target, sem):
        source = self.sources[0 if from_mine else 1]
        refs = refs[: len(source)] if from_mine else refs[len(self.sources[0]) :]

        def start(ref, kind, places, bit):
            for low, high, base in self.spans(kind, bit):
                begin, end = max(row, low), min(row + target.shape[1], high)
                for index, place in enumerate(places if begin < end else []):
                    pltpu.make_async_copy(
                        ref.at[index, pl.ds(base + begin - low, end - begin)],
                        target.at[places_ref[place], pl.ds(begin - row, end - begin)],
                        sem,
                    ).start()

        for ref, (_, kind, places) in zip(refs, source):
            if kind == "all":
                start(ref, kind, places, 0)
        if any(kind != "all" for _, kind, _ in source):
            for bit in (0, 1):

                @pl.when(spot_ref[1] == bit)
                def _():
                    for ref, (_, kind, places) in zip(refs, source):
                        if kind != "all":
                            start(ref, kind, places, bit)

    def load_block(self, refs, places_ref, spot_ref, block, target, sem, first=0):
        rows = target.shape[1]
        owner, row = block // 2, first * rows + (block % 2) * (self.stride or rows)

        @pl.when(spot_ref[0] == owner)
        def _():
            self.load(refs, places_ref, spot_ref, True, row, target, sem)

        @pl.when(spot_ref[0] != owner)
        def _():
            self.load(refs, places_ref, spot_ref, False, row, target, sem)


def wait_block(target, sem):
    pltpu.make_async_copy(target, target, sem).wait()


def square(weight):
    return weight.reshape(-1, weight.shape[-1])


def split_heads(values, store):
    rows = values.shape[0]
    blank = jnp.zeros((rows, LANES - HD), values.dtype)
    for head in range(H):
        store(head, jnp.concatenate([values[:, head * HD : (head + 1) * HD], blank], axis=1))


def project_kernel(core_ref, places_ref, norm_ref, small_ref, *rest, chunks):
    refs, (out_ref, weight, sems) = rest[: len(chunks.arrays)], rest[len(chunks.arrays) :]
    step, part = pl.program_id(0), pl.program_id(1)

    @pl.when((step == 0) & (part == 0))
    def _():
        for block in range(3):
            chunks.load_block(refs, places_ref, core_ref, block, weight.at[block], sems.at[block])

    @pl.when(part == 0)
    def _():
        wait_block(weight.at[step], sems.at[step])

    key_free = jnp.where(step == 1, 0.0, 1.0)
    bias = jnp.where(step == 0, small_ref[1:2], small_ref[2:3]) * key_free
    result = product(norm_ref[...], square(weight[step])) + bias

    def store(head, value):
        out_ref[0, head] = value

    split_heads(result.astype(bf16), store)


def project_call(core, places, norm, small, chunks):
    seq_len, width = norm.shape
    return pl.pallas_call(
        functools.partial(project_kernel, chunks=chunks),
        grid=(3, 2),
        in_specs=[
            smem,
            smem,
            pl.BlockSpec((seq_len // 2, width), lambda i, j: (j, 0)),
            whole_block(small),
        ]
        + chunks.specs,
        out_specs=pl.BlockSpec((1, H, seq_len // 2, LANES), lambda i, j: (i, 0, j, 0)),
        out_shape=jax.ShapeDtypeStruct((3, H, seq_len, LANES), bf16),
        scratch_shapes=[
            pltpu.VMEM((3, 8, width // 8, width), bf16),
            pltpu.SemaphoreType.DMA((3,)),
        ],
        compiler_params=params(),
        cost_estimate=cost(6 * seq_len * width * width, 12 * seq_len * width + 6 * width * width),
    )(core, places, norm, small, *chunks.arrays)


heads_a_step = 2
forward_groups = ((0, 8), (8, 8))
back_groups = ((0, 4), (4, 8), (12, 4))
groups = len(back_groups)


def attend_kernel(query_ref, key_ref, value_ref, *rest, factor):
    mix_ref, log_ref = rest[-2:]
    for head in range(query_ref.shape[1]):
        scores = product(key_ref[0, head], query_ref[0, head], right_turned)
        top = jnp.max(scores, axis=0, keepdims=True)
        weights = jnp.exp2((scores - top) * factor)
        total = jnp.sum(weights, axis=0, keepdims=True)
        mix = product(value_ref[0, head].T, weights.astype(bf16))
        mix_ref[head] = (mix / total).T.astype(bf16)
        log_ref[head] = top * factor + jnp.log2(total)


def head_block(place, seq_len, first):
    first = first // heads_a_step
    return pl.BlockSpec((1, heads_a_step, seq_len, LANES), lambda h: (place, first + h, 0, 0))


def head_rows(first, *rest):
    first = first // heads_a_step
    return pl.BlockSpec((heads_a_step,) + rest, lambda h: (first + h, 0, 0))


def attend_call(projected, first, heads, earlier=None):
    seq_len = projected.shape[2]
    kept = [] if earlier is None else list(earlier)
    return pl.pallas_call(
        functools.partial(
            attend_kernel, factor=math.log2(math.e) / math.sqrt(HD)
        ),
        grid=(heads // heads_a_step,),
        in_specs=[head_block(place, seq_len, first) for place in range(3)] + [anywhere] * len(kept),
        out_specs=[
            head_rows(first, seq_len, LANES),
            head_rows(first, 1, seq_len),
        ],
        out_shape=[
            jax.ShapeDtypeStruct((H, seq_len, LANES), bf16),
            jax.ShapeDtypeStruct((H, 1, seq_len), f32),
        ],
        input_output_aliases={3: 0, 4: 1} if kept else {},
        compiler_params=params(),
        cost_estimate=cost(4 * heads * seq_len * seq_len * 256, 8 * heads * seq_len * LANES, heads * seq_len * seq_len),
    )(projected, projected, projected, *kept)


def attend_back_kernel(
    query_ref, key_ref, value_ref, mix_ref, log_ref, grad_ref, query_grad_ref, key_grad_ref,
    value_grad_ref, *, factor
):
    base_two = factor * math.log2(math.e)
    for head in range(query_ref.shape[1]):
        query, key, value = query_ref[0, head], key_ref[0, head], value_ref[0, head]
        grad = grad_ref[head]
        scores = product(key, query, right_turned)
        weights = jnp.exp2(scores * base_two - log_ref[head])
        value_grad_ref[head] = product(weights.astype(bf16), grad).astype(bf16)
        weight_grad = product(value, grad, right_turned)
        inner = column_sum((grad.astype(f32) * mix_ref[head].astype(f32)).T)
        score_grad = (weights * (weight_grad - inner)).astype(bf16)
        key_grad_ref[head] = (product(score_grad, query) * factor).astype(bf16)
        query_grad_ref[head] = (product(key.T, score_grad) * factor).T.astype(bf16)


def attend_back_call(projected, attended, grad, first, heads):
    seq_len = projected.shape[2]
    mix, logs = attended
    flat = head_rows(0, seq_len, LANES)
    return pl.pallas_call(
        functools.partial(attend_back_kernel, factor=1.0 / math.sqrt(HD)),
        grid=(heads // heads_a_step,),
        in_specs=[head_block(place, seq_len, first) for place in range(3)]
        + [
            head_rows(first, seq_len, LANES),
            head_rows(first, 1, seq_len),
            head_rows(first, seq_len, LANES),
        ],
        out_specs=[flat] * 3,
        out_shape=[jax.ShapeDtypeStruct((heads, seq_len, LANES), bf16)] * 3,
        compiler_params=params(),
        cost_estimate=cost(10 * heads * seq_len * seq_len * 256, 16 * heads * seq_len * LANES, heads * seq_len * seq_len),
    )(projected, projected, projected, mix, logs, grad)


def join_heads(refs):
    return jnp.concatenate(
        [ref[head][:, :HD] for ref in refs for head in range(ref.shape[0])], axis=1
    )


def mix_kernel(core_ref, places_ref, start_ref, small_ref, mod_ref, *rest, chunks):
    mix_refs, rest = rest[:1], rest[1:]
    refs, rest = rest[: len(chunks.arrays)], rest[len(chunks.arrays) :]
    joined_ref, branch_ref, middle_ref, norm_ref, weight, sem = rest

    @pl.when(pl.program_id(0) == 0)
    def _():
        chunks.load_block(refs, places_ref, core_ref, 3, weight, sem)
        wait_block(weight, sem)

    joined = join_heads(mix_refs)
    joined_ref[...] = joined
    branch = product(joined, square(weight[...])) + small_ref[3:4]
    branch_ref[...] = branch.astype(bf16)
    middle = start_ref[...] + mod_ref[2:3] * branch
    middle_ref[...] = middle
    unit, _ = normalize(middle)
    norm_ref[...] = (unit * (1.0 + mod_ref[4:5]) + mod_ref[3:4]).astype(bf16)


def mix_call(core, places, mix, start, small, mod, chunks):
    seq_len, width = start.shape
    rows = seq_len // 4
    block = row_block(rows, width)
    return pl.pallas_call(
        functools.partial(mix_kernel, chunks=chunks),
        grid=(4,),
        in_specs=[smem, smem, block, whole_block(small), whole_block(mod)]
        + [pl.BlockSpec((H, rows, LANES), lambda i: (0, i, 0))]
        + chunks.specs,
        out_specs=[block] * 4,
        out_shape=[
            jax.ShapeDtypeStruct((seq_len, width), kind) for kind in (bf16, bf16, f32, bf16)
        ],
        scratch_shapes=[pltpu.VMEM((8, width // 8, width), bf16), pltpu.SemaphoreType.DMA],
        compiler_params=params(),
        cost_estimate=cost(2 * seq_len * width * width, 18 * seq_len * width),
    )(core, places, start, small, mod, mix, *chunks.arrays)


def gelu_parts(values):
    inner = 0.7978845608028654 * (values + 0.044715 * values * values * values)
    turned = jnp.tanh(inner)
    half = 0.5 * (1.0 + turned)
    slope = half + 0.5 * values * (1.0 - turned * turned) * (
        0.7978845608028654 * (1.0 + 0.134145 * values * values)
    )
    return values * half, slope


def feed_kernel(
    core_ref, places_ref, norm_ref, middle_ref, cot_ref, branch_ref, mod_ref, small_ref, *rest, source
):
    refs, rest = rest[: len(source.arrays)], rest[len(source.arrays) :]
    (
        out_ref, hidden_ref, pre_ref, grad_two_ref, middle_grad_ref, grad_one_ref, sums_ref,
        up_sums_ref, up, down, slopes, sems,
    ) = rest
    step = pl.program_id(0)
    chunks = 4

    @pl.when(step == 0)
    def _():
        for chunk in range(chunks):
            for side, target in enumerate((up, down)):
                source.load_block(
                    refs, places_ref, core_ref, chunk, target.at[chunk], sems.at[side, chunk], 2 * side
                )
        sums_ref[...] = jnp.zeros_like(sums_ref)
        up_sums_ref[...] = jnp.zeros_like(up_sums_ref)

    norm = norm_ref[...]
    total = None
    for chunk in range(chunks):

        @pl.when(step == 0)
        def _():
            wait_block(up.at[chunk], sems.at[0, chunk])
            wait_block(down.at[chunk], sems.at[1, chunk])

        before = product(norm, square(up[chunk])) + small_ref[5 + chunk : 6 + chunk]
        hidden, slope = gelu_parts(before)
        hidden = hidden.astype(bf16)
        hidden_ref[chunk] = hidden
        slopes[chunk] = slope.astype(slopes.dtype)
        part = product(hidden, square(down[chunk]))
        total = part if total is None else total + part
    branch_two = total + small_ref[4:5]
    middle, cot = middle_ref[...], cot_ref[...]
    gate_two = mod_ref[5:6]
    out_ref[...] = middle + gate_two * branch_two
    grad_two = (gate_two * cot).astype(bf16)
    grad_two_ref[...] = grad_two
    sums_ref[0:1] += column_sum(cot * branch_two)
    sums_ref[1:2] += column_sum(grad_two.astype(f32))
    total = None
    for chunk in range(chunks):
        pre = (product(grad_two, square(down[chunk]), right_turned) * slopes[chunk].astype(f32)).astype(bf16)
        pre_ref[chunk] = pre
        up_sums_ref[chunk] += column_sum(pre.astype(f32))
        part = product(pre, square(up[chunk]), right_turned)
        total = part if total is None else total + part
    unit, inverse = normalize(middle)
    sums_ref[2:3] += column_sum(total * unit)
    sums_ref[3:4] += column_sum(total)
    middle_grad = cot + normalize_back(total, unit, inverse, mod_ref[4:5])
    middle_grad_ref[...] = middle_grad
    sums_ref[4:5] += column_sum(middle_grad * branch_ref[...].astype(f32))
    grad_one = (mod_ref[2:3] * middle_grad).astype(bf16)
    grad_one_ref[...] = grad_one
    sums_ref[5:6] += column_sum(grad_one.astype(f32))


def feed_call(core, places, norm, middle, cot, branch, mod, small, source):
    seq_len, width = middle.shape
    steps = 4
    rows = seq_len // steps
    block = row_block(rows, width)
    chunked = pl.BlockSpec((4, rows, width), lambda i: (0, i, 0))
    wide = jax.ShapeDtypeStruct((4, seq_len, width), bf16)
    return pl.pallas_call(
        functools.partial(feed_kernel, source=source),
        grid=(steps,),
        in_specs=[
            smem,
            smem,
            block,
            block,
            block,
            block,
            whole_block(mod),
            whole_block(small),
        ]
        + source.specs,
        out_specs=[
            block,
            chunked,
            chunked,
            block,
            block,
            block,
            pl.BlockSpec((8, width), lambda i: (0, 0)),
            pl.BlockSpec((4, 1, width), lambda i: (0, 0, 0)),
        ],
        out_shape=[
            jax.ShapeDtypeStruct((seq_len, width), f32),
            wide,
            wide,
            jax.ShapeDtypeStruct((seq_len, width), bf16),
            jax.ShapeDtypeStruct((seq_len, width), f32),
            jax.ShapeDtypeStruct((seq_len, width), bf16),
            jax.ShapeDtypeStruct((8, width), f32),
            jax.ShapeDtypeStruct((4, 1, width), f32),
        ],
        scratch_shapes=[
            pltpu.VMEM((4, 8, width // 8, width), bf16),
            pltpu.VMEM((4, 8, width // 8, width), bf16),
            pltpu.VMEM((4, rows, width), f32),
            pltpu.SemaphoreType.DMA((2, 4)),
        ],
        compiler_params=params(),
        cost_estimate=cost(32 * seq_len * width * width, 60 * seq_len * width, 4 * seq_len * width),
    )(core, places, norm, middle, cot, branch, mod, small, *source.arrays)


def feed_weight_kernel(first_ref, left_ref, right_ref, *rest):
    out_ref = rest[-1]
    left = left_ref[0] if left_ref.ndim == 3 else left_ref[...]
    right = right_ref[0] if right_ref.ndim == 3 else right_ref[...]
    result = product(left, right, left_turned).reshape(out_ref.shape)
    if len(rest) > 1:
        result = result + rest[0][...].astype(f32)
    out_ref[...] = result.astype(bf16)


def feed_weight_call(first, left, right, got=None, base=None, row=0, rows=2):
    width = left.shape[-1]
    seq_len = left.shape[-2]
    out_block = (8, width // 8, width)

    def spec(array):
        if array.ndim == 2:
            return pl.BlockSpec(array.shape, lambda i, f: (0, 0))
        return pl.BlockSpec((1, seq_len, width), lambda i, f: (f[0] + i, 0, 0))

    more, specs, aliases = [], [], {}
    if got is not None:
        more, specs = [got], [pl.BlockSpec(out_block, lambda i, f: (0, i, 0))]
    if base is not None:
        aliases = {3 + len(more): 0}
        more, specs = more + [base], specs + [anywhere]
    return pl.pallas_call(
        feed_weight_kernel,
        grid_spec=pltpu.PrefetchScalarGridSpec(
            num_scalar_prefetch=1,
            grid=(2,),
            in_specs=[spec(left), spec(right)] + specs,
            out_specs=pl.BlockSpec(out_block, lambda i, f: (0, row + i, 0)),
        ),
        out_shape=jax.ShapeDtypeStruct((8, rows * width // 8, width), bf16),
        input_output_aliases=aliases,
        compiler_params=params(),
        cost_estimate=cost(4 * seq_len * width * width, 8 * seq_len * width + 4 * width * width),
    )(first, left, right, *more)


def attention_weight_kernel(owner_ref, norm_ref, joined_ref, grad_ref, *rest):
    head_refs = [rest[block * groups : (block + 1) * groups] for block in range(3)]
    out_ref, left, heads, right, sems = rest[3 * groups :]
    step = pl.program_id(0)

    def copies(block, slot):
        if block == 3:
            return [(joined_ref, left.at[slot]), (grad_ref, right.at[slot])]
        return [(norm_ref, left.at[slot])] + [
            (ref, heads.at[slot, pl.ds(first, count)])
            for (first, count), ref in zip(back_groups, head_refs[block])
        ]

    @pl.when(step == 0)
    def _():
        for block in range(4):

            @pl.when(owner_ref[0] == block // 2)
            def _():
                for source, target in copies(block, block % 2):
                    pltpu.make_async_copy(source, target, sems.at[block % 2]).start()

    for block in range(4):

        @pl.when((owner_ref[0] == block // 2) & (step == block % 2))
        def _():
            slot = block % 2
            wait_block(left.at[slot], sems.at[slot])
            if block == 3:
                wait_block(right.at[slot], sems.at[slot])
            else:
                wait_block(heads.at[slot], sems.at[slot])
                right[slot] = jnp.concatenate(
                    [heads[slot, head][:, :HD] for head in range(H)], axis=1
                )

    result = product(left[step], right[step], left_turned)
    out_ref[...] = result.astype(bf16).reshape(out_ref.shape)


def attention_weight_call(owner, norm, joined, grad_one, grads):
    seq_len, width = norm.shape
    return pl.pallas_call(
        attention_weight_kernel,
        grid=(2,),
        in_specs=[smem] + [anywhere] * (3 + 3 * groups),
        out_specs=pl.BlockSpec((8, width // 8, width), lambda i: (0, i, 0)),
        out_shape=jax.ShapeDtypeStruct((8, width // 4, width), bf16),
        scratch_shapes=[
            pltpu.VMEM((2, seq_len, width), bf16),
            pltpu.VMEM((2, H, seq_len, LANES), bf16),
            pltpu.VMEM((2, seq_len, width), bf16),
            pltpu.SemaphoreType.DMA((2,)),
        ],
        compiler_params=params(),
        cost_estimate=cost(4 * seq_len * width * width, 10 * seq_len * width + 4 * width * width),
    )(owner, norm, joined, grad_one, *grads)


def mix_grad_kernel(core_ref, places_ref, grad_ref, *rest, chunks):
    refs, (out_ref, weight, sem) = rest[: len(chunks.arrays)], rest[len(chunks.arrays) :]

    @pl.when(pl.program_id(0) == 0)
    def _():
        chunks.load_block(refs, places_ref, core_ref, 3, weight, sem)
        wait_block(weight, sem)

    def store(head, value):
        out_ref[head] = value

    split_heads(product(grad_ref[...], square(weight[...]), right_turned).astype(bf16), store)


def mix_grad_call(core, places, grad_one, chunks):
    seq_len, width = grad_one.shape
    rows = seq_len // 4
    return pl.pallas_call(
        functools.partial(mix_grad_kernel, chunks=chunks),
        grid=(4,),
        in_specs=[smem, smem, row_block(rows, width)] + chunks.specs,
        out_specs=pl.BlockSpec((H, rows, LANES), lambda i: (0, i, 0)),
        out_shape=jax.ShapeDtypeStruct((H, seq_len, LANES), bf16),
        scratch_shapes=[pltpu.VMEM((8, width // 8, width), bf16), pltpu.SemaphoreType.DMA],
        compiler_params=params(),
        cost_estimate=cost(2 * seq_len * width * width, 8 * seq_len * width),
    )(core, places, grad_one, *chunks.arrays)


def start_back_kernel(
    core_ref, places_ref, count_ref, index_row_ref, index_ref, middle_grad_ref, start_ref, mod_ref,
    *rest, chunks, first
):
    grad_refs = [rest[block * groups : (block + 1) * groups] for block in range(3)]
    rest = rest[3 * groups :]
    refs, rest = rest[: len(chunks.arrays)], rest[len(chunks.arrays) :]
    row_grad_ref, slot_ref, sums_ref, weight, sems = rest[-5:]
    earlier = rest[:-5]
    rows, width = start_ref.shape
    toks, per_tok = slot_ref.shape[0], index_ref.shape[0] // slot_ref.shape[0]
    slot_count = index_ref.shape[0]

    for block in range(3):
        chunks.load_block(refs, places_ref, core_ref, block, weight.at[block], sems.at[block])
    sums = {}
    total = None
    for block, refs in enumerate(grad_refs):
        joined = join_heads(refs)
        if block != 1:
            sums[block // 2] = column_sum(joined.astype(f32))
        wait_block(weight.at[block], sems.at[block])
        part = product(joined, square(weight[block]), right_turned)
        total = part if total is None else total + part
    unit, inverse = normalize(start_ref[...])
    sums[2] = column_sum(total * unit)
    sums[3] = column_sum(total)
    row_grad = middle_grad_ref[...] + normalize_back(total, unit, inverse, mod_ref[1:2])
    row_low = row_grad.astype(bf16)
    row_grad_ref[...] = row_low
    base = first * rows
    place = lax.broadcasted_iota(jnp.int32, (slot_count, rows), 1) + base
    slot = lax.broadcasted_iota(jnp.int32, (slot_count, rows), 0)
    chosen = jnp.where((index_ref[...] == place) & (slot < count_ref[0]), 1.0, 0.0)
    part = product(chosen.astype(bf16), row_low)

    part = part.astype(bf16).reshape(toks, per_tok, width)
    if earlier:
        part = part + earlier[0][:, :per_tok]
    slot_ref[:, :per_tok] = part
    here = lax.broadcasted_iota(jnp.int32, (rows, slot_count), 0) + base
    lane = lax.broadcasted_iota(jnp.int32, (rows, slot_count), 1)
    taken = jnp.where((index_row_ref[...] == here) & (lane < count_ref[0]), 1.0, 0.0)
    empty = 1.0 - jnp.sum(taken, axis=1, keepdims=True)
    sums[4] = column_sum(row_grad * empty)
    sums_ref[...] = jnp.concatenate(
        [sums[number] for number in range(5)] + [jnp.zeros((3, width), f32)]
    )


def start_back_call(quarter, earlier, core, places, count, index, grads, middle_grad, start, mod, chunks):
    seq_len, width = start.shape
    slot_count = index.shape[1]
    toks = lax.axis_size("tok")
    rows = seq_len // 4
    heads = [
        pl.BlockSpec((array.shape[0], rows, LANES), lambda i: (0, quarter, 0)) for array in grads
    ]
    block = pl.BlockSpec((rows, width), lambda i: (quarter, 0))
    kept = [] if earlier is None else [earlier]
    column = index.reshape(slot_count, 1)
    return pl.pallas_call(
        functools.partial(start_back_kernel, chunks=chunks, first=quarter),
        grid=(1,),
        in_specs=[
            smem,
            smem,
            smem,
            whole_block(index),
            whole_block(column),
            block,
            block,
            whole_block(mod),
        ]
        + heads
        + chunks.specs
        + [whole_block(array) for array in kept],
        out_specs=[
            row_block(rows, width),
            pl.BlockSpec((toks, slot_count // toks + 8, width), lambda i: (0, 0, 0)),
            pl.BlockSpec((8, width), lambda i: (0, 0)),
        ],
        out_shape=[
            jax.ShapeDtypeStruct((rows, width), bf16),
            jax.ShapeDtypeStruct((toks, slot_count // toks + 8, width), bf16),
            jax.ShapeDtypeStruct((8, width), f32),
        ],
        scratch_shapes=[
            pltpu.VMEM((3, 8, width // 8, width), bf16),
            pltpu.SemaphoreType.DMA((3,)),
        ],
        compiler_params=params(),
        cost_estimate=cost(2 * seq_len * width * width, 7 * seq_len * width),
    )(core, places, count, index, column, middle_grad, start, mod, *grads, *chunks.arrays, *kept)


def collect_kernel(feed_ref, up_ref, *rest):
    *start_refs, _, mod_ref, small_ref = rest
    start = start_refs[0][...]
    for ref in start_refs[1:]:
        start = start + ref[...]
    feed = feed_ref[...]
    row = lambda values, number: values[number : number + 1]
    blank = jnp.zeros((7, start.shape[1]), f32)
    width = start.shape[1]
    rows = [row(start, 3), row(start, 2), row(feed, 4), row(feed, 3), row(feed, 2), row(feed, 0)]
    share = 6 * width // mod_ref.shape[0]
    for tok in range(mod_ref.shape[0]):
        place, left, pieces = tok * share, share, []
        while left:
            within = place % width
            count = min(left, width - within)
            pieces.append(rows[place // width][:, within : within + count])
            place, left = place + count, left - count
        pieces.append(jnp.zeros((1, width - share), f32))
        line = jnp.concatenate(pieces, axis=1)
        mod_ref[tok] = jnp.broadcast_to(line, (8, width)).astype(bf16)
    small_ref[...] = jnp.concatenate(
        [row(start, 4), row(start, 0), row(start, 1), row(feed, 5), row(feed, 1)]
        + [up_ref[block] for block in range(4)]
        + [blank]
    ).astype(bf16)


def collect_call(feed, up, slots, *starts):
    toks, rows, width = slots.shape
    return pl.pallas_call(
        collect_kernel,
        grid=(1,),
        in_specs=[whole_block(feed), whole_block(up)]
        + [whole_block(start) for start in starts]
        + [anywhere],
        out_specs=[
            pl.BlockSpec((toks, 8, width), lambda i: (0, rows // 8 - 1, 0)),
            pl.BlockSpec((16, width), lambda i: (0, 0)),
        ],
        out_shape=[
            jax.ShapeDtypeStruct(slots.shape, bf16),
            jax.ShapeDtypeStruct((16, width), bf16),
        ],
        input_output_aliases={2 + len(starts): 0},
        compiler_params=params(),
    )(feed, up, *starts, slots)


def swap_pairs(size, bit):
    return [(place, place ^ bit) for place in range(size)]


def swap_core(values):
    return lax.ppermute(values, "grp", swap_pairs(lax.axis_size("grp"), 1))


def add_low(*parts):
    total = parts[0].astype(f32)
    for part in parts[1:]:
        total = total + part.astype(f32)
    return total.astype(bf16)


def swap_x(values):
    return lax.ppermute(values, "grp", swap_pairs(lax.axis_size("grp"), 2))


class Ring:
    def __init__(self):
        size = lax.axis_size("tok")
        self.size = size
        order = list(range(0, size, 2)) + list(range(1, size, 2))[::-1]
        self.ahead = [(order[i], order[(i + 1) % size]) for i in range(size)]
        self.behind = [(after, before) for before, after in self.ahead]
        tok = lax.axis_index("tok")
        self.place = jnp.where(tok % 2 == 0, tok // 2, size - 1 - tok // 2)
        self.x_bit = (lax.axis_index("grp") // 2) % 2

    def tok_at(self, distance):
        place = (self.place + distance) % self.size
        return jnp.where(place < self.size // 2, 2 * place, 2 * (self.size - 1 - place) + 1)

    def forward(self, values):
        return lax.ppermute(values, "tok", self.ahead)

    def backward(self, values):
        return lax.ppermute(values, "tok", self.behind)


def sync(*values):
    return lax.optimization_barrier(values)


class Gather:
    def __init__(self, ring, mine, other, part, middle):
        self.ring, self.part, self.middle = ring, part, middle
        self.mine, self.other = [(mine[None], "all", [0])], [(other[None], "all", [0])]
        payload = lax.dynamic_slice_in_dim(mine, part * ring.x_bit, part + middle, 0)
        self.pieces = [payload, payload]
        self.distance = 0
        self.own = None
        self.making, self.ready = [], []

    def issue(self):
        ring, flight = self.ring, {}
        middle, half = self.middle, ring.size // 2
        if self.distance == half:
            self.ready, self.making = self.ready + self.making, []
        flight["pair"] = [array for array, _ in self.making]
        self.made = [places for _, places in self.making]
        self.making = []
        flight["core"] = [swap_core(array) for array, _ in self.ready]
        self.sent = [places for _, places in self.ready]
        if self.distance < half:
            self.distance += 1
            ahead, behind = self.pieces
            if self.distance == half:
                ahead, behind = ahead[:middle], behind[middle:]
            flight["ring"] = [ring.forward(ahead), ring.backward(behind)]
        if self.own is not None:
            flight["x"] = swap_x(self.own)
        return flight

    def land(self, flight):
        bit, part, middle = self.ring.x_bit, self.part, self.middle
        self.other += [(array, "pair", places) for array, places in zip(flight["core"], self.sent)]
        self.ready = list(zip(flight["pair"], self.made))
        self.own = None
        if "x" in flight:
            got = flight["x"]
            self.mine.append((got, "got", self.places))
            if len(self.places) == 1:
                ahead, behind = self.pieces
                pair = jnp.concatenate([ahead, behind, got[0]])[None]
            else:
                pair = jnp.concatenate([jnp.stack(self.pieces), got], axis=1)
            self.making = [(pair, self.places)]
        if "ring" in flight:
            ahead, behind = self.pieces = flight["ring"]
            place = 2 * self.distance - 1
            if self.distance == self.ring.size // 2:
                self.places = [place]
                self.mine += [(ahead[None], "first", [place]), (behind[None], "second", [place])]
                self.own = jnp.where(bit == 0, ahead[:part], behind)[None]
            else:
                self.places = [place, place + 1]
                self.mine += [(ahead[None], "piece", [place]), (behind[None], "piece", [place + 1])]
                self.own = jnp.stack(
                    [
                        lax.dynamic_slice_in_dim(piece, middle * bit, part, 0)
                        for piece in self.pieces
                    ]
                )

    def chunks(self, stride=0):
        return Chunks(self.mine, self.other, self.part, self.middle, stride)

    def rows(self, first, count):
        bit, part, middle = self.ring.x_bit, self.part, self.middle
        low = first - part
        ahead, behind = self.pieces
        parts = [self.mine[0][0][0, first : first + count]]
        for array, kind, _ in self.mine:
            if kind == "piece":
                parts.append(lax.dynamic_slice_in_dim(array[0], first - part * bit, count, 0))
        parts.append(jnp.where(bit == 0, behind[first - middle :][:count], ahead[low:][:count]))
        return jnp.stack(parts)


class Scatter:
    def __init__(self, ring, *values):
        self.ring, self.values = ring, values
        self.distance = ring.size // 2
        self.split = values[0].shape[1] // 2

    def piece(self, place, row, count):
        tok, width = self.ring.tok_at(place), self.values[0].shape[2]
        return sum(
            lax.dynamic_slice(values, (tok, row, 0), (1, count, width))[0].astype(f32)
            for values in self.values
        )

    def hop(self):
        ring, distance, split = self.ring, self.distance, self.split
        rows = self.values[0].shape[1]
        if distance == ring.size // 2:
            ahead = self.piece(distance, 0, split)
            behind = self.piece(distance, split, rows - split)
        else:
            ahead, behind = self.ahead.astype(f32), self.behind.astype(f32)
            if distance == ring.size // 2 - 1:
                ahead = jnp.pad(ahead, ((0, rows - split), (0, 0)))
                behind = jnp.pad(behind, ((split, 0), (0, 0)))
            ahead = self.piece(distance, 0, rows) + ahead
            behind = self.piece(-distance, 0, rows) + behind
        self.distance -= 1
        return ring.forward(ahead.astype(bf16)), ring.backward(behind.astype(bf16))

    def land(self, flight):
        self.ahead, self.behind = flight

    def total(self):
        rows = self.values[0].shape[1]
        total = self.piece(0, 0, rows) + self.ahead.astype(f32) + self.behind.astype(f32)
        return total.astype(bf16)


class CrossScatter:
    def __init__(self, ring, part, middle, *values):
        self.ring, self.values, self.part, self.middle = ring, values, part, middle
        self.half = self.distance = ring.size // 2
        self.split = (part + middle) // 2
        self.extras = {}

    def chip(self, place, row, count):
        tok, width = self.ring.tok_at(place), self.values[0].shape[2]
        return sum(
            lax.dynamic_slice(values, (tok, row, 0), (1, count, width))[0].astype(f32)
            for values in self.values
        )

    def cross(self, *distances):
        row = (self.part + self.middle) * (1 - self.ring.x_bit)
        places = [place for d in distances for place in ((d,) if d in (0, self.half) else (d, -d))]
        sent = jnp.stack([self.chip(place, row, self.part).astype(bf16) for place in places])
        return places, swap_x(sent)

    def land_cross(self, places, got):
        for number, place in enumerate(places):
            self.extras[place] = got[number]

    def piece(self, place):
        part, bit = self.part, self.ring.x_bit
        extra = self.extras[place].astype(f32)
        blank = jnp.zeros((self.middle, extra.shape[1]), f32)
        return self.chip(place, part * bit, part + self.middle) + jnp.where(
            bit == 0, jnp.concatenate([extra, blank]), jnp.concatenate([blank, extra])
        )

    def hop(self):
        ring, distance, split = self.ring, self.distance, self.split
        if distance == self.half:
            farthest = self.piece(distance)
            ahead, behind = farthest[:split], farthest[split:]
        else:
            ahead, behind = self.ahead.astype(f32), self.behind.astype(f32)
            if distance == self.half - 1:
                rows = self.part + self.middle
                ahead = jnp.pad(ahead, ((0, rows - split), (0, 0)))
                behind = jnp.pad(behind, ((split, 0), (0, 0)))
            ahead = self.piece(distance) + ahead
            behind = self.piece(-distance) + behind
        self.distance -= 1
        return ring.forward(ahead.astype(bf16)), ring.backward(behind.astype(bf16))

    def land(self, flight):
        self.ahead, self.behind = flight

    def total(self):
        total = self.piece(0) + self.ahead.astype(f32) + self.behind.astype(f32)
        return total.astype(bf16)

    def join(self, total, far):
        part, bit = self.part, self.ring.x_bit
        low, high = jnp.where(bit == 0, total, far), jnp.where(bit == 0, far, total)
        return jnp.concatenate(
            [low[:part], add_low(low[part:], high[: self.middle]), high[self.middle :]]
        )


def gather_plain(shard, share):
    size, width = lax.axis_size("tok"), shard.shape[1]
    full = lax.all_gather(shard, "tok", axis=0)
    blocks = [
        full[:, row : row + share].reshape(8, -1, width) for row in range(0, shard.shape[0], share)
    ]
    return jnp.concatenate(blocks, axis=1)


def by_tok(values, share):
    size = lax.axis_size("tok")
    if size == 8:
        return values
    rows = share * size // 8
    blocks = [
        values[:, row : row + rows].reshape(size, share, -1)
        for row in range(0, values.shape[1], rows)
    ]
    return jnp.concatenate(blocks, axis=1)


def scatter_plain(chip):
    return lax.psum_scatter(chip, "tok", scatter_dimension=0, tiled=True)[0]


def gather_grp(values):
    step = 1
    while step < lax.axis_size("grp"):
        got = lax.ppermute(values, "grp", swap_pairs(lax.axis_size("grp"), step))
        values = jnp.concatenate([values, got])
        step *= 2
    return values


def add_x(shard):
    step = 2
    while step < lax.axis_size("grp"):
        shard = add_low(shard, lax.ppermute(shard, "grp", swap_pairs(lax.axis_size("grp"), step)))
        step *= 2
    return shard


def spread_kernel(weight_ref, out_ref, *, count):
    share = weight_ref.shape[0]
    for block in range(4):
        pieces = [
            weight_ref[:, (4 * tok + block) * share : (4 * tok + block + 1) * share]
            for tok in range(count)
        ]
        out_ref[block] = jnp.concatenate(pieces, axis=1).astype(bf16)


def spread_call(weight, count):
    share = weight.shape[0]
    return pl.pallas_call(
        functools.partial(spread_kernel, count=count),
        out_shape=jax.ShapeDtypeStruct((4, share, weight.shape[1] // 4), bf16),
        compiler_params=params(),
    )(weight)


def unspread_kernel(core_ref, mine_ref, other_ref, out_ref, *, count):
    share = mine_ref.shape[1]

    def write(refs):
        pieces = [
            refs[block // 2][block % 2, :, tok * share : (tok + 1) * share].astype(f32)
            for tok in range(count)
            for block in range(4)
        ]
        out_ref[...] = jnp.concatenate(pieces, axis=1)

    @pl.when(core_ref[0] == 0)
    def _():
        write((mine_ref, other_ref))

    @pl.when(core_ref[0] != 0)
    def _():
        write((other_ref, mine_ref))


def unspread_call(core, mine, other, count):
    share, width = mine.shape[1:]
    return pl.pallas_call(
        functools.partial(unspread_kernel, count=count),
        in_specs=[smem, whole_block(mine), whole_block(other)],
        out_shape=jax.ShapeDtypeStruct((share, 4 * width), f32),
        compiler_params=params(),
    )(core, mine, other)


def on_device(
    kept_tokens,
    kept_index,
    kept_count,
    condition,
    mask_token,
    position_table,
    modulation_weight,
    modulation_bias,
    input_weight,
    query_bias,
    value_bias,
    output_weight,
    output_bias,
    up_weight,
    up_bias,
    down_weight,
    down_bias,
    cotangent,
):
    _, seq_len, width = cotangent.shape
    tok_count = lax.axis_size("tok")
    core = lax.axis_index("grp") % 2
    share = input_weight.shape[0]
    position_rows = position_table.shape[0]

    def by_core(first, second):
        return jnp.where(core == 0, first, second)

    def by_core_pair(pairs):
        return [by_core(first, second) for first, second in zip(*pairs)]

    def exchange(values):
        return lax.all_to_all(values, "tok", split_axis=0, concat_axis=0, tiled=True)

    ring = Ring()

    core_row = jnp.stack([core, ring.x_bit])
    condition_low = jax.nn.silu(condition).astype(bf16)
    slots_here = kept_tokens.shape[1]
    small_here = jnp.concatenate(
        [
            jnp.stack([mask_token, query_bias, value_bias, output_bias, down_bias]),
            up_bias.reshape(4, share),
        ]
    ).astype(bf16)
    extra = lax.dynamic_update_slice(
        jnp.zeros((16, width), bf16), small_here, (0, share * lax.axis_index("tok"))
    )
    extra = jnp.concatenate([extra[:9], condition_low, extra[10:]])
    arrived = exchange(
        jnp.concatenate(
            [kept_tokens.astype(bf16), jnp.broadcast_to(extra, (tok_count, 16, width))], axis=1
        )
    )
    condition_group = arrived[:, slots_here + 9]
    small = jnp.sum(arrived[:, slots_here:].astype(f32), axis=0)

    def modulate_all(conditions, weight):
        modulation_part = jnp.dot(
            conditions, weight, preferred_element_type=f32
        ) + modulation_bias.astype(bf16).astype(f32)
        return exchange(modulation_part).reshape(6, width)

    condition_all = gather_grp(condition_group)

    ringed = share % 16 == 0 and lax.axis_size("grp") == 4
    table_rows = position_rows // 2

    input_low = input_weight.astype(bf16)
    input_blocks = [input_low[:, number * width : (number + 1) * width] for number in range(3)]
    position_low = position_table.astype(bf16)
    attention_pairs = input_blocks[:2], [input_blocks[2], output_weight.astype(bf16)]
    attention_low = tuple(
        jnp.concatenate([pair[0], position_low[half * table_rows : (half + 1) * table_rows], pair[1]])
        for half, pair in enumerate(attention_pairs)
    )
    attention_cut, feed_cut = (7 * share // 9, 8 * share // 9), (4 * share // 3, 4 * share // 3)
    if ringed:
        mine, other = by_core(*attention_low), by_core(*attention_low[::-1])
        gather = Gather(ring, mine, other, *attention_cut)
        flight, up_weight, down_weight, modulation_weight = sync(
            gather.issue(), up_weight, down_weight, modulation_weight
        )
        gather.land(flight)
        (flight,) = sync(gather.issue())
        gather.land(flight)
    modulation_low = modulation_weight.astype(bf16)
    up_low = spread_call(up_weight, tok_count)
    down_low = down_weight.astype(bf16).reshape(4, share, width)
    feed_low = tuple(
        jnp.concatenate([up_low[half : half + 2], down_low[half : half + 2]]).reshape(-1, width)
        for half in (0, 2)
    )
    if ringed:
        mine, other = by_core(*feed_low), by_core(*feed_low[::-1])
        flight, condition_group, arrived, small, mine, other, modulation_low = sync(
            gather.issue(), condition_group, arrived, small, mine, other, modulation_low
        )
        gather.land(flight)
        feed_gather = Gather(ring, mine, other, *feed_cut)
        flight, condition_group = sync(gather.issue(), condition_group)
        gather.land(flight)
    mod = modulate_all(condition_group, modulation_low)
    if ringed:
        table_mine = gather.rows(share, table_rows)
        feed_flight = feed_gather.issue()
        flight, table_mine, table_other, mod = sync(
            gather.issue(), table_mine, swap_core(table_mine), mod
        )
        gather.land(flight)
        flight = gather.issue()
        distances = [0]
        for distance in range(1, ring.size // 2):
            distances += [-distance, distance]
        places = ring.tok_at(jnp.array(distances + [ring.size // 2], jnp.int32))
    else:
        places = jnp.arange(8, dtype=jnp.int32)
        mine = gather_plain(jnp.concatenate(by_core_pair(attention_pairs)), share)
        everywhere = list(range(8))
        plain_chunks = lambda mine: Chunks(
            [(mine, "all", everywhere)], [(swap_core(mine), "all", everywhere)]
        )
        attention_chunks = plain_chunks(mine)
        feed_chunks = plain_chunks(gather_plain(by_core(*feed_low), share))
        table = lax.all_gather(position_low, "tok").reshape(8, -1, width)

        halves = jnp.split(table, 2, axis=1)
        table_mine, table_other = by_core(*halves), by_core(*halves[::-1])
    table_chunks = Chunks(
        [(table_mine, "all", list(range(8)))], [(table_other, "all", list(range(8)))]
    )
    start, norm_one = start_call(
        core_row, places, kept_count, kept_index, arrived, small, mod, table_chunks, 0,
        table_mine.shape[1], seq_len,
    )
    if ringed:
        flight, feed_flight, start, norm_one = sync(flight, feed_flight, start, norm_one)
        gather.land(flight)
        attention_chunks = gather.chunks(share + table_rows)
        feed_gather.land(feed_flight)
    projected = project_call(core_row, places, norm_one, small, attention_chunks)
    if ringed:
        flight, projected, start = sync(feed_gather.issue(), projected, start)
        feed_gather.land(flight)
    attended = None
    for first, heads in forward_groups:
        attended = attend_call(projected, first, heads, attended)
        if ringed:
            flight, attended, projected = sync(feed_gather.issue(), attended, projected)
            feed_gather.land(flight)
    joined, branch_one, middle, norm_two = mix_call(
        core_row, places, attended[0], start, small, mod, attention_chunks
    )
    if ringed:
        flight, norm_two = sync(feed_gather.issue(), norm_two)
        feed_gather.land(flight)
        (flight,) = sync(feed_gather.issue())
        feed_gather.land(flight)
        feed_chunks = feed_gather.chunks()
    (
        block_output,
        hidden,
        pre_grad,
        grad_two,
        middle_grad,
        grad_one,
        feed_sums,
        up_bias_sum,
    ) = feed_call(
        core_row, places, norm_two, middle, cotangent[0], branch_one, mod, small, feed_chunks
    )
    far, near = 2 - 2 * core_row[:1], 2 * core_row[:1]
    other_up = feed_weight_call(far, norm_two, pre_grad)
    other_up, hidden, grad_one = sync(other_up, hidden, grad_one)
    other_down = feed_weight_call(far, hidden, grad_two)
    got_up, other_down, norm_two = sync(swap_core(other_up), other_down, norm_two)
    feed_chip = feed_weight_call(near, norm_two, pre_grad, got_up, rows=4)
    got_down, feed_chip, hidden = sync(swap_core(other_down), feed_chip, hidden)
    feed_chip = feed_weight_call(near, hidden, grad_two, got_down, feed_chip, 2, 4)
    feed_chip, grad_one = sync(feed_chip, grad_one)
    mix_grad = mix_grad_call(core_row, places, grad_one, attention_chunks)
    if ringed:
        feed_scatter = Scatter(ring, feed_chip)
    grads = []
    for group, (first, heads) in enumerate(back_groups):
        grads.append(attend_back_call(projected, attended, mix_grad, first, heads))
        if ringed and group < 2:
            flight, grads, mix_grad = sync(feed_scatter.hop(), grads, mix_grad)
            feed_scatter.land(flight)
    grads = [triple[block] for block in range(3) for triple in grads]

    def attention_weights(owner, norm):
        return attention_weight_call(owner, norm, joined, grad_one, grads)

    def start_back(quarter, earlier, grads):
        return start_back_call(
            quarter, earlier, core_row, places, kept_count, kept_index, grads, middle_grad, start, mod,
            attention_chunks,
        )

    attention_other = attention_weights(1 - core_row[:1], norm_one)
    if ringed:
        flight, attention_other, norm_one, grads = sync(
            feed_scatter.hop(), attention_other, norm_one, grads
        )
        feed_scatter.land(flight)
        feed_flight = feed_scatter.hop()
    attention_mine = attention_weights(core_row[:1], norm_one)
    attention_got = swap_core(attention_other)
    if ringed:
        attention_mine, attention_got, grads = sync(attention_mine, attention_got, grads)
        scatter = CrossScatter(ring, 2 * share // 3, 2 * share // 3, attention_mine, attention_got)
    quarters = []
    slot_grad = None
    for quarter in range(4):
        part = start_back(quarter, slot_grad, grads)
        if ringed:
            if quarter == 0:
                places_crossed, crossed = scatter.cross(scatter.half, scatter.half - 1)
                crossed, part, grads, feed_flight = sync(crossed, part, grads, feed_flight)
                feed_scatter.land(feed_flight)
                feed_shard = feed_scatter.total()
                feed_cross = swap_x(feed_shard)
            else:
                following = (scatter.half - 1 - quarter,)
                if quarter == 3:
                    following = tuple(range(scatter.half - 4, -1, -1))
                places_crossed, crossed = scatter.cross(*following)
                flight, crossed, part, grads = sync(scatter.hop(), crossed, part, grads)
                scatter.land(flight)
            scatter.land_cross(places_crossed, crossed)
        quarters.append(part)
        slot_grad = part[1]
    row_grad = jnp.concatenate([part[0] for part in quarters])
    slot_grad, small_grad = collect_call(
        feed_sums, up_bias_sum, slot_grad, *[part[2] for part in quarters]
    )

    position_grad = row_grad.reshape(tok_count, position_rows, width)
    halves = [
        half.reshape(-1, width)
        for half in (position_grad[:, :table_rows], position_grad[:, table_rows:])
    ]
    table_got = swap_core(jnp.concatenate([by_core(halves[1], halves[0]), small_grad]))
    arrived = exchange(slot_grad)
    table_chip = add_low(jnp.concatenate([by_core(halves[0], halves[1]), small_grad]), table_got)
    small_chip = table_chip[-16:]
    table_chip = table_chip[:-16].reshape(tok_count, table_rows, width)
    half_rows = table_rows // 2
    table_near, table_away = (
        jnp.concatenate(
            [
                lax.dynamic_slice_in_dim(table_chip, half_rows * place, half_rows, 1).reshape(-1, width),
                small_chip,
            ]
        )
        for place in (ring.x_bit, 1 - ring.x_bit)
    )
    table_got = swap_x(table_away)
    if ringed:
        while scatter.distance > 0:
            scatter.land(scatter.hop())
        attention_shard = scatter.total()
        attention_cross = swap_x(attention_shard)
    table_pair = add_low(table_near, table_got)
    table_pair, small_grad, arrived = sync(table_pair[:-16], table_pair[-16:], arrived)
    kept_low = arrived[:, :slots_here]
    modulation_grad_group = arrived[:, slots_here, : modulation_bias.shape[0]]
    condition_part = jnp.einsum(
        "ie,de->id", modulation_grad_group, modulation_low, preferred_element_type=f32
    )
    condition_high = condition_part.astype(bf16)
    condition_rest = (condition_part - condition_high.astype(f32)).astype(bf16)
    table_parts = exchange(
        jnp.concatenate(
            [
                table_pair.reshape(tok_count, half_rows, width),
                jnp.broadcast_to(small_grad[:14], (tok_count, 14, width)),
                condition_high[:, None],
                condition_rest[:, None],
            ],
            axis=1,
        )
    )
    modulation_grad_all = gather_grp(modulation_grad_group)
    modulation_total = jnp.einsum(
        "id,ie->de", condition_all, modulation_grad_all, preferred_element_type=f32
    )
    modulation_bias_total = jnp.sum(modulation_grad_all.astype(f32), axis=0)
    table_sum = jnp.sum(table_parts.astype(f32), axis=0)
    table_shard = table_sum.astype(bf16)
    condition_low_grad = table_sum[-2:-1] + table_sum[-1:]
    step = 4
    while step < lax.axis_size("grp"):
        table_shard = add_low(
            table_shard, lax.ppermute(table_shard, "grp", swap_pairs(lax.axis_size("grp"), step))
        )
        step *= 2
    table_cross = swap_x(table_shard[:half_rows])
    table_half = jnp.concatenate(
        [
            jnp.where(ring.x_bit == 0, table_shard[:half_rows], table_cross),
            jnp.where(ring.x_bit == 0, table_cross, table_shard[:half_rows]),
        ]
    )
    if ringed:
        attention_shard = scatter.join(attention_shard, attention_cross)
        feed_shard = add_low(feed_shard, feed_cross)
    else:
        attention_chip = by_tok(add_low(attention_mine, attention_got), share)
        attention_shard = add_x(scatter_plain(attention_chip))
        feed_shard = add_x(scatter_plain(by_tok(feed_chip, share)))
    table_far = swap_core(table_half)
    position_total = jnp.concatenate(
        [by_core(table_half, table_far), by_core(table_far, table_half)]
    ).astype(f32)
    small_total = lax.dynamic_slice_in_dim(
        table_shard[half_rows:], share * lax.axis_index("tok"), share, 1
    ).astype(f32)
    mask_total, query_bias_total, value_bias_total, output_bias_total, down_bias_total = (
        small_total[number] for number in range(5)
    )
    up_bias_total = small_total[5:9].reshape(-1)
    kept_grad = kept_low.astype(f32)
    far = swap_core(attention_shard)
    first, second = by_core(attention_shard, far).astype(f32), by_core(far, attention_shard).astype(f32)
    input_total = jnp.concatenate([first[:share], first[share:], second[:share]], axis=1)
    output_total = second[share:]
    feed_shard = feed_shard.reshape(4, share, width)
    feed_far = swap_core(feed_shard)
    up_total = unspread_call(core_row, feed_shard[:2], feed_far[:2], tok_count)
    down_total = jnp.concatenate(
        [by_core(feed_shard[2:], feed_far[2:]), by_core(feed_far[2:], feed_shard[2:])]
    ).reshape(-1, width).astype(f32)

    _, silu_back = jax.vjp(jax.nn.silu, condition)
    condition_grad = silu_back(condition_low_grad)[0]
    return (
        block_output[None],
        kept_grad,
        condition_grad,
        mask_total,
        position_total,
        modulation_total,
        modulation_bias_total,
        input_total,
        query_bias_total,
        value_bias_total,
        output_total,
        output_bias_total,
        up_total,
        up_bias_total,
        down_total,
        down_bias_total,
    )


def solution(mesh):
    return jax.shard_map(
        on_device,
        mesh=mesh,
        in_specs=(
            P("grp", "tok", None),
            P(("grp", "tok"), None),
            P(("grp", "tok")),
            P(("grp", "tok"), None),
            P("tok"),
            P("tok", None),
            P(None, "tok"),
            P("tok"),
            P("tok", None),
            P("tok"),
            P("tok"),
            P("tok", None),
            P("tok"),
            P("tok", None),
            P("tok"),
            P("tok", None),
            P("tok"),
            P(("grp", "tok"), None, None),
        ),
        out_specs=(
            P(("grp", "tok"), None, None),
            P("grp", "tok", None),
            P(("grp", "tok"), None),
            P("tok"),
            P("tok", None),
            P(None, "tok"),
            P("tok"),
            P("tok", None),
            P("tok"),
            P("tok"),
            P("tok", None),
            P("tok"),
            P("tok", None),
            P("tok"),
            P("tok", None),
            P("tok"),
        ),
        check_vma=False,
    )
```

```python
import functools
import math

import jax
import jax.numpy as jnp
from jax import lax
from jax.experimental import pallas as pl
from jax.experimental.pallas import tpu as pltpu
from jax.sharding import PartitionSpec as P

H = 16
HD = 72
LANES = 128

epsilon = 1e-06
f32 = jnp.float32
bf16 = jnp.bfloat16
plain = (((1,), (0,)), ((), ()))
right_turned = (((1,), (1,)), ((), ()))
left_turned = (((0,), (0,)), ((), ()))
vmem_limit = 60 << 20


def product(left, right, dims=plain):
    return lax.dot_general(left, right, dims, preferred_element_type=f32)


def whole_block(array):
    zeros = (0,) * array.ndim
    return pl.BlockSpec(array.shape, lambda *_: zeros)


def row_block(rows, *rest):
    return pl.BlockSpec((rows,) + rest, lambda i: (i,) + (0,) * len(rest))


smem = pl.BlockSpec(memory_space=pltpu.SMEM)
anywhere = pl.BlockSpec(memory_space=pl.ANY)


def params():
    return pltpu.CompilerParams(vmem_limit_bytes=vmem_limit)


def cost(flops, moved, exps=0):
    return pl.CostEstimate(flops=int(flops), bytes_accessed=int(moved), transcendentals=int(exps))


def column_sum(values):
    return jnp.sum(values, axis=0, keepdims=True)


def normalize(values):
    center = values - jnp.mean(values, axis=-1, keepdims=True)
    spread = jnp.mean(center * center, axis=-1, keepdims=True)
    inverse = lax.rsqrt(spread + epsilon)
    return center * inverse, inverse


def normalize_back(grad, unit, inverse, scale):
    scaled = grad * (1.0 + scale)
    first = jnp.mean(scaled, axis=-1, keepdims=True)
    second = jnp.mean(scaled * unit, axis=-1, keepdims=True)
    return (scaled - first - unit * second) * inverse


def start_kernel(core_ref, places_ref, count_ref, index_ref, kept_ref, small_ref, mod_ref, *rest, chunks, row, share):
    refs, (start_ref, norm_ref, table, sems) = rest[: len(chunks.arrays)], rest[len(chunks.arrays) :]
    rows, slots = start_ref.shape[0], index_ref.shape[1]
    step = pl.program_id(0)
    low, high = table.at[:, :share], table.at[:, share:]

    @pl.when(step == 0)
    def _():
        @pl.when(core_ref[0] == 0)
        def _():
            chunks.load(refs, places_ref, core_ref, True, row, low, sems.at[0])
            chunks.load(refs, places_ref, core_ref, False, row, high, sems.at[1])

        @pl.when(core_ref[0] != 0)
        def _():
            chunks.load(refs, places_ref, core_ref, False, row, low, sems.at[0])
            chunks.load(refs, places_ref, core_ref, True, row, high, sems.at[1])

        wait_block(low, sems.at[0])
        wait_block(high, sems.at[1])

    base = step * rows
    here = lax.broadcasted_iota(jnp.int32, (rows, slots), 0) + base
    slot = lax.broadcasted_iota(jnp.int32, (rows, slots), 1)
    chosen = jnp.where((index_ref[...] == here) & (slot < count_ref[0]), 1.0, 0.0)
    kept = kept_ref[:, : slots // kept_ref.shape[0]].reshape(slots, -1)
    filled = product(chosen.astype(bf16), kept)
    empty = 1.0 - jnp.sum(chosen, axis=1, keepdims=True)
    groups_here = rows // table.shape[1]
    position = table[pl.ds(step * groups_here, groups_here)].reshape(rows, -1)
    start = filled + empty * small_ref[0:1] + position.astype(f32)
    start_ref[...] = start
    unit, _ = normalize(start)
    norm_ref[...] = (unit * (1.0 + mod_ref[1:2]) + mod_ref[0:1]).astype(bf16)


def start_call(core, places, count, index, kept, small, mod, chunks, row, share, seq_len):
    width = kept.shape[2]
    rows = seq_len // 4
    return pl.pallas_call(
        functools.partial(start_kernel, chunks=chunks, row=row, share=share),
        grid=(4,),
        in_specs=[
            smem,
            smem,
            smem,
            whole_block(index),
            whole_block(kept),
            whole_block(small),
            whole_block(mod),
        ]
        + chunks.specs,
        out_specs=[row_block(rows, width)] * 2,
        out_shape=[
            jax.ShapeDtypeStruct((seq_len, width), f32),
            jax.ShapeDtypeStruct((seq_len, width), bf16),
        ],
        scratch_shapes=[
            pltpu.VMEM((8, seq_len // 8, width), bf16),
            pltpu.SemaphoreType.DMA((2,)),
        ],
        compiler_params=params(),
        cost_estimate=cost(2 * seq_len * width * index.shape[1], 14 * seq_len * width),
    )(core, places, count, index, kept, small, mod, *chunks.arrays)


class Chunks:
    def __init__(self, mine, other, part=0, middle=0, stride=0):
        self.sources = list(mine), list(other)
        self.part, self.middle, self.stride = part, middle, stride
        self.arrays = [entry[0] for source in self.sources for entry in source]
        self.specs = [anywhere] * len(self.arrays)

    def span(self, kind, bit):
        part, middle = self.part, self.middle
        start = part * bit
        return {
            "piece": (start, start + part + middle),
            "first": (start, start + middle),
            "second": (start + middle, start + part + middle),
            "got": ((0, part) if bit else (part + middle, 2 * part + middle)),
            "all": (0, 1 << 20),
        }[kind]

    def spans(self, kind, bit):
        if kind == "pair":
            return [self.span("piece", bit) + (0,), self.span("got", bit) + (self.part + self.middle,)]
        return [self.span(kind, bit) + (0,)]

    def load(self, refs, places_ref, spot_ref, from_mine, row, target, sem):
        source = self.sources[0 if from_mine else 1]
        refs = refs[: len(source)] if from_mine else refs[len(self.sources[0]) :]

        def start(ref, kind, places, bit):
            for low, high, base in self.spans(kind, bit):
                begin, end = max(row, low), min(row + target.shape[1], high)
                for index, place in enumerate(places if begin < end else []):
                    pltpu.make_async_copy(
                        ref.at[index, pl.ds(base + begin - low, end - begin)],
                        target.at[places_ref[place], pl.ds(begin - row, end - begin)],
                        sem,
                    ).start()

        for ref, (_, kind, places) in zip(refs, source):
            if kind == "all":
                start(ref, kind, places, 0)
        if any(kind != "all" for _, kind, _ in source):
            for bit in (0, 1):

                @pl.when(spot_ref[1] == bit)
                def _():
                    for ref, (_, kind, places) in zip(refs, source):
                        if kind != "all":
                            start(ref, kind, places, bit)

    def load_block(self, refs, places_ref, spot_ref, block, target, sem, first=0):
        rows = target.shape[1]
        owner, row = block // 2, first * rows + (block % 2) * (self.stride or rows)

        @pl.when(spot_ref[0] == owner)
        def _():
            self.load(refs, places_ref, spot_ref, True, row, target, sem)

        @pl.when(spot_ref[0] != owner)
        def _():
            self.load(refs, places_ref, spot_ref, False, row, target, sem)


def wait_block(target, sem):
    pltpu.make_async_copy(target, target, sem).wait()


def square(weight):
    return weight.reshape(-1, weight.shape[-1])


def split_heads(values, store):
    rows = values.shape[0]
    blank = jnp.zeros((rows, LANES - HD), values.dtype)
    for head in range(H):
        store(head, jnp.concatenate([values[:, head * HD : (head + 1) * HD], blank], axis=1))


def project_kernel(core_ref, places_ref, norm_ref, small_ref, *rest, chunks):
    refs, (out_ref, weight, sems) = rest[: len(chunks.arrays)], rest[len(chunks.arrays) :]
    step, part = pl.program_id(0), pl.program_id(1)

    @pl.when((step == 0) & (part == 0))
    def _():
        for block in range(3):
            chunks.load_block(refs, places_ref, core_ref, block, weight.at[block], sems.at[block])

    @pl.when(part == 0)
    def _():
        wait_block(weight.at[step], sems.at[step])

    key_free = jnp.where(step == 1, 0.0, 1.0)
    bias = jnp.where(step == 0, small_ref[1:2], small_ref[2:3]) * key_free
    result = product(norm_ref[...], square(weight[step])) + bias

    def store(head, value):
        out_ref[0, head] = value

    split_heads(result.astype(bf16), store)


def project_call(core, places, norm, small, chunks):
    seq_len, width = norm.shape
    return pl.pallas_call(
        functools.partial(project_kernel, chunks=chunks),
        grid=(3, 2),
        in_specs=[
            smem,
            smem,
            pl.BlockSpec((seq_len // 2, width), lambda i, j: (j, 0)),
            whole_block(small),
        ]
        + chunks.specs,
        out_specs=pl.BlockSpec((1, H, seq_len // 2, LANES), lambda i, j: (i, 0, j, 0)),
        out_shape=jax.ShapeDtypeStruct((3, H, seq_len, LANES), bf16),
        scratch_shapes=[
            pltpu.VMEM((3, 8, width // 8, width), bf16),
            pltpu.SemaphoreType.DMA((3,)),
        ],
        compiler_params=params(),
        cost_estimate=cost(6 * seq_len * width * width, 12 * seq_len * width + 6 * width * width),
    )(core, places, norm, small, *chunks.arrays)


heads_a_step = 2
forward_groups = ((0, 8), (8, 8))
back_groups = ((0, 4), (4, 8), (12, 4))
groups = len(back_groups)


def attend_kernel(query_ref, key_ref, value_ref, *rest, factor):
    mix_ref, log_ref = rest[-2:]
    for head in range(query_ref.shape[1]):
        scores = product(key_ref[0, head], query_ref[0, head], right_turned)
        top = jnp.max(scores, axis=0, keepdims=True)
        weights = jnp.exp2((scores - top) * factor)
        total = jnp.sum(weights, axis=0, keepdims=True)
        mix = product(value_ref[0, head].T, weights.astype(bf16))
        mix_ref[head] = (mix / total).T.astype(bf16)
        log_ref[head] = top * factor + jnp.log2(total)


def head_block(place, seq_len, first):
    first = first // heads_a_step
    return pl.BlockSpec((1, heads_a_step, seq_len, LANES), lambda h: (place, first + h, 0, 0))


def head_rows(first, *rest):
    first = first // heads_a_step
    return pl.BlockSpec((heads_a_step,) + rest, lambda h: (first + h, 0, 0))


def attend_call(projected, first, heads, earlier=None):
    seq_len = projected.shape[2]
    kept = [] if earlier is None else list(earlier)
    return pl.pallas_call(
        functools.partial(
            attend_kernel, factor=math.log2(math.e) / math.sqrt(HD)
        ),
        grid=(heads // heads_a_step,),
        in_specs=[head_block(place, seq_len, first) for place in range(3)] + [anywhere] * len(kept),
        out_specs=[
            head_rows(first, seq_len, LANES),
            head_rows(first, 1, seq_len),
        ],
        out_shape=[
            jax.ShapeDtypeStruct((H, seq_len, LANES), bf16),
            jax.ShapeDtypeStruct((H, 1, seq_len), f32),
        ],
        input_output_aliases={3: 0, 4: 1} if kept else {},
        compiler_params=params(),
        cost_estimate=cost(4 * heads * seq_len * seq_len * 256, 8 * heads * seq_len * LANES, heads * seq_len * seq_len),
    )(projected, projected, projected, *kept)


def attend_back_kernel(
    query_ref, key_ref, value_ref, mix_ref, log_ref, grad_ref, query_grad_ref, key_grad_ref,
    value_grad_ref, *, factor
):
    base_two = factor * math.log2(math.e)
    for head in range(query_ref.shape[1]):
        query, key, value = query_ref[0, head], key_ref[0, head], value_ref[0, head]
        grad = grad_ref[head]
        scores = product(key, query, right_turned)
        weights = jnp.exp2(scores * base_two - log_ref[head])
        value_grad_ref[head] = product(weights.astype(bf16), grad).astype(bf16)
        weight_grad = product(value, grad, right_turned)
        inner = column_sum((grad.astype(f32) * mix_ref[head].astype(f32)).T)
        score_grad = (weights * (weight_grad - inner)).astype(bf16)
        key_grad_ref[head] = (product(score_grad, query) * factor).astype(bf16)
        query_grad_ref[head] = (product(key.T, score_grad) * factor).T.astype(bf16)


def attend_back_call(projected, attended, grad, first, heads):
    seq_len = projected.shape[2]
    mix, logs = attended
    flat = head_rows(0, seq_len, LANES)
    return pl.pallas_call(
        functools.partial(attend_back_kernel, factor=1.0 / math.sqrt(HD)),
        grid=(heads // heads_a_step,),
        in_specs=[head_block(place, seq_len, first) for place in range(3)]
        + [
            head_rows(first, seq_len, LANES),
            head_rows(first, 1, seq_len),
            head_rows(first, seq_len, LANES),
        ],
        out_specs=[flat] * 3,
        out_shape=[jax.ShapeDtypeStruct((heads, seq_len, LANES), bf16)] * 3,
        compiler_params=params(),
        cost_estimate=cost(10 * heads * seq_len * seq_len * 256, 16 * heads * seq_len * LANES, heads * seq_len * seq_len),
    )(projected, projected, projected, mix, logs, grad)


def join_heads(refs):
    return jnp.concatenate(
        [ref[head][:, :HD] for ref in refs for head in range(ref.shape[0])], axis=1
    )


def mix_kernel(core_ref, places_ref, start_ref, small_ref, mod_ref, *rest, chunks):
    mix_refs, rest = rest[:1], rest[1:]
    refs, rest = rest[: len(chunks.arrays)], rest[len(chunks.arrays) :]
    joined_ref, branch_ref, middle_ref, norm_ref, weight, sem = rest

    @pl.when(pl.program_id(0) == 0)
    def _():
        chunks.load_block(refs, places_ref, core_ref, 3, weight, sem)
        wait_block(weight, sem)

    joined = join_heads(mix_refs)
    joined_ref[...] = joined
    branch = product(joined, square(weight[...])) + small_ref[3:4]
    branch_ref[...] = branch.astype(bf16)
    middle = start_ref[...] + mod_ref[2:3] * branch
    middle_ref[...] = middle
    unit, _ = normalize(middle)
    norm_ref[...] = (unit * (1.0 + mod_ref[4:5]) + mod_ref[3:4]).astype(bf16)


def mix_call(core, places, mix, start, small, mod, chunks):
    seq_len, width = start.shape
    rows = seq_len // 4
    block = row_block(rows, width)
    return pl.pallas_call(
        functools.partial(mix_kernel, chunks=chunks),
        grid=(4,),
        in_specs=[smem, smem, block, whole_block(small), whole_block(mod)]
        + [pl.BlockSpec((H, rows, LANES), lambda i: (0, i, 0))]
        + chunks.specs,
        out_specs=[block] * 4,
        out_shape=[
            jax.ShapeDtypeStruct((seq_len, width), kind) for kind in (bf16, bf16, f32, bf16)
        ],
        scratch_shapes=[pltpu.VMEM((8, width // 8, width), bf16), pltpu.SemaphoreType.DMA],
        compiler_params=params(),
        cost_estimate=cost(2 * seq_len * width * width, 18 * seq_len * width),
    )(core, places, start, small, mod, mix, *chunks.arrays)


def gelu_parts(values):
    inner = 0.7978845608028654 * (values + 0.044715 * values * values * values)
    turned = jnp.tanh(inner)
    half = 0.5 * (1.0 + turned)
    slope = half + 0.5 * values * (1.0 - turned * turned) * (
        0.7978845608028654 * (1.0 + 0.134145 * values * values)
    )
    return values * half, slope


def feed_kernel(
    core_ref, places_ref, norm_ref, middle_ref, cot_ref, branch_ref, mod_ref, small_ref, *rest, source
):
    refs, rest = rest[: len(source.arrays)], rest[len(source.arrays) :]
    (
        out_ref, hidden_ref, pre_ref, grad_two_ref, middle_grad_ref, grad_one_ref, sums_ref,
        up_sums_ref, up, down, slopes, sems,
    ) = rest
    step = pl.program_id(0)
    chunks = 4

    @pl.when(step == 0)
    def _():
        for chunk in range(chunks):
            for side, target in enumerate((up, down)):
                source.load_block(
                    refs, places_ref, core_ref, chunk, target.at[chunk], sems.at[side, chunk], 2 * side
                )
        sums_ref[...] = jnp.zeros_like(sums_ref)
        up_sums_ref[...] = jnp.zeros_like(up_sums_ref)

    norm = norm_ref[...]
    total = None
    for chunk in range(chunks):

        @pl.when(step == 0)
        def _():
            wait_block(up.at[chunk], sems.at[0, chunk])
            wait_block(down.at[chunk], sems.at[1, chunk])

        before = product(norm, square(up[chunk])) + small_ref[5 + chunk : 6 + chunk]
        hidden, slope = gelu_parts(before)
        hidden = hidden.astype(bf16)
        hidden_ref[chunk] = hidden
        slopes[chunk] = slope.astype(slopes.dtype)
        part = product(hidden, square(down[chunk]))
        total = part if total is None else total + part
    branch_two = total + small_ref[4:5]
    middle, cot = middle_ref[...], cot_ref[...]
    gate_two = mod_ref[5:6]
    out_ref[...] = middle + gate_two * branch_two
    grad_two = (gate_two * cot).astype(bf16)
    grad_two_ref[...] = grad_two
    sums_ref[0:1] += column_sum(cot * branch_two)
    sums_ref[1:2] += column_sum(grad_two.astype(f32))
    total = None
    for chunk in range(chunks):
        pre = (product(grad_two, square(down[chunk]), right_turned) * slopes[chunk].astype(f32)).astype(bf16)
        pre_ref[chunk] = pre
        up_sums_ref[chunk] += column_sum(pre.astype(f32))
        part = product(pre, square(up[chunk]), right_turned)
        total = part if total is None else total + part
    unit, inverse = normalize(middle)
    sums_ref[2:3] += column_sum(total * unit)
    sums_ref[3:4] += column_sum(total)
    middle_grad = cot + normalize_back(total, unit, inverse, mod_ref[4:5])
    middle_grad_ref[...] = middle_grad
    sums_ref[4:5] += column_sum(middle_grad * branch_ref[...].astype(f32))
    grad_one = (mod_ref[2:3] * middle_grad).astype(bf16)
    grad_one_ref[...] = grad_one
    sums_ref[5:6] += column_sum(grad_one.astype(f32))


def feed_call(core, places, norm, middle, cot, branch, mod, small, source):
    seq_len, width = middle.shape
    steps = 4
    rows = seq_len // steps
    block = row_block(rows, width)
    chunked = pl.BlockSpec((4, rows, width), lambda i: (0, i, 0))
    wide = jax.ShapeDtypeStruct((4, seq_len, width), bf16)
    return pl.pallas_call(
        functools.partial(feed_kernel, source=source),
        grid=(steps,),
        in_specs=[
            smem,
            smem,
            block,
            block,
            block,
            block,
            whole_block(mod),
            whole_block(small),
        ]
        + source.specs,
        out_specs=[
            block,
            chunked,
            chunked,
            block,
            block,
            block,
            pl.BlockSpec((8, width), lambda i: (0, 0)),
            pl.BlockSpec((4, 1, width), lambda i: (0, 0, 0)),
        ],
        out_shape=[
            jax.ShapeDtypeStruct((seq_len, width), f32),
            wide,
            wide,
            jax.ShapeDtypeStruct((seq_len, width), bf16),
            jax.ShapeDtypeStruct((seq_len, width), f32),
            jax.ShapeDtypeStruct((seq_len, width), bf16),
            jax.ShapeDtypeStruct((8, width), f32),
            jax.ShapeDtypeStruct((4, 1, width), f32),
        ],
        scratch_shapes=[
            pltpu.VMEM((4, 8, width // 8, width), bf16),
            pltpu.VMEM((4, 8, width // 8, width), bf16),
            pltpu.VMEM((4, rows, width), f32),
            pltpu.SemaphoreType.DMA((2, 4)),
        ],
        compiler_params=params(),
        cost_estimate=cost(32 * seq_len * width * width, 60 * seq_len * width, 4 * seq_len * width),
    )(core, places, norm, middle, cot, branch, mod, small, *source.arrays)


def feed_weight_kernel(first_ref, left_ref, right_ref, *rest):
    out_ref = rest[-1]
    left = left_ref[0] if left_ref.ndim == 3 else left_ref[...]
    right = right_ref[0] if right_ref.ndim == 3 else right_ref[...]
    result = product(left, right, left_turned).reshape(out_ref.shape)
    if len(rest) > 1:
        result = result + rest[0][...].astype(f32)
    out_ref[...] = result.astype(bf16)


def feed_weight_call(first, left, right, got=None, base=None, row=0, rows=2):
    width = left.shape[-1]
    seq_len = left.shape[-2]
    out_block = (8, width // 8, width)

    def spec(array):
        if array.ndim == 2:
            return pl.BlockSpec(array.shape, lambda i, f: (0, 0))
        return pl.BlockSpec((1, seq_len, width), lambda i, f: (f[0] + i, 0, 0))

    more, specs, aliases = [], [], {}
    if got is not None:
        more, specs = [got], [pl.BlockSpec(out_block, lambda i, f: (0, i, 0))]
    if base is not None:
        aliases = {3 + len(more): 0}
        more, specs = more + [base], specs + [anywhere]
    return pl.pallas_call(
        feed_weight_kernel,
        grid_spec=pltpu.PrefetchScalarGridSpec(
            num_scalar_prefetch=1,
            grid=(2,),
            in_specs=[spec(left), spec(right)] + specs,
            out_specs=pl.BlockSpec(out_block, lambda i, f: (0, row + i, 0)),
        ),
        out_shape=jax.ShapeDtypeStruct((8, rows * width // 8, width), bf16),
        input_output_aliases=aliases,
        compiler_params=params(),
        cost_estimate=cost(4 * seq_len * width * width, 8 * seq_len * width + 4 * width * width),
    )(first, left, right, *more)


def attention_weight_kernel(owner_ref, norm_ref, joined_ref, grad_ref, *rest):
    head_refs = [rest[block * groups : (block + 1) * groups] for block in range(3)]
    out_ref, left, heads, right, sems = rest[3 * groups :]
    step = pl.program_id(0)

    def copies(block, slot):
        if block == 3:
            return [(joined_ref, left.at[slot]), (grad_ref, right.at[slot])]
        return [(norm_ref, left.at[slot])] + [
            (ref, heads.at[slot, pl.ds(first, count)])
            for (first, count), ref in zip(back_groups, head_refs[block])
        ]

    @pl.when(step == 0)
    def _():
        for block in range(4):

            @pl.when(owner_ref[0] == block // 2)
            def _():
                for source, target in copies(block, block % 2):
                    pltpu.make_async_copy(source, target, sems.at[block % 2]).start()

    for block in range(4):

        @pl.when((owner_ref[0] == block // 2) & (step == block % 2))
        def _():
            slot = block % 2
            wait_block(left.at[slot], sems.at[slot])
            if block == 3:
                wait_block(right.at[slot], sems.at[slot])
            else:
                wait_block(heads.at[slot], sems.at[slot])
                right[slot] = jnp.concatenate(
                    [heads[slot, head][:, :HD] for head in range(H)], axis=1
                )

    result = product(left[step], right[step], left_turned)
    out_ref[...] = result.astype(bf16).reshape(out_ref.shape)


def attention_weight_call(owner, norm, joined, grad_one, grads):
    seq_len, width = norm.shape
    return pl.pallas_call(
        attention_weight_kernel,
        grid=(2,),
        in_specs=[smem] + [anywhere] * (3 + 3 * groups),
        out_specs=pl.BlockSpec((8, width // 8, width), lambda i: (0, i, 0)),
        out_shape=jax.ShapeDtypeStruct((8, width // 4, width), bf16),
        scratch_shapes=[
            pltpu.VMEM((2, seq_len, width), bf16),
            pltpu.VMEM((2, H, seq_len, LANES), bf16),
            pltpu.VMEM((2, seq_len, width), bf16),
            pltpu.SemaphoreType.DMA((2,)),
        ],
        compiler_params=params(),
        cost_estimate=cost(4 * seq_len * width * width, 10 * seq_len * width + 4 * width * width),
    )(owner, norm, joined, grad_one, *grads)


def mix_grad_kernel(core_ref, places_ref, grad_ref, *rest, chunks):
    refs, (out_ref, weight, sem) = rest[: len(chunks.arrays)], rest[len(chunks.arrays) :]

    @pl.when(pl.program_id(0) == 0)
    def _():
        chunks.load_block(refs, places_ref, core_ref, 3, weight, sem)
        wait_block(weight, sem)

    def store(head, value):
        out_ref[head] = value

    split_heads(product(grad_ref[...], square(weight[...]), right_turned).astype(bf16), store)


def mix_grad_call(core, places, grad_one, chunks):
    seq_len, width = grad_one.shape
    rows = seq_len // 4
    return pl.pallas_call(
        functools.partial(mix_grad_kernel, chunks=chunks),
        grid=(4,),
        in_specs=[smem, smem, row_block(rows, width)] + chunks.specs,
        out_specs=pl.BlockSpec((H, rows, LANES), lambda i: (0, i, 0)),
        out_shape=jax.ShapeDtypeStruct((H, seq_len, LANES), bf16),
        scratch_shapes=[pltpu.VMEM((8, width // 8, width), bf16), pltpu.SemaphoreType.DMA],
        compiler_params=params(),
        cost_estimate=cost(2 * seq_len * width * width, 8 * seq_len * width),
    )(core, places, grad_one, *chunks.arrays)


def start_back_kernel(
    core_ref, places_ref, count_ref, index_row_ref, index_ref, middle_grad_ref, start_ref, mod_ref,
    *rest, chunks, first
):
    grad_refs = [rest[block * groups : (block + 1) * groups] for block in range(3)]
    rest = rest[3 * groups :]
    refs, rest = rest[: len(chunks.arrays)], rest[len(chunks.arrays) :]
    row_grad_ref, slot_ref, sums_ref, weight, sems = rest[-5:]
    earlier = rest[:-5]
    rows, width = start_ref.shape
    toks, per_tok = slot_ref.shape[0], index_ref.shape[0] // slot_ref.shape[0]
    slot_count = index_ref.shape[0]

    for block in range(3):
        chunks.load_block(refs, places_ref, core_ref, block, weight.at[block], sems.at[block])
    sums = {}
    total = None
    for block, refs in enumerate(grad_refs):
        joined = join_heads(refs)
        if block != 1:
            sums[block // 2] = column_sum(joined.astype(f32))
        wait_block(weight.at[block], sems.at[block])
        part = product(joined, square(weight[block]), right_turned)
        total = part if total is None else total + part
    unit, inverse = normalize(start_ref[...])
    sums[2] = column_sum(total * unit)
    sums[3] = column_sum(total)
    row_grad = middle_grad_ref[...] + normalize_back(total, unit, inverse, mod_ref[1:2])
    row_low = row_grad.astype(bf16)
    row_grad_ref[...] = row_low
    base = first * rows
    place = lax.broadcasted_iota(jnp.int32, (slot_count, rows), 1) + base
    slot = lax.broadcasted_iota(jnp.int32, (slot_count, rows), 0)
    chosen = jnp.where((index_ref[...] == place) & (slot < count_ref[0]), 1.0, 0.0)
    part = product(chosen.astype(bf16), row_low)

    part = part.astype(bf16).reshape(toks, per_tok, width)
    if earlier:
        part = part + earlier[0][:, :per_tok]
    slot_ref[:, :per_tok] = part
    here = lax.broadcasted_iota(jnp.int32, (rows, slot_count), 0) + base
    lane = lax.broadcasted_iota(jnp.int32, (rows, slot_count), 1)
    taken = jnp.where((index_row_ref[...] == here) & (lane < count_ref[0]), 1.0, 0.0)
    empty = 1.0 - jnp.sum(taken, axis=1, keepdims=True)
    sums[4] = column_sum(row_grad * empty)
    sums_ref[...] = jnp.concatenate(
        [sums[number] for number in range(5)] + [jnp.zeros((3, width), f32)]
    )


def start_back_call(quarter, earlier, core, places, count, index, grads, middle_grad, start, mod, chunks):
    seq_len, width = start.shape
    slot_count = index.shape[1]
    toks = lax.axis_size("tok")
    rows = seq_len // 4
    heads = [
        pl.BlockSpec((array.shape[0], rows, LANES), lambda i: (0, quarter, 0)) for array in grads
    ]
    block = pl.BlockSpec((rows, width), lambda i: (quarter, 0))
    kept = [] if earlier is None else [earlier]
    column = index.reshape(slot_count, 1)
    return pl.pallas_call(
        functools.partial(start_back_kernel, chunks=chunks, first=quarter),
        grid=(1,),
        in_specs=[
            smem,
            smem,
            smem,
            whole_block(index),
            whole_block(column),
            block,
            block,
            whole_block(mod),
        ]
        + heads
        + chunks.specs
        + [whole_block(array) for array in kept],
        out_specs=[
            row_block(rows, width),
            pl.BlockSpec((toks, slot_count // toks + 8, width), lambda i: (0, 0, 0)),
            pl.BlockSpec((8, width), lambda i: (0, 0)),
        ],
        out_shape=[
            jax.ShapeDtypeStruct((rows, width), bf16),
            jax.ShapeDtypeStruct((toks, slot_count // toks + 8, width), bf16),
            jax.ShapeDtypeStruct((8, width), f32),
        ],
        scratch_shapes=[
            pltpu.VMEM((3, 8, width // 8, width), bf16),
            pltpu.SemaphoreType.DMA((3,)),
        ],
        compiler_params=params(),
        cost_estimate=cost(2 * seq_len * width * width, 7 * seq_len * width),
    )(core, places, count, index, column, middle_grad, start, mod, *grads, *chunks.arrays, *kept)


def collect_kernel(feed_ref, up_ref, *rest):
    *start_refs, _, mod_ref, small_ref = rest
    start = start_refs[0][...]
    for ref in start_refs[1:]:
        start = start + ref[...]
    feed = feed_ref[...]
    row = lambda values, number: values[number : number + 1]
    blank = jnp.zeros((7, start.shape[1]), f32)
    width = start.shape[1]
    rows = [row(start, 3), row(start, 2), row(feed, 4), row(feed, 3), row(feed, 2), row(feed, 0)]
    share = 6 * width // mod_ref.shape[0]
    for tok in range(mod_ref.shape[0]):
        place, left, pieces = tok * share, share, []
        while left:
            within = place % width
            count = min(left, width - within)
            pieces.append(rows[place // width][:, within : within + count])
            place, left = place + count, left - count
        pieces.append(jnp.zeros((1, width - share), f32))
        line = jnp.concatenate(pieces, axis=1)
        mod_ref[tok] = jnp.broadcast_to(line, (8, width)).astype(bf16)
    small_ref[...] = jnp.concatenate(
        [row(start, 4), row(start, 0), row(start, 1), row(feed, 5), row(feed, 1)]
        + [up_ref[block] for block in range(4)]
        + [blank]
    ).astype(bf16)


def collect_call(feed, up, slots, *starts):
    toks, rows, width = slots.shape
    return pl.pallas_call(
        collect_kernel,
        grid=(1,),
        in_specs=[whole_block(feed), whole_block(up)]
        + [whole_block(start) for start in starts]
        + [anywhere],
        out_specs=[
            pl.BlockSpec((toks, 8, width), lambda i: (0, rows // 8 - 1, 0)),
            pl.BlockSpec((16, width), lambda i: (0, 0)),
        ],
        out_shape=[
            jax.ShapeDtypeStruct(slots.shape, bf16),
            jax.ShapeDtypeStruct((16, width), bf16),
        ],
        input_output_aliases={2 + len(starts): 0},
        compiler_params=params(),
    )(feed, up, *starts, slots)


def swap_pairs(size, bit):
    return [(place, place ^ bit) for place in range(size)]


def swap_core(values):
    return lax.ppermute(values, "grp", swap_pairs(lax.axis_size("grp"), 1))


def add_low(*parts):
    total = parts[0].astype(f32)
    for part in parts[1:]:
        total = total + part.astype(f32)
    return total.astype(bf16)


def swap_x(values):
    return lax.ppermute(values, "grp", swap_pairs(lax.axis_size("grp"), 2))


class Ring:
    def __init__(self):
        size = lax.axis_size("tok")
        self.size = size
        order = list(range(0, size, 2)) + list(range(1, size, 2))[::-1]
        self.ahead = [(order[i], order[(i + 1) % size]) for i in range(size)]
        self.behind = [(after, before) for before, after in self.ahead]
        tok = lax.axis_index("tok")
        self.place = jnp.where(tok % 2 == 0, tok // 2, size - 1 - tok // 2)
        self.x_bit = (lax.axis_index("grp") // 2) % 2

    def tok_at(self, distance):
        place = (self.place + distance) % self.size
        return jnp.where(place < self.size // 2, 2 * place, 2 * (self.size - 1 - place) + 1)

    def forward(self, values):
        return lax.ppermute(values, "tok", self.ahead)

    def backward(self, values):
        return lax.ppermute(values, "tok", self.behind)


def sync(*values):
    return lax.optimization_barrier(values)


class Gather:
    def __init__(self, ring, mine, other, part, middle, early=False):
        self.ring, self.part, self.middle, self.early = ring, part, middle, early
        self.mine, self.other = [(mine[None], "all", [0])], [(other[None], "all", [0])]
        payload = lax.dynamic_slice_in_dim(mine, part * ring.x_bit, part + middle, 0)
        self.pieces = [payload, payload]
        self.distance = 0
        self.own = None
        self.making, self.ready = [], []

    def issue(self):
        ring, flight = self.ring, {}
        middle, half = self.middle, ring.size // 2
        if self.distance == half:
            self.ready, self.making = self.ready + self.making, []
        flight["pair"] = [entry[0] for entry in self.making]
        self.made = [entry[1:] for entry in self.making]
        self.making = []
        flight["core"] = [swap_core(entry[0]) for entry in self.ready]
        self.sent = [entry[1:] for entry in self.ready]
        self.ready = []
        if self.distance < half:
            self.distance += 1
            ahead, behind = self.pieces
            if self.distance == half:
                ahead, behind = ahead[:middle], behind[middle:]
            flight["ring"] = [ring.forward(ahead), ring.backward(behind)]
        if self.own is not None:
            flight["x"] = swap_x(self.own)
        return flight

    def land(self, flight):
        bit, part, middle = self.ring.x_bit, self.part, self.middle
        self.other += [(array,) + entry for array, entry in zip(flight["core"], self.sent)]
        self.ready = [(array,) + entry for array, entry in zip(flight["pair"], self.made)]
        self.own = None
        if "x" in flight:
            got = flight["x"]
            self.mine.append((got, "got", self.places))
            if len(self.places) == 1:
                if self.early:
                    self.making = [(got, "got", self.places)]
                else:
                    pair = jnp.concatenate(self.pieces + [got[0]])[None]
                    self.making = [(pair, "pair", self.places)]
            else:
                pair = jnp.concatenate([jnp.stack(self.pieces), got], axis=1)
                self.making = [(pair, "pair", self.places)]
        if "ring" in flight:
            ahead, behind = self.pieces = flight["ring"]
            place = 2 * self.distance - 1
            if self.distance == self.ring.size // 2:
                self.places = [place]
                self.mine += [(ahead[None], "first", [place]), (behind[None], "second", [place])]
                if self.early:
                    self.ready.append((jnp.concatenate([ahead, behind])[None], "piece", [place]))
                self.own = jnp.where(bit == 0, ahead[:part], behind)[None]
            else:
                self.places = [place, place + 1]
                self.mine += [(ahead[None], "piece", [place]), (behind[None], "piece", [place + 1])]
                self.own = jnp.stack(
                    [
                        lax.dynamic_slice_in_dim(piece, middle * bit, part, 0)
                        for piece in self.pieces
                    ]
                )

    def chunks(self, stride=0):
        return Chunks(self.mine, self.other, self.part, self.middle, stride)

    def rows(self, first, count):
        bit, part, middle = self.ring.x_bit, self.part, self.middle
        low = first - part
        ahead, behind = self.pieces
        parts = [self.mine[0][0][0, first : first + count]]
        for array, kind, _ in self.mine:
            if kind == "piece":
                parts.append(lax.dynamic_slice_in_dim(array[0], first - part * bit, count, 0))
        parts.append(jnp.where(bit == 0, behind[first - middle :][:count], ahead[low:][:count]))
        return jnp.stack(parts)


class Scatter:
    def __init__(self, ring, *values):
        self.ring, self.values = ring, values
        self.distance = ring.size // 2
        self.split = values[0].shape[1] // 2

    def piece(self, place, row, count):
        tok, width = self.ring.tok_at(place), self.values[0].shape[2]
        return sum(
            lax.dynamic_slice(values, (tok, row, 0), (1, count, width))[0].astype(f32)
            for values in self.values
        )

    def hop(self):
        ring, distance, split = self.ring, self.distance, self.split
        rows = self.values[0].shape[1]
        if distance == ring.size // 2:
            ahead = self.piece(distance, 0, split)
            behind = self.piece(distance, split, rows - split)
        else:
            ahead, behind = self.ahead.astype(f32), self.behind.astype(f32)
            if distance == ring.size // 2 - 1:
                ahead = jnp.pad(ahead, ((0, rows - split), (0, 0)))
                behind = jnp.pad(behind, ((split, 0), (0, 0)))
            ahead = self.piece(distance, 0, rows) + ahead
            behind = self.piece(-distance, 0, rows) + behind
        self.distance -= 1
        return ring.forward(ahead.astype(bf16)), ring.backward(behind.astype(bf16))

    def land(self, flight):
        self.ahead, self.behind = flight

    def total(self):
        rows = self.values[0].shape[1]
        total = self.piece(0, 0, rows) + self.ahead.astype(f32) + self.behind.astype(f32)
        return total.astype(bf16)


class CrossScatter:
    def __init__(self, ring, part, middle, *values):
        self.ring, self.values, self.part, self.middle = ring, values, part, middle
        self.half = self.distance = ring.size // 2
        self.split = (part + middle) // 2
        self.extras = {}

    def chip(self, place, row, count):
        tok, width = self.ring.tok_at(place), self.values[0].shape[2]
        return sum(
            lax.dynamic_slice(values, (tok, row, 0), (1, count, width))[0].astype(f32)
            for values in self.values
        )

    def cross(self, *distances):
        row = (self.part + self.middle) * (1 - self.ring.x_bit)
        places = [place for d in distances for place in ((d,) if d in (0, self.half) else (d, -d))]
        sent = jnp.stack([self.chip(place, row, self.part).astype(bf16) for place in places])
        return places, swap_x(sent)

    def land_cross(self, places, got):
        for number, place in enumerate(places):
            self.extras[place] = got[number]

    def piece(self, place):
        part, bit = self.part, self.ring.x_bit
        extra = self.extras[place].astype(f32)
        blank = jnp.zeros((self.middle, extra.shape[1]), f32)
        return self.chip(place, part * bit, part + self.middle) + jnp.where(
            bit == 0, jnp.concatenate([extra, blank]), jnp.concatenate([blank, extra])
        )

    def hop(self):
        ring, distance, split = self.ring, self.distance, self.split
        if distance == self.half:
            farthest = self.piece(distance)
            ahead, behind = farthest[:split], farthest[split:]
        else:
            ahead, behind = self.ahead.astype(f32), self.behind.astype(f32)
            if distance == self.half - 1:
                rows = self.part + self.middle
                ahead = jnp.pad(ahead, ((0, rows - split), (0, 0)))
                behind = jnp.pad(behind, ((split, 0), (0, 0)))
            ahead = self.piece(distance) + ahead
            behind = self.piece(-distance) + behind
        self.distance -= 1
        return ring.forward(ahead.astype(bf16)), ring.backward(behind.astype(bf16))

    def land(self, flight):
        self.ahead, self.behind = flight

    def total(self):
        total = self.piece(0) + self.ahead.astype(f32) + self.behind.astype(f32)
        return total.astype(bf16)

    def join(self, total, far):
        part, bit = self.part, self.ring.x_bit
        low, high = jnp.where(bit == 0, total, far), jnp.where(bit == 0, far, total)
        return jnp.concatenate(
            [low[:part], add_low(low[part:], high[: self.middle]), high[self.middle :]]
        )


def gather_plain(shard, share):
    size, width = lax.axis_size("tok"), shard.shape[1]
    full = lax.all_gather(shard, "tok", axis=0)
    blocks = [
        full[:, row : row + share].reshape(8, -1, width) for row in range(0, shard.shape[0], share)
    ]
    return jnp.concatenate(blocks, axis=1)


def by_tok(values, share):
    size = lax.axis_size("tok")
    if size == 8:
        return values
    rows = share * size // 8
    blocks = [
        values[:, row : row + rows].reshape(size, share, -1)
        for row in range(0, values.shape[1], rows)
    ]
    return jnp.concatenate(blocks, axis=1)


def scatter_plain(chip):
    return lax.psum_scatter(chip, "tok", scatter_dimension=0, tiled=True)[0]


def gather_grp(values):
    step = 1
    while step < lax.axis_size("grp"):
        got = lax.ppermute(values, "grp", swap_pairs(lax.axis_size("grp"), step))
        values = jnp.concatenate([values, got])
        step *= 2
    return values


def add_x(shard):
    step = 2
    while step < lax.axis_size("grp"):
        shard = add_low(shard, lax.ppermute(shard, "grp", swap_pairs(lax.axis_size("grp"), step)))
        step *= 2
    return shard


def spread_kernel(weight_ref, out_ref, *, count):
    share = weight_ref.shape[0]
    for block in range(4):
        pieces = [
            weight_ref[:, (4 * tok + block) * share : (4 * tok + block + 1) * share]
            for tok in range(count)
        ]
        out_ref[block] = jnp.concatenate(pieces, axis=1).astype(bf16)


def spread_call(weight, count):
    share = weight.shape[0]
    return pl.pallas_call(
        functools.partial(spread_kernel, count=count),
        out_shape=jax.ShapeDtypeStruct((4, share, weight.shape[1] // 4), bf16),
        compiler_params=params(),
    )(weight)


def unspread_kernel(core_ref, mine_ref, other_ref, out_ref, *, count):
    share = mine_ref.shape[1]

    def write(refs):
        pieces = [
            refs[block // 2][block % 2, :, tok * share : (tok + 1) * share].astype(f32)
            for tok in range(count)
            for block in range(4)
        ]
        out_ref[...] = jnp.concatenate(pieces, axis=1)

    @pl.when(core_ref[0] == 0)
    def _():
        write((mine_ref, other_ref))

    @pl.when(core_ref[0] != 0)
    def _():
        write((other_ref, mine_ref))


def unspread_call(core, mine, other, count):
    share, width = mine.shape[1:]
    return pl.pallas_call(
        functools.partial(unspread_kernel, count=count),
        in_specs=[smem, whole_block(mine), whole_block(other)],
        out_shape=jax.ShapeDtypeStruct((share, 4 * width), f32),
        compiler_params=params(),
    )(core, mine, other)


def on_device(
    kept_tokens,
    kept_index,
    kept_count,
    condition,
    mask_token,
    position_table,
    modulation_weight,
    modulation_bias,
    input_weight,
    query_bias,
    value_bias,
    output_weight,
    output_bias,
    up_weight,
    up_bias,
    down_weight,
    down_bias,
    cotangent,
):
    _, seq_len, width = cotangent.shape
    tok_count = lax.axis_size("tok")
    core = lax.axis_index("grp") % 2
    share = input_weight.shape[0]
    position_rows = position_table.shape[0]

    def by_core(first, second):
        return jnp.where(core == 0, first, second)

    def by_core_pair(pairs):
        return [by_core(first, second) for first, second in zip(*pairs)]

    def exchange(values):
        return lax.all_to_all(values, "tok", split_axis=0, concat_axis=0, tiled=True)

    ring = Ring()

    core_row = jnp.stack([core, ring.x_bit])
    condition_low = jax.nn.silu(condition).astype(bf16)
    slots_here = kept_tokens.shape[1]
    small_here = jnp.concatenate(
        [
            jnp.stack([mask_token, query_bias, value_bias, output_bias, down_bias]),
            up_bias.reshape(4, share),
        ]
    ).astype(bf16)
    extra = lax.dynamic_update_slice(
        jnp.zeros((16, width), bf16), small_here, (0, share * lax.axis_index("tok"))
    )
    extra = jnp.concatenate([extra[:9], condition_low, extra[10:]])
    arrived = exchange(
        jnp.concatenate(
            [kept_tokens.astype(bf16), jnp.broadcast_to(extra, (tok_count, 16, width))], axis=1
        )
    )
    condition_group = arrived[:, slots_here + 9]
    small = jnp.sum(arrived[:, slots_here:].astype(f32), axis=0)

    def modulate_all(conditions, weight):
        modulation_part = jnp.dot(
            conditions, weight, preferred_element_type=f32
        ) + modulation_bias.astype(bf16).astype(f32)
        return exchange(modulation_part).reshape(6, width)

    condition_all = gather_grp(condition_group)

    ringed = share % 16 == 0 and lax.axis_size("grp") == 4
    table_rows = position_rows // 2

    input_low = input_weight.astype(bf16)
    input_blocks = [input_low[:, number * width : (number + 1) * width] for number in range(3)]
    position_low = position_table.astype(bf16)
    attention_pairs = input_blocks[:2], [input_blocks[2], output_weight.astype(bf16)]
    attention_low = tuple(
        jnp.concatenate([pair[0], position_low[half * table_rows : (half + 1) * table_rows], pair[1]])
        for half, pair in enumerate(attention_pairs)
    )
    attention_cut, feed_cut = (7 * share // 9, 8 * share // 9), (4 * share // 3, 4 * share // 3)
    if ringed:
        mine, other = by_core(*attention_low), by_core(*attention_low[::-1])
        gather = Gather(ring, mine, other, *attention_cut)
        flight, up_weight, down_weight, modulation_weight = sync(
            gather.issue(), up_weight, down_weight, modulation_weight
        )
        gather.land(flight)
        (flight,) = sync(gather.issue())
        gather.land(flight)
    modulation_low = modulation_weight.astype(bf16)
    up_low = spread_call(up_weight, tok_count)
    down_low = down_weight.astype(bf16).reshape(4, share, width)
    feed_low = tuple(
        jnp.concatenate([up_low[half : half + 2], down_low[half : half + 2]]).reshape(-1, width)
        for half in (0, 2)
    )
    if ringed:
        mine, other = by_core(*feed_low), by_core(*feed_low[::-1])
        flight, condition_group, arrived, small, mine, other, modulation_low = sync(
            gather.issue(), condition_group, arrived, small, mine, other, modulation_low
        )
        gather.land(flight)
        feed_gather = Gather(ring, mine, other, *feed_cut, early=True)
        flight, condition_group = sync(gather.issue(), condition_group)
        gather.land(flight)
    mod = modulate_all(condition_group, modulation_low)
    if ringed:
        table_mine = gather.rows(share, table_rows)
        feed_flight = feed_gather.issue()
        flight, table_mine, table_other, mod = sync(
            gather.issue(), table_mine, swap_core(table_mine), mod
        )
        gather.land(flight)
        flight = gather.issue()
        distances = [0]
        for distance in range(1, ring.size // 2):
            distances += [-distance, distance]
        places = ring.tok_at(jnp.array(distances + [ring.size // 2], jnp.int32))
    else:
        places = jnp.arange(8, dtype=jnp.int32)
        mine = gather_plain(jnp.concatenate(by_core_pair(attention_pairs)), share)
        everywhere = list(range(8))
        plain_chunks = lambda mine: Chunks(
            [(mine, "all", everywhere)], [(swap_core(mine), "all", everywhere)]
        )
        attention_chunks = plain_chunks(mine)
        feed_chunks = plain_chunks(gather_plain(by_core(*feed_low), share))
        table = lax.all_gather(position_low, "tok").reshape(8, -1, width)

        halves = jnp.split(table, 2, axis=1)
        table_mine, table_other = by_core(*halves), by_core(*halves[::-1])
    table_chunks = Chunks(
        [(table_mine, "all", list(range(8)))], [(table_other, "all", list(range(8)))]
    )
    start, norm_one = start_call(
        core_row, places, kept_count, kept_index, arrived, small, mod, table_chunks, 0,
        table_mine.shape[1], seq_len,
    )
    if ringed:
        flight, feed_flight, start, norm_one = sync(flight, feed_flight, start, norm_one)
        gather.land(flight)
        attention_chunks = gather.chunks(share + table_rows)
        feed_gather.land(feed_flight)
    projected = project_call(core_row, places, norm_one, small, attention_chunks)
    if ringed:
        flight, projected, start = sync(feed_gather.issue(), projected, start)
        feed_gather.land(flight)
    attended = None
    for first, heads in forward_groups:
        attended = attend_call(projected, first, heads, attended)
        if ringed:
            flight, attended, projected = sync(feed_gather.issue(), attended, projected)
            feed_gather.land(flight)
    joined, branch_one, middle, norm_two = mix_call(
        core_row, places, attended[0], start, small, mod, attention_chunks
    )
    if ringed:
        flight, norm_two = sync(feed_gather.issue(), norm_two)
        feed_gather.land(flight)
        (flight,) = sync(feed_gather.issue())
        feed_gather.land(flight)
        feed_chunks = feed_gather.chunks()
    (
        block_output,
        hidden,
        pre_grad,
        grad_two,
        middle_grad,
        grad_one,
        feed_sums,
        up_bias_sum,
    ) = feed_call(
        core_row, places, norm_two, middle, cotangent[0], branch_one, mod, small, feed_chunks
    )
    far, near = 2 - 2 * core_row[:1], 2 * core_row[:1]
    other_up = feed_weight_call(far, norm_two, pre_grad)
    other_up, hidden, grad_one = sync(other_up, hidden, grad_one)
    other_down = feed_weight_call(far, hidden, grad_two)
    got_up, other_down, norm_two = sync(swap_core(other_up), other_down, norm_two)
    feed_chip = feed_weight_call(near, norm_two, pre_grad, got_up, rows=4)
    got_down, feed_chip, hidden = sync(swap_core(other_down), feed_chip, hidden)
    feed_chip = feed_weight_call(near, hidden, grad_two, got_down, feed_chip, 2, 4)
    feed_chip, grad_one = sync(feed_chip, grad_one)
    mix_grad = mix_grad_call(core_row, places, grad_one, attention_chunks)
    if ringed:
        feed_scatter = Scatter(ring, feed_chip)
    grads = []
    for group, (first, heads) in enumerate(back_groups):
        grads.append(attend_back_call(projected, attended, mix_grad, first, heads))
        if ringed and group < 2:
            flight, grads, mix_grad = sync(feed_scatter.hop(), grads, mix_grad)
            feed_scatter.land(flight)
    grads = [triple[block] for block in range(3) for triple in grads]

    def attention_weights(owner, norm):
        return attention_weight_call(owner, norm, joined, grad_one, grads)

    def start_back(quarter, earlier, grads):
        return start_back_call(
            quarter, earlier, core_row, places, kept_count, kept_index, grads, middle_grad, start, mod,
            attention_chunks,
        )

    attention_other = attention_weights(1 - core_row[:1], norm_one)
    if ringed:
        flight, attention_other, norm_one, grads = sync(
            feed_scatter.hop(), attention_other, norm_one, grads
        )
        feed_scatter.land(flight)
        feed_flight = feed_scatter.hop()
    attention_mine = attention_weights(core_row[:1], norm_one)
    attention_got = swap_core(attention_other)
    if ringed:
        attention_mine, attention_got, grads = sync(attention_mine, attention_got, grads)
        scatter = CrossScatter(ring, 2 * share // 3, 2 * share // 3, attention_mine, attention_got)
    quarters = []
    slot_grad = None
    for quarter in range(4):
        part = start_back(quarter, slot_grad, grads)
        if ringed:
            if quarter == 0:
                places_crossed, crossed = scatter.cross(scatter.half, scatter.half - 1)
                crossed, part, grads, feed_flight = sync(crossed, part, grads, feed_flight)
                feed_scatter.land(feed_flight)
                feed_shard = feed_scatter.total()
                feed_cross = swap_x(feed_shard)
            else:
                following = (scatter.half - 1 - quarter,)
                if quarter == 3:
                    following = tuple(range(scatter.half - 4, -1, -1))
                places_crossed, crossed = scatter.cross(*following)
                flight, crossed, part, grads = sync(scatter.hop(), crossed, part, grads)
                scatter.land(flight)
            scatter.land_cross(places_crossed, crossed)
        quarters.append(part)
        slot_grad = part[1]
    row_grad = jnp.concatenate([part[0] for part in quarters])
    slot_grad, small_grad = collect_call(
        feed_sums, up_bias_sum, slot_grad, *[part[2] for part in quarters]
    )

    position_grad = row_grad.reshape(tok_count, position_rows, width)
    halves = [
        half.reshape(-1, width)
        for half in (position_grad[:, :table_rows], position_grad[:, table_rows:])
    ]
    table_got = swap_core(jnp.concatenate([by_core(halves[1], halves[0]), small_grad]))
    arrived = exchange(slot_grad)
    table_chip = add_low(jnp.concatenate([by_core(halves[0], halves[1]), small_grad]), table_got)
    small_chip = table_chip[-16:]
    table_chip = table_chip[:-16].reshape(tok_count, table_rows, width)
    half_rows = table_rows // 2
    table_near, table_away = (
        jnp.concatenate(
            [
                lax.dynamic_slice_in_dim(table_chip, half_rows * place, half_rows, 1).reshape(-1, width),
                small_chip,
            ]
        )
        for place in (ring.x_bit, 1 - ring.x_bit)
    )
    table_got = swap_x(table_away)
    if ringed:
        while scatter.distance > 0:
            scatter.land(scatter.hop())
        attention_shard = scatter.total()
        attention_cross = swap_x(attention_shard)
    table_pair = add_low(table_near, table_got)
    table_pair, small_grad, arrived = sync(table_pair[:-16], table_pair[-16:], arrived)
    kept_low = arrived[:, :slots_here]
    modulation_grad_group = arrived[:, slots_here, : modulation_bias.shape[0]]
    condition_part = jnp.einsum(
        "ie,de->id", modulation_grad_group, modulation_low, preferred_element_type=f32
    )
    condition_high = condition_part.astype(bf16)
    condition_rest = (condition_part - condition_high.astype(f32)).astype(bf16)
    table_parts = exchange(
        jnp.concatenate(
            [
                table_pair.reshape(tok_count, half_rows, width),
                jnp.broadcast_to(small_grad[:14], (tok_count, 14, width)),
                condition_high[:, None],
                condition_rest[:, None],
            ],
            axis=1,
        )
    )
    modulation_grad_all = gather_grp(modulation_grad_group)
    modulation_total = jnp.einsum(
        "id,ie->de", condition_all, modulation_grad_all, preferred_element_type=f32
    )
    modulation_bias_total = jnp.sum(modulation_grad_all.astype(f32), axis=0)
    table_sum = jnp.sum(table_parts.astype(f32), axis=0)
    table_shard = table_sum.astype(bf16)
    condition_low_grad = table_sum[-2:-1] + table_sum[-1:]
    step = 4
    while step < lax.axis_size("grp"):
        table_shard = add_low(
            table_shard, lax.ppermute(table_shard, "grp", swap_pairs(lax.axis_size("grp"), step))
        )
        step *= 2
    table_cross = swap_x(table_shard[:half_rows])
    table_half = jnp.concatenate(
        [
            jnp.where(ring.x_bit == 0, table_shard[:half_rows], table_cross),
            jnp.where(ring.x_bit == 0, table_cross, table_shard[:half_rows]),
        ]
    )
    if ringed:
        attention_shard = scatter.join(attention_shard, attention_cross)
        feed_shard = add_low(feed_shard, feed_cross)
    else:
        attention_chip = by_tok(add_low(attention_mine, attention_got), share)
        attention_shard = add_x(scatter_plain(attention_chip))
        feed_shard = add_x(scatter_plain(by_tok(feed_chip, share)))
    table_far = swap_core(table_half)
    position_total = jnp.concatenate(
        [by_core(table_half, table_far), by_core(table_far, table_half)]
    ).astype(f32)
    small_total = lax.dynamic_slice_in_dim(
        table_shard[half_rows:], share * lax.axis_index("tok"), share, 1
    ).astype(f32)
    mask_total, query_bias_total, value_bias_total, output_bias_total, down_bias_total = (
        small_total[number] for number in range(5)
    )
    up_bias_total = small_total[5:9].reshape(-1)
    kept_grad = kept_low.astype(f32)
    far = swap_core(attention_shard)
    first, second = by_core(attention_shard, far).astype(f32), by_core(far, attention_shard).astype(f32)
    input_total = jnp.concatenate([first[:share], first[share:], second[:share]], axis=1)
    output_total = second[share:]
    feed_shard = feed_shard.reshape(4, share, width)
    feed_far = swap_core(feed_shard)
    up_total = unspread_call(core_row, feed_shard[:2], feed_far[:2], tok_count)
    down_total = jnp.concatenate(
        [by_core(feed_shard[2:], feed_far[2:]), by_core(feed_far[2:], feed_shard[2:])]
    ).reshape(-1, width).astype(f32)

    _, silu_back = jax.vjp(jax.nn.silu, condition)
    condition_grad = silu_back(condition_low_grad)[0]
    return (
        block_output[None],
        kept_grad,
        condition_grad,
        mask_total,
        position_total,
        modulation_total,
        modulation_bias_total,
        input_total,
        query_bias_total,
        value_bias_total,
        output_total,
        output_bias_total,
        up_total,
        up_bias_total,
        down_total,
        down_bias_total,
    )


def solution(mesh):
    return jax.shard_map(
        on_device,
        mesh=mesh,
        in_specs=(
            P("grp", "tok", None),
            P(("grp", "tok"), None),
            P(("grp", "tok")),
            P(("grp", "tok"), None),
            P("tok"),
            P("tok", None),
            P(None, "tok"),
            P("tok"),
            P("tok", None),
            P("tok"),
            P("tok"),
            P("tok", None),
            P("tok"),
            P("tok", None),
            P("tok"),
            P("tok", None),
            P("tok"),
            P(("grp", "tok"), None, None),
        ),
        out_specs=(
            P(("grp", "tok"), None, None),
            P("grp", "tok", None),
            P(("grp", "tok"), None),
            P("tok"),
            P("tok", None),
            P(None, "tok"),
            P("tok"),
            P("tok", None),
            P("tok"),
            P("tok"),
            P("tok", None),
            P("tok"),
            P("tok", None),
            P("tok"),
            P("tok", None),
            P("tok"),
        ),
        check_vma=False,
    )
```

```python
import functools
import math

import jax
import jax.numpy as jnp
from jax import lax
from jax.experimental import pallas as pl
from jax.experimental.pallas import tpu as pltpu
from jax.sharding import PartitionSpec as P

H = 16
HD = 72
LANES = 128

epsilon = 1e-06
f32 = jnp.float32
bf16 = jnp.bfloat16
plain = (((1,), (0,)), ((), ()))
right_turned = (((1,), (1,)), ((), ()))
left_turned = (((0,), (0,)), ((), ()))
vmem_limit = 60 << 20


def product(left, right, dims=plain):
    return lax.dot_general(left, right, dims, preferred_element_type=f32)


def whole_block(array):
    zeros = (0,) * array.ndim
    return pl.BlockSpec(array.shape, lambda *_: zeros)


def row_block(rows, *rest):
    return pl.BlockSpec((rows,) + rest, lambda i: (i,) + (0,) * len(rest))


smem = pl.BlockSpec(memory_space=pltpu.SMEM)
anywhere = pl.BlockSpec(memory_space=pl.ANY)


def params():
    return pltpu.CompilerParams(vmem_limit_bytes=vmem_limit)


def cost(flops, moved, exps=0):
    return pl.CostEstimate(flops=int(flops), bytes_accessed=int(moved), transcendentals=int(exps))


def column_sum(values):
    return jnp.sum(values, axis=0, keepdims=True)


def normalize(values):
    center = values - jnp.mean(values, axis=-1, keepdims=True)
    spread = jnp.mean(center * center, axis=-1, keepdims=True)
    inverse = lax.rsqrt(spread + epsilon)
    return center * inverse, inverse


def normalize_back(grad, unit, inverse, scale):
    scaled = grad * (1.0 + scale)
    first = jnp.mean(scaled, axis=-1, keepdims=True)
    second = jnp.mean(scaled * unit, axis=-1, keepdims=True)
    return (scaled - first - unit * second) * inverse


def start_kernel(core_ref, places_ref, count_ref, index_ref, kept_ref, small_ref, mod_ref, *rest, chunks, row, share):
    refs, (start_ref, norm_ref, table, sems) = rest[: len(chunks.arrays)], rest[len(chunks.arrays) :]
    rows, slots = start_ref.shape[0], index_ref.shape[1]
    step = pl.program_id(0)
    low, high = table.at[:, :share], table.at[:, share:]

    @pl.when(step == 0)
    def _():
        @pl.when(core_ref[0] == 0)
        def _():
            chunks.load(refs, places_ref, core_ref, True, row, low, sems.at[0])
            chunks.load(refs, places_ref, core_ref, False, row, high, sems.at[1])

        @pl.when(core_ref[0] != 0)
        def _():
            chunks.load(refs, places_ref, core_ref, False, row, low, sems.at[0])
            chunks.load(refs, places_ref, core_ref, True, row, high, sems.at[1])

        wait_block(low, sems.at[0])
        wait_block(high, sems.at[1])

    base = step * rows
    here = lax.broadcasted_iota(jnp.int32, (rows, slots), 0) + base
    slot = lax.broadcasted_iota(jnp.int32, (rows, slots), 1)
    chosen = jnp.where((index_ref[...] == here) & (slot < count_ref[0]), 1.0, 0.0)
    kept = kept_ref[:, : slots // kept_ref.shape[0]].reshape(slots, -1)
    filled = product(chosen.astype(bf16), kept)
    empty = 1.0 - jnp.sum(chosen, axis=1, keepdims=True)
    groups_here = rows // table.shape[1]
    position = table[pl.ds(step * groups_here, groups_here)].reshape(rows, -1)
    start = filled + empty * small_ref[0:1] + position.astype(f32)
    start_ref[...] = start
    unit, _ = normalize(start)
    norm_ref[...] = (unit * (1.0 + mod_ref[1:2]) + mod_ref[0:1]).astype(bf16)


def start_call(core, places, count, index, kept, small, mod, chunks, row, share, seq_len):
    width = kept.shape[2]
    rows = seq_len // 4
    return pl.pallas_call(
        functools.partial(start_kernel, chunks=chunks, row=row, share=share),
        grid=(4,),
        in_specs=[
            smem,
            smem,
            smem,
            whole_block(index),
            whole_block(kept),
            whole_block(small),
            whole_block(mod),
        ]
        + chunks.specs,
        out_specs=[row_block(rows, width)] * 2,
        out_shape=[
            jax.ShapeDtypeStruct((seq_len, width), f32),
            jax.ShapeDtypeStruct((seq_len, width), bf16),
        ],
        scratch_shapes=[
            pltpu.VMEM((8, seq_len // 8, width), bf16),
            pltpu.SemaphoreType.DMA((2,)),
        ],
        compiler_params=params(),
        cost_estimate=cost(2 * seq_len * width * index.shape[1], 14 * seq_len * width),
    )(core, places, count, index, kept, small, mod, *chunks.arrays)


class Chunks:
    def __init__(self, mine, other, part=0, middle=0, stride=0):
        self.sources = list(mine), list(other)
        self.part, self.middle, self.stride = part, middle, stride
        self.arrays = [entry[0] for source in self.sources for entry in source]
        self.specs = [anywhere] * len(self.arrays)

    def span(self, kind, bit):
        part, middle = self.part, self.middle
        start = part * bit
        return {
            "piece": (start, start + part + middle),
            "first": (start, start + middle),
            "second": (start + middle, start + part + middle),
            "got": ((0, part) if bit else (part + middle, 2 * part + middle)),
            "all": (0, 1 << 20),
        }[kind]

    def spans(self, kind, bit):
        if kind == "pair":
            return [self.span("piece", bit) + (0,), self.span("got", bit) + (self.part + self.middle,)]
        return [self.span(kind, bit) + (0,)]

    def load(self, refs, places_ref, spot_ref, from_mine, row, target, sem):
        source = self.sources[0 if from_mine else 1]
        refs = refs[: len(source)] if from_mine else refs[len(self.sources[0]) :]

        def start(ref, kind, places, bit):
            for low, high, base in self.spans(kind, bit):
                begin, end = max(row, low), min(row + target.shape[1], high)
                for index, place in enumerate(places if begin < end else []):
                    pltpu.make_async_copy(
                        ref.at[index, pl.ds(base + begin - low, end - begin)],
                        target.at[places_ref[place], pl.ds(begin - row, end - begin)],
                        sem,
                    ).start()

        for ref, (_, kind, places) in zip(refs, source):
            if kind == "all":
                start(ref, kind, places, 0)
        if any(kind != "all" for _, kind, _ in source):
            for bit in (0, 1):

                @pl.when(spot_ref[1] == bit)
                def _():
                    for ref, (_, kind, places) in zip(refs, source):
                        if kind != "all":
                            start(ref, kind, places, bit)

    def load_block(self, refs, places_ref, spot_ref, block, target, sem, first=0):
        rows = target.shape[1]
        owner, row = block // 2, first * rows + (block % 2) * (self.stride or rows)

        @pl.when(spot_ref[0] == owner)
        def _():
            self.load(refs, places_ref, spot_ref, True, row, target, sem)

        @pl.when(spot_ref[0] != owner)
        def _():
            self.load(refs, places_ref, spot_ref, False, row, target, sem)


def wait_block(target, sem):
    pltpu.make_async_copy(target, target, sem).wait()


def square(weight):
    return weight.reshape(-1, weight.shape[-1])


def split_heads(values, store):
    rows = values.shape[0]
    blank = jnp.zeros((rows, LANES - HD), values.dtype)
    for head in range(H):
        store(head, jnp.concatenate([values[:, head * HD : (head + 1) * HD], blank], axis=1))


def project_kernel(core_ref, places_ref, norm_ref, small_ref, *rest, chunks):
    refs, (out_ref, weight, sems) = rest[: len(chunks.arrays)], rest[len(chunks.arrays) :]
    step, part = pl.program_id(0), pl.program_id(1)

    @pl.when((step == 0) & (part == 0))
    def _():
        for block in range(3):
            chunks.load_block(refs, places_ref, core_ref, block, weight.at[block], sems.at[block])

    @pl.when(part == 0)
    def _():
        wait_block(weight.at[step], sems.at[step])

    key_free = jnp.where(step == 1, 0.0, 1.0)
    bias = jnp.where(step == 0, small_ref[1:2], small_ref[2:3]) * key_free
    result = product(norm_ref[...], square(weight[step])) + bias

    def store(head, value):
        out_ref[0, head] = value

    split_heads(result.astype(bf16), store)


def project_call(core, places, norm, small, chunks):
    seq_len, width = norm.shape
    return pl.pallas_call(
        functools.partial(project_kernel, chunks=chunks),
        grid=(3, 2),
        in_specs=[
            smem,
            smem,
            pl.BlockSpec((seq_len // 2, width), lambda i, j: (j, 0)),
            whole_block(small),
        ]
        + chunks.specs,
        out_specs=pl.BlockSpec((1, H, seq_len // 2, LANES), lambda i, j: (i, 0, j, 0)),
        out_shape=jax.ShapeDtypeStruct((3, H, seq_len, LANES), bf16),
        scratch_shapes=[
            pltpu.VMEM((3, 8, width // 8, width), bf16),
            pltpu.SemaphoreType.DMA((3,)),
        ],
        compiler_params=params(),
        cost_estimate=cost(6 * seq_len * width * width, 12 * seq_len * width + 6 * width * width),
    )(core, places, norm, small, *chunks.arrays)


heads_a_step = 2
forward_groups = ((0, 8), (8, 8))
back_groups = ((0, 2), (2, 8), (10, 6))
groups = len(back_groups)


def attend_kernel(query_ref, key_ref, value_ref, *rest, factor):
    mix_ref, log_ref = rest[-2:]
    for head in range(query_ref.shape[1]):
        scores = product(key_ref[0, head], query_ref[0, head], right_turned)
        top = jnp.max(scores, axis=0, keepdims=True)
        weights = jnp.exp2((scores - top) * factor)
        total = jnp.sum(weights, axis=0, keepdims=True)
        mix = product(value_ref[0, head].T, weights.astype(bf16))
        mix_ref[head] = (mix / total).T.astype(bf16)
        log_ref[head] = top * factor + jnp.log2(total)


def head_block(place, seq_len, first):
    first = first // heads_a_step
    return pl.BlockSpec((1, heads_a_step, seq_len, LANES), lambda h: (place, first + h, 0, 0))


def head_rows(first, *rest):
    first = first // heads_a_step
    return pl.BlockSpec((heads_a_step,) + rest, lambda h: (first + h, 0, 0))


def attend_call(projected, first, heads, earlier=None):
    seq_len = projected.shape[2]
    kept = [] if earlier is None else list(earlier)
    return pl.pallas_call(
        functools.partial(
            attend_kernel, factor=math.log2(math.e) / math.sqrt(HD)
        ),
        grid=(heads // heads_a_step,),
        in_specs=[head_block(place, seq_len, first) for place in range(3)] + [anywhere] * len(kept),
        out_specs=[
            head_rows(first, seq_len, LANES),
            head_rows(first, 1, seq_len),
        ],
        out_shape=[
            jax.ShapeDtypeStruct((H, seq_len, LANES), bf16),
            jax.ShapeDtypeStruct((H, 1, seq_len), f32),
        ],
        input_output_aliases={3: 0, 4: 1} if kept else {},
        compiler_params=params(),
        cost_estimate=cost(4 * heads * seq_len * seq_len * 256, 8 * heads * seq_len * LANES, heads * seq_len * seq_len),
    )(projected, projected, projected, *kept)


def attend_back_kernel(
    query_ref, key_ref, value_ref, mix_ref, log_ref, grad_ref, query_grad_ref, key_grad_ref,
    value_grad_ref, *, factor
):
    base_two = factor * math.log2(math.e)
    for head in range(query_ref.shape[1]):
        query, key, value = query_ref[0, head], key_ref[0, head], value_ref[0, head]
        grad = grad_ref[head]
        scores = product(key, query, right_turned)
        weights = jnp.exp2(scores * base_two - log_ref[head])
        value_grad_ref[head] = product(weights.astype(bf16), grad).astype(bf16)
        weight_grad = product(value, grad, right_turned)
        inner = column_sum((grad.astype(f32) * mix_ref[head].astype(f32)).T)
        score_grad = (weights * (weight_grad - inner)).astype(bf16)
        key_grad_ref[head] = (product(score_grad, query) * factor).astype(bf16)
        query_grad_ref[head] = (product(key.T, score_grad) * factor).T.astype(bf16)


def attend_back_call(projected, attended, grad, first, heads):
    seq_len = projected.shape[2]
    mix, logs = attended
    flat = head_rows(0, seq_len, LANES)
    return pl.pallas_call(
        functools.partial(attend_back_kernel, factor=1.0 / math.sqrt(HD)),
        grid=(heads // heads_a_step,),
        in_specs=[head_block(place, seq_len, first) for place in range(3)]
        + [
            head_rows(first, seq_len, LANES),
            head_rows(first, 1, seq_len),
            head_rows(first, seq_len, LANES),
        ],
        out_specs=[flat] * 3,
        out_shape=[jax.ShapeDtypeStruct((heads, seq_len, LANES), bf16)] * 3,
        compiler_params=params(),
        cost_estimate=cost(10 * heads * seq_len * seq_len * 256, 16 * heads * seq_len * LANES, heads * seq_len * seq_len),
    )(projected, projected, projected, mix, logs, grad)


def join_heads(refs):
    return jnp.concatenate(
        [ref[head][:, :HD] for ref in refs for head in range(ref.shape[0])], axis=1
    )


def mix_kernel(core_ref, places_ref, start_ref, small_ref, mod_ref, *rest, chunks):
    mix_refs, rest = rest[:1], rest[1:]
    refs, rest = rest[: len(chunks.arrays)], rest[len(chunks.arrays) :]
    joined_ref, branch_ref, middle_ref, norm_ref, weight, sem = rest

    @pl.when(pl.program_id(0) == 0)
    def _():
        chunks.load_block(refs, places_ref, core_ref, 3, weight, sem)
        wait_block(weight, sem)

    joined = join_heads(mix_refs)
    joined_ref[...] = joined
    branch = product(joined, square(weight[...])) + small_ref[3:4]
    branch_ref[...] = branch.astype(bf16)
    middle = start_ref[...] + mod_ref[2:3] * branch
    middle_ref[...] = middle
    unit, _ = normalize(middle)
    norm_ref[...] = (unit * (1.0 + mod_ref[4:5]) + mod_ref[3:4]).astype(bf16)


def mix_call(core, places, mix, start, small, mod, chunks):
    seq_len, width = start.shape
    rows = seq_len // 4
    block = row_block(rows, width)
    return pl.pallas_call(
        functools.partial(mix_kernel, chunks=chunks),
        grid=(4,),
        in_specs=[smem, smem, block, whole_block(small), whole_block(mod)]
        + [pl.BlockSpec((H, rows, LANES), lambda i: (0, i, 0))]
        + chunks.specs,
        out_specs=[block] * 4,
        out_shape=[
            jax.ShapeDtypeStruct((seq_len, width), kind) for kind in (bf16, bf16, f32, bf16)
        ],
        scratch_shapes=[pltpu.VMEM((8, width // 8, width), bf16), pltpu.SemaphoreType.DMA],
        compiler_params=params(),
        cost_estimate=cost(2 * seq_len * width * width, 18 * seq_len * width),
    )(core, places, start, small, mod, mix, *chunks.arrays)


def gelu_parts(values):
    inner = 0.7978845608028654 * (values + 0.044715 * values * values * values)
    turned = jnp.tanh(inner)
    half = 0.5 * (1.0 + turned)
    slope = half + 0.5 * values * (1.0 - turned * turned) * (
        0.7978845608028654 * (1.0 + 0.134145 * values * values)
    )
    return values * half, slope


def feed_kernel(
    core_ref, places_ref, norm_ref, middle_ref, cot_ref, branch_ref, mod_ref, small_ref, *rest, source
):
    refs, rest = rest[: len(source.arrays)], rest[len(source.arrays) :]
    (
        out_ref, hidden_ref, pre_ref, grad_two_ref, middle_grad_ref, grad_one_ref, sums_ref,
        up_sums_ref, up, down, slopes, sems,
    ) = rest
    step = pl.program_id(0)
    chunks = 4

    @pl.when(step == 0)
    def _():
        for chunk in range(chunks):
            for side, target in enumerate((up, down)):
                source.load_block(
                    refs, places_ref, core_ref, chunk, target.at[chunk], sems.at[side, chunk], 2 * side
                )
        sums_ref[...] = jnp.zeros_like(sums_ref)
        up_sums_ref[...] = jnp.zeros_like(up_sums_ref)

    norm = norm_ref[...]
    total = None
    for chunk in range(chunks):

        @pl.when(step == 0)
        def _():
            wait_block(up.at[chunk], sems.at[0, chunk])
            wait_block(down.at[chunk], sems.at[1, chunk])

        before = product(norm, square(up[chunk])) + small_ref[5 + chunk : 6 + chunk]
        hidden, slope = gelu_parts(before)
        hidden = hidden.astype(bf16)
        hidden_ref[chunk] = hidden
        slopes[chunk] = slope.astype(slopes.dtype)
        part = product(hidden, square(down[chunk]))
        total = part if total is None else total + part
    branch_two = total + small_ref[4:5]
    middle, cot = middle_ref[...], cot_ref[...]
    gate_two = mod_ref[5:6]
    out_ref[...] = middle + gate_two * branch_two
    grad_two = (gate_two * cot).astype(bf16)
    grad_two_ref[...] = grad_two
    sums_ref[0:1] += column_sum(cot * branch_two)
    sums_ref[1:2] += column_sum(grad_two.astype(f32))
    total = None
    for chunk in range(chunks):
        pre = (product(grad_two, square(down[chunk]), right_turned) * slopes[chunk].astype(f32)).astype(bf16)
        pre_ref[chunk] = pre
        up_sums_ref[chunk] += column_sum(pre.astype(f32))
        part = product(pre, square(up[chunk]), right_turned)
        total = part if total is None else total + part
    unit, inverse = normalize(middle)
    sums_ref[2:3] += column_sum(total * unit)
    sums_ref[3:4] += column_sum(total)
    middle_grad = cot + normalize_back(total, unit, inverse, mod_ref[4:5])
    middle_grad_ref[...] = middle_grad
    sums_ref[4:5] += column_sum(middle_grad * branch_ref[...].astype(f32))
    grad_one = (mod_ref[2:3] * middle_grad).astype(bf16)
    grad_one_ref[...] = grad_one
    sums_ref[5:6] += column_sum(grad_one.astype(f32))


def feed_call(core, places, norm, middle, cot, branch, mod, small, source):
    seq_len, width = middle.shape
    steps = 4
    rows = seq_len // steps
    block = row_block(rows, width)
    chunked = pl.BlockSpec((4, rows, width), lambda i: (0, i, 0))
    wide = jax.ShapeDtypeStruct((4, seq_len, width), bf16)
    return pl.pallas_call(
        functools.partial(feed_kernel, source=source),
        grid=(steps,),
        in_specs=[
            smem,
            smem,
            block,
            block,
            block,
            block,
            whole_block(mod),
            whole_block(small),
        ]
        + source.specs,
        out_specs=[
            block,
            chunked,
            chunked,
            block,
            block,
            block,
            pl.BlockSpec((8, width), lambda i: (0, 0)),
            pl.BlockSpec((4, 1, width), lambda i: (0, 0, 0)),
        ],
        out_shape=[
            jax.ShapeDtypeStruct((seq_len, width), f32),
            wide,
            wide,
            jax.ShapeDtypeStruct((seq_len, width), bf16),
            jax.ShapeDtypeStruct((seq_len, width), f32),
            jax.ShapeDtypeStruct((seq_len, width), bf16),
            jax.ShapeDtypeStruct((8, width), f32),
            jax.ShapeDtypeStruct((4, 1, width), f32),
        ],
        scratch_shapes=[
            pltpu.VMEM((4, 8, width // 8, width), bf16),
            pltpu.VMEM((4, 8, width // 8, width), bf16),
            pltpu.VMEM((4, rows, width), f32),
            pltpu.SemaphoreType.DMA((2, 4)),
        ],
        compiler_params=params(),
        cost_estimate=cost(32 * seq_len * width * width, 60 * seq_len * width, 4 * seq_len * width),
    )(core, places, norm, middle, cot, branch, mod, small, *source.arrays)


def feed_weight_kernel(first_ref, left_ref, right_ref, *rest):
    out_ref = rest[-1]
    left = left_ref[0] if left_ref.ndim == 3 else left_ref[...]
    right = right_ref[0] if right_ref.ndim == 3 else right_ref[...]
    result = product(left, right, left_turned).reshape(out_ref.shape)
    if len(rest) > 1:
        result = result + rest[0][...].astype(f32)
    out_ref[...] = result.astype(bf16)


def feed_weight_call(first, left, right, got=None, base=None, row=0, rows=2):
    width = left.shape[-1]
    seq_len = left.shape[-2]
    out_block = (8, width // 8, width)

    def spec(array):
        if array.ndim == 2:
            return pl.BlockSpec(array.shape, lambda i, f: (0, 0))
        return pl.BlockSpec((1, seq_len, width), lambda i, f: (f[0] + i, 0, 0))

    more, specs, aliases = [], [], {}
    if got is not None:
        more, specs = [got], [pl.BlockSpec(out_block, lambda i, f: (0, i, 0))]
    if base is not None:
        aliases = {3 + len(more): 0}
        more, specs = more + [base], specs + [anywhere]
    return pl.pallas_call(
        feed_weight_kernel,
        grid_spec=pltpu.PrefetchScalarGridSpec(
            num_scalar_prefetch=1,
            grid=(2,),
            in_specs=[spec(left), spec(right)] + specs,
            out_specs=pl.BlockSpec(out_block, lambda i, f: (0, row + i, 0)),
        ),
        out_shape=jax.ShapeDtypeStruct((8, rows * width // 8, width), bf16),
        input_output_aliases=aliases,
        compiler_params=params(),
        cost_estimate=cost(4 * seq_len * width * width, 8 * seq_len * width + 4 * width * width),
    )(first, left, right, *more)


def attention_weight_kernel(owner_ref, norm_ref, joined_ref, grad_ref, *rest):
    head_refs = [rest[block * groups : (block + 1) * groups] for block in range(3)]
    out_ref, left, heads, right, sems = rest[3 * groups :]
    step = pl.program_id(0)

    def copies(block, slot):
        if block == 3:
            return [(joined_ref, left.at[slot]), (grad_ref, right.at[slot])]
        return [(norm_ref, left.at[slot])] + [
            (ref, heads.at[slot, pl.ds(first, count)])
            for (first, count), ref in zip(back_groups, head_refs[block])
        ]

    @pl.when(step == 0)
    def _():
        for block in range(4):

            @pl.when(owner_ref[0] == block // 2)
            def _():
                for source, target in copies(block, block % 2):
                    pltpu.make_async_copy(source, target, sems.at[block % 2]).start()

    for block in range(4):

        @pl.when((owner_ref[0] == block // 2) & (step == block % 2))
        def _():
            slot = block % 2
            wait_block(left.at[slot], sems.at[slot])
            if block == 3:
                wait_block(right.at[slot], sems.at[slot])
            else:
                wait_block(heads.at[slot], sems.at[slot])
                right[slot] = jnp.concatenate(
                    [heads[slot, head][:, :HD] for head in range(H)], axis=1
                )

    result = product(left[step], right[step], left_turned)
    out_ref[...] = result.astype(bf16).reshape(out_ref.shape)


def attention_weight_call(owner, norm, joined, grad_one, grads):
    seq_len, width = norm.shape
    return pl.pallas_call(
        attention_weight_kernel,
        grid=(2,),
        in_specs=[smem] + [anywhere] * (3 + 3 * groups),
        out_specs=pl.BlockSpec((8, width // 8, width), lambda i: (0, i, 0)),
        out_shape=jax.ShapeDtypeStruct((8, width // 4, width), bf16),
        scratch_shapes=[
            pltpu.VMEM((2, seq_len, width), bf16),
            pltpu.VMEM((2, H, seq_len, LANES), bf16),
            pltpu.VMEM((2, seq_len, width), bf16),
            pltpu.SemaphoreType.DMA((2,)),
        ],
        compiler_params=params(),
        cost_estimate=cost(4 * seq_len * width * width, 10 * seq_len * width + 4 * width * width),
    )(owner, norm, joined, grad_one, *grads)


def mix_grad_kernel(core_ref, places_ref, grad_ref, *rest, chunks):
    refs, (out_ref, weight, sem) = rest[: len(chunks.arrays)], rest[len(chunks.arrays) :]

    @pl.when(pl.program_id(0) == 0)
    def _():
        chunks.load_block(refs, places_ref, core_ref, 3, weight, sem)
        wait_block(weight, sem)

    def store(head, value):
        out_ref[head] = value

    split_heads(product(grad_ref[...], square(weight[...]), right_turned).astype(bf16), store)


def mix_grad_call(core, places, grad_one, chunks):
    seq_len, width = grad_one.shape
    rows = seq_len // 4
    return pl.pallas_call(
        functools.partial(mix_grad_kernel, chunks=chunks),
        grid=(4,),
        in_specs=[smem, smem, row_block(rows, width)] + chunks.specs,
        out_specs=pl.BlockSpec((H, rows, LANES), lambda i: (0, i, 0)),
        out_shape=jax.ShapeDtypeStruct((H, seq_len, LANES), bf16),
        scratch_shapes=[pltpu.VMEM((8, width // 8, width), bf16), pltpu.SemaphoreType.DMA],
        compiler_params=params(),
        cost_estimate=cost(2 * seq_len * width * width, 8 * seq_len * width),
    )(core, places, grad_one, *chunks.arrays)


def start_back_kernel(
    core_ref, places_ref, count_ref, index_row_ref, index_ref, middle_grad_ref, start_ref, mod_ref,
    *rest, chunks, first
):
    grad_refs = [rest[block * groups : (block + 1) * groups] for block in range(3)]
    rest = rest[3 * groups :]
    refs, rest = rest[: len(chunks.arrays)], rest[len(chunks.arrays) :]
    row_grad_ref, slot_ref, sums_ref, weight, sems = rest[-5:]
    earlier = rest[:-5]
    rows, width = start_ref.shape
    toks, per_tok = slot_ref.shape[0], index_ref.shape[0] // slot_ref.shape[0]
    slot_count = index_ref.shape[0]

    for block in range(3):
        chunks.load_block(refs, places_ref, core_ref, block, weight.at[block], sems.at[block])
    sums = {}
    total = None
    for block, refs in enumerate(grad_refs):
        joined = join_heads(refs)
        if block != 1:
            sums[block // 2] = column_sum(joined.astype(f32))
        wait_block(weight.at[block], sems.at[block])
        part = product(joined, square(weight[block]), right_turned)
        total = part if total is None else total + part
    unit, inverse = normalize(start_ref[...])
    sums[2] = column_sum(total * unit)
    sums[3] = column_sum(total)
    row_grad = middle_grad_ref[...] + normalize_back(total, unit, inverse, mod_ref[1:2])
    row_low = row_grad.astype(bf16)
    row_grad_ref[...] = row_low
    base = first * rows
    place = lax.broadcasted_iota(jnp.int32, (slot_count, rows), 1) + base
    slot = lax.broadcasted_iota(jnp.int32, (slot_count, rows), 0)
    chosen = jnp.where((index_ref[...] == place) & (slot < count_ref[0]), 1.0, 0.0)
    part = product(chosen.astype(bf16), row_low)

    part = part.astype(bf16).reshape(toks, per_tok, width)
    if earlier:
        part = part + earlier[0][:, :per_tok]
    slot_ref[:, :per_tok] = part
    here = lax.broadcasted_iota(jnp.int32, (rows, slot_count), 0) + base
    lane = lax.broadcasted_iota(jnp.int32, (rows, slot_count), 1)
    taken = jnp.where((index_row_ref[...] == here) & (lane < count_ref[0]), 1.0, 0.0)
    empty = 1.0 - jnp.sum(taken, axis=1, keepdims=True)
    sums[4] = column_sum(row_grad * empty)
    sums_ref[...] = jnp.concatenate(
        [sums[number] for number in range(5)] + [jnp.zeros((3, width), f32)]
    )


def start_back_call(quarter, earlier, core, places, count, index, grads, middle_grad, start, mod, chunks):
    seq_len, width = start.shape
    slot_count = index.shape[1]
    toks = lax.axis_size("tok")
    rows = seq_len // 4
    heads = [
        pl.BlockSpec((array.shape[0], rows, LANES), lambda i: (0, quarter, 0)) for array in grads
    ]
    block = pl.BlockSpec((rows, width), lambda i: (quarter, 0))
    kept = [] if earlier is None else [earlier]
    column = index.reshape(slot_count, 1)
    return pl.pallas_call(
        functools.partial(start_back_kernel, chunks=chunks, first=quarter),
        grid=(1,),
        in_specs=[
            smem,
            smem,
            smem,
            whole_block(index),
            whole_block(column),
            block,
            block,
            whole_block(mod),
        ]
        + heads
        + chunks.specs
        + [whole_block(array) for array in kept],
        out_specs=[
            row_block(rows, width),
            pl.BlockSpec((toks, slot_count // toks + 8, width), lambda i: (0, 0, 0)),
            pl.BlockSpec((8, width), lambda i: (0, 0)),
        ],
        out_shape=[
            jax.ShapeDtypeStruct((rows, width), bf16),
            jax.ShapeDtypeStruct((toks, slot_count // toks + 8, width), bf16),
            jax.ShapeDtypeStruct((8, width), f32),
        ],
        scratch_shapes=[
            pltpu.VMEM((3, 8, width // 8, width), bf16),
            pltpu.SemaphoreType.DMA((3,)),
        ],
        compiler_params=params(),
        cost_estimate=cost(2 * seq_len * width * width, 7 * seq_len * width),
    )(core, places, count, index, column, middle_grad, start, mod, *grads, *chunks.arrays, *kept)


def collect_kernel(feed_ref, up_ref, *rest):
    *start_refs, _, mod_ref, small_ref = rest
    start = start_refs[0][...]
    for ref in start_refs[1:]:
        start = start + ref[...]
    feed = feed_ref[...]
    row = lambda values, number: values[number : number + 1]
    blank = jnp.zeros((7, start.shape[1]), f32)
    width = start.shape[1]
    rows = [row(start, 3), row(start, 2), row(feed, 4), row(feed, 3), row(feed, 2), row(feed, 0)]
    share = 6 * width // mod_ref.shape[0]
    for tok in range(mod_ref.shape[0]):
        place, left, pieces = tok * share, share, []
        while left:
            within = place % width
            count = min(left, width - within)
            pieces.append(rows[place // width][:, within : within + count])
            place, left = place + count, left - count
        pieces.append(jnp.zeros((1, width - share), f32))
        line = jnp.concatenate(pieces, axis=1)
        mod_ref[tok] = jnp.broadcast_to(line, (8, width)).astype(bf16)
    small_ref[...] = jnp.concatenate(
        [row(start, 4), row(start, 0), row(start, 1), row(feed, 5), row(feed, 1)]
        + [up_ref[block] for block in range(4)]
        + [blank]
    ).astype(bf16)


def collect_call(feed, up, slots, *starts):
    toks, rows, width = slots.shape
    return pl.pallas_call(
        collect_kernel,
        grid=(1,),
        in_specs=[whole_block(feed), whole_block(up)]
        + [whole_block(start) for start in starts]
        + [anywhere],
        out_specs=[
            pl.BlockSpec((toks, 8, width), lambda i: (0, rows // 8 - 1, 0)),
            pl.BlockSpec((16, width), lambda i: (0, 0)),
        ],
        out_shape=[
            jax.ShapeDtypeStruct(slots.shape, bf16),
            jax.ShapeDtypeStruct((16, width), bf16),
        ],
        input_output_aliases={2 + len(starts): 0},
        compiler_params=params(),
    )(feed, up, *starts, slots)


def swap_pairs(size, bit):
    return [(place, place ^ bit) for place in range(size)]


def swap_core(values):
    return lax.ppermute(values, "grp", swap_pairs(lax.axis_size("grp"), 1))


def add_low(*parts):
    total = parts[0].astype(f32)
    for part in parts[1:]:
        total = total + part.astype(f32)
    return total.astype(bf16)


def swap_x(values):
    return lax.ppermute(values, "grp", swap_pairs(lax.axis_size("grp"), 2))


class Ring:
    def __init__(self):
        size = lax.axis_size("tok")
        self.size = size
        order = list(range(0, size, 2)) + list(range(1, size, 2))[::-1]
        self.ahead = [(order[i], order[(i + 1) % size]) for i in range(size)]
        self.behind = [(after, before) for before, after in self.ahead]
        tok = lax.axis_index("tok")
        self.place = jnp.where(tok % 2 == 0, tok // 2, size - 1 - tok // 2)
        self.x_bit = (lax.axis_index("grp") // 2) % 2

    def tok_at(self, distance):
        place = (self.place + distance) % self.size
        return jnp.where(place < self.size // 2, 2 * place, 2 * (self.size - 1 - place) + 1)

    def forward(self, values):
        return lax.ppermute(values, "tok", self.ahead)

    def backward(self, values):
        return lax.ppermute(values, "tok", self.behind)


def sync(*values):
    return lax.optimization_barrier(values)


class Gather:
    def __init__(self, ring, mine, other, part, middle, early=False):
        self.ring, self.part, self.middle, self.early = ring, part, middle, early
        self.mine, self.other = [(mine[None], "all", [0])], [(other[None], "all", [0])]
        payload = lax.dynamic_slice_in_dim(mine, part * ring.x_bit, part + middle, 0)
        self.pieces = [payload, payload]
        self.distance = 0
        self.own = None
        self.making, self.ready = [], []

    def issue(self):
        ring, flight = self.ring, {}
        middle, half = self.middle, ring.size // 2
        if self.distance == half:
            self.ready, self.making = self.ready + self.making, []
        flight["pair"] = [entry[0] for entry in self.making]
        self.made = [entry[1:] for entry in self.making]
        self.making = []
        flight["core"] = [swap_core(entry[0]) for entry in self.ready]
        self.sent = [entry[1:] for entry in self.ready]
        self.ready = []
        if self.distance < half:
            self.distance += 1
            ahead, behind = self.pieces
            if self.distance == half:
                ahead, behind = ahead[:middle], behind[middle:]
            flight["ring"] = [ring.forward(ahead), ring.backward(behind)]
        if self.own is not None:
            flight["x"] = swap_x(self.own)
        return flight

    def land(self, flight):
        bit, part, middle = self.ring.x_bit, self.part, self.middle
        self.other += [(array,) + entry for array, entry in zip(flight["core"], self.sent)]
        self.ready = [(array,) + entry for array, entry in zip(flight["pair"], self.made)]
        self.own = None
        if "x" in flight:
            got = flight["x"]
            self.mine.append((got, "got", self.places))
            if len(self.places) == 1:
                if self.early:
                    self.making = [(got, "got", self.places)]
                else:
                    pair = jnp.concatenate(self.pieces + [got[0]])[None]
                    self.making = [(pair, "pair", self.places)]
            else:
                pair = jnp.concatenate([jnp.stack(self.pieces), got], axis=1)
                self.making = [(pair, "pair", self.places)]
        if "ring" in flight:
            ahead, behind = self.pieces = flight["ring"]
            place = 2 * self.distance - 1
            if self.distance == self.ring.size // 2:
                self.places = [place]
                self.mine += [(ahead[None], "first", [place]), (behind[None], "second", [place])]
                if self.early:
                    self.ready.append((jnp.concatenate([ahead, behind])[None], "piece", [place]))
                self.own = jnp.where(bit == 0, ahead[:part], behind)[None]
            else:
                self.places = [place, place + 1]
                self.mine += [(ahead[None], "piece", [place]), (behind[None], "piece", [place + 1])]
                self.own = jnp.stack(
                    [
                        lax.dynamic_slice_in_dim(piece, middle * bit, part, 0)
                        for piece in self.pieces
                    ]
                )

    def chunks(self, stride=0):
        return Chunks(self.mine, self.other, self.part, self.middle, stride)

    def rows(self, first, count):
        bit, part, middle = self.ring.x_bit, self.part, self.middle
        low = first - part
        ahead, behind = self.pieces
        parts = [self.mine[0][0][0, first : first + count]]
        for array, kind, _ in self.mine:
            if kind == "piece":
                parts.append(lax.dynamic_slice_in_dim(array[0], first - part * bit, count, 0))
        parts.append(jnp.where(bit == 0, behind[first - middle :][:count], ahead[low:][:count]))
        return jnp.stack(parts)


class Scatter:
    def __init__(self, ring, *values):
        self.ring, self.values = ring, values
        self.distance = ring.size // 2
        self.split = values[0].shape[1] // 2

    def piece(self, place, row, count):
        tok, width = self.ring.tok_at(place), self.values[0].shape[2]
        return sum(
            lax.dynamic_slice(values, (tok, row, 0), (1, count, width))[0].astype(f32)
            for values in self.values
        )

    def prepare(self):
        ring, distance, split = self.ring, self.distance, self.split
        rows = self.values[0].shape[1]
        if distance == ring.size // 2:
            ahead = self.piece(distance, 0, split)
            behind = self.piece(distance, split, rows - split)
        else:
            ahead, behind = self.ahead.astype(f32), self.behind.astype(f32)
            if distance == ring.size // 2 - 1:
                ahead = jnp.pad(ahead, ((0, rows - split), (0, 0)))
                behind = jnp.pad(behind, ((split, 0), (0, 0)))
            ahead = self.piece(distance, 0, rows) + ahead
            behind = self.piece(-distance, 0, rows) + behind
        self.distance -= 1
        return ahead.astype(bf16), behind.astype(bf16)

    def send(self, payload):
        return self.ring.forward(payload[0]), self.ring.backward(payload[1])

    def hop(self):
        return self.send(self.prepare())

    def land(self, flight):
        self.ahead, self.behind = flight

    def total(self):
        rows = self.values[0].shape[1]
        total = self.piece(0, 0, rows) + self.ahead.astype(f32) + self.behind.astype(f32)
        return total.astype(bf16)


class CrossScatter:
    def __init__(self, ring, part, middle, *values):
        self.ring, self.values, self.part, self.middle = ring, values, part, middle
        self.half = self.distance = ring.size // 2
        self.split = (part + middle) // 2
        self.extras = {}

    def chip(self, place, row, count):
        tok, width = self.ring.tok_at(place), self.values[0].shape[2]
        return sum(
            lax.dynamic_slice(values, (tok, row, 0), (1, count, width))[0].astype(f32)
            for values in self.values
        )

    def cross(self, *distances):
        row = (self.part + self.middle) * (1 - self.ring.x_bit)
        places = [place for d in distances for place in ((d,) if d in (0, self.half) else (d, -d))]
        sent = jnp.stack([self.chip(place, row, self.part).astype(bf16) for place in places])
        return places, swap_x(sent)

    def land_cross(self, places, got):
        for number, place in enumerate(places):
            self.extras[place] = got[number]

    def piece(self, place):
        part, bit = self.part, self.ring.x_bit
        extra = self.extras[place].astype(f32)
        blank = jnp.zeros((self.middle, extra.shape[1]), f32)
        return self.chip(place, part * bit, part + self.middle) + jnp.where(
            bit == 0, jnp.concatenate([extra, blank]), jnp.concatenate([blank, extra])
        )

    def hop(self):
        ring, distance, split = self.ring, self.distance, self.split
        if distance == self.half:
            farthest = self.piece(distance)
            ahead, behind = farthest[:split], farthest[split:]
        else:
            ahead, behind = self.ahead.astype(f32), self.behind.astype(f32)
            if distance == self.half - 1:
                rows = self.part + self.middle
                ahead = jnp.pad(ahead, ((0, rows - split), (0, 0)))
                behind = jnp.pad(behind, ((split, 0), (0, 0)))
            ahead = self.piece(distance) + ahead
            behind = self.piece(-distance) + behind
        self.distance -= 1
        return ring.forward(ahead.astype(bf16)), ring.backward(behind.astype(bf16))

    def land(self, flight):
        self.ahead, self.behind = flight

    def total(self):
        total = self.piece(0) + self.ahead.astype(f32) + self.behind.astype(f32)
        return total.astype(bf16)

    def join(self, total, far):
        part, bit = self.part, self.ring.x_bit
        low, high = jnp.where(bit == 0, total, far), jnp.where(bit == 0, far, total)
        return jnp.concatenate(
            [low[:part], add_low(low[part:], high[: self.middle]), high[self.middle :]]
        )


def gather_plain(shard, share):
    size, width = lax.axis_size("tok"), shard.shape[1]
    full = lax.all_gather(shard, "tok", axis=0)
    blocks = [
        full[:, row : row + share].reshape(8, -1, width) for row in range(0, shard.shape[0], share)
    ]
    return jnp.concatenate(blocks, axis=1)


def by_tok(values, share):
    size = lax.axis_size("tok")
    if size == 8:
        return values
    rows = share * size // 8
    blocks = [
        values[:, row : row + rows].reshape(size, share, -1)
        for row in range(0, values.shape[1], rows)
    ]
    return jnp.concatenate(blocks, axis=1)


def scatter_plain(chip):
    return lax.psum_scatter(chip, "tok", scatter_dimension=0, tiled=True)[0]


def gather_grp(values):
    step = 1
    while step < lax.axis_size("grp"):
        got = lax.ppermute(values, "grp", swap_pairs(lax.axis_size("grp"), step))
        values = jnp.concatenate([values, got])
        step *= 2
    return values


def add_x(shard):
    step = 2
    while step < lax.axis_size("grp"):
        shard = add_low(shard, lax.ppermute(shard, "grp", swap_pairs(lax.axis_size("grp"), step)))
        step *= 2
    return shard


def spread_kernel(weight_ref, out_ref, *, count):
    share = weight_ref.shape[0]
    for block in range(4):
        pieces = [
            weight_ref[:, (4 * tok + block) * share : (4 * tok + block + 1) * share]
            for tok in range(count)
        ]
        out_ref[block] = jnp.concatenate(pieces, axis=1).astype(bf16)


def spread_call(weight, count):
    share = weight.shape[0]
    return pl.pallas_call(
        functools.partial(spread_kernel, count=count),
        out_shape=jax.ShapeDtypeStruct((4, share, weight.shape[1] // 4), bf16),
        compiler_params=params(),
    )(weight)


def unspread_kernel(core_ref, mine_ref, other_ref, out_ref, *, count):
    share = mine_ref.shape[1]

    def write(refs):
        pieces = [
            refs[block // 2][block % 2, :, tok * share : (tok + 1) * share].astype(f32)
            for tok in range(count)
            for block in range(4)
        ]
        out_ref[...] = jnp.concatenate(pieces, axis=1)

    @pl.when(core_ref[0] == 0)
    def _():
        write((mine_ref, other_ref))

    @pl.when(core_ref[0] != 0)
    def _():
        write((other_ref, mine_ref))


def unspread_call(core, mine, other, count):
    share, width = mine.shape[1:]
    return pl.pallas_call(
        functools.partial(unspread_kernel, count=count),
        in_specs=[smem, whole_block(mine), whole_block(other)],
        out_shape=jax.ShapeDtypeStruct((share, 4 * width), f32),
        compiler_params=params(),
    )(core, mine, other)


def on_device(
    kept_tokens,
    kept_index,
    kept_count,
    condition,
    mask_token,
    position_table,
    modulation_weight,
    modulation_bias,
    input_weight,
    query_bias,
    value_bias,
    output_weight,
    output_bias,
    up_weight,
    up_bias,
    down_weight,
    down_bias,
    cotangent,
):
    _, seq_len, width = cotangent.shape
    tok_count = lax.axis_size("tok")
    core = lax.axis_index("grp") % 2
    share = input_weight.shape[0]
    position_rows = position_table.shape[0]

    def by_core(first, second):
        return jnp.where(core == 0, first, second)

    def by_core_pair(pairs):
        return [by_core(first, second) for first, second in zip(*pairs)]

    def exchange(values):
        return lax.all_to_all(values, "tok", split_axis=0, concat_axis=0, tiled=True)

    ring = Ring()

    core_row = jnp.stack([core, ring.x_bit])
    condition_low = jax.nn.silu(condition).astype(bf16)
    slots_here = kept_tokens.shape[1]
    small_here = jnp.concatenate(
        [
            jnp.stack([mask_token, query_bias, value_bias, output_bias, down_bias]),
            up_bias.reshape(4, share),
        ]
    ).astype(bf16)
    extra = lax.dynamic_update_slice(
        jnp.zeros((16, width), bf16), small_here, (0, share * lax.axis_index("tok"))
    )
    extra = jnp.concatenate([extra[:9], condition_low, extra[10:]])
    arrived = exchange(
        jnp.concatenate(
            [kept_tokens.astype(bf16), jnp.broadcast_to(extra, (tok_count, 16, width))], axis=1
        )
    )
    condition_group = arrived[:, slots_here + 9]
    small = jnp.sum(arrived[:, slots_here:].astype(f32), axis=0)

    def modulate_all(conditions, weight):
        modulation_part = jnp.dot(
            conditions, weight, preferred_element_type=f32
        ) + modulation_bias.astype(bf16).astype(f32)
        return exchange(modulation_part).reshape(6, width)

    condition_all = gather_grp(condition_group)

    ringed = share % 16 == 0 and lax.axis_size("grp") == 4
    table_rows = position_rows // 2

    input_low = input_weight.astype(bf16)
    input_blocks = [input_low[:, number * width : (number + 1) * width] for number in range(3)]
    position_low = position_table.astype(bf16)
    attention_pairs = input_blocks[:2], [input_blocks[2], output_weight.astype(bf16)]
    attention_low = tuple(
        jnp.concatenate([pair[0], position_low[half * table_rows : (half + 1) * table_rows], pair[1]])
        for half, pair in enumerate(attention_pairs)
    )
    attention_cut, feed_cut = (7 * share // 9, 8 * share // 9), (4 * share // 3, 4 * share // 3)
    if ringed:
        mine, other = by_core(*attention_low), by_core(*attention_low[::-1])
        gather = Gather(ring, mine, other, *attention_cut)
        flight, up_weight, down_weight, modulation_weight = sync(
            gather.issue(), up_weight, down_weight, modulation_weight
        )
        gather.land(flight)
        (flight,) = sync(gather.issue())
        gather.land(flight)
    modulation_low = modulation_weight.astype(bf16)
    up_low = spread_call(up_weight, tok_count)
    down_low = down_weight.astype(bf16).reshape(4, share, width)
    feed_low = tuple(
        jnp.concatenate([up_low[half : half + 2], down_low[half : half + 2]]).reshape(-1, width)
        for half in (0, 2)
    )
    if ringed:
        mine, other = by_core(*feed_low), by_core(*feed_low[::-1])
        flight, condition_group, arrived, small, mine, other, modulation_low = sync(
            gather.issue(), condition_group, arrived, small, mine, other, modulation_low
        )
        gather.land(flight)
        feed_gather = Gather(ring, mine, other, *feed_cut, early=True)
        flight, condition_group = sync(gather.issue(), condition_group)
        gather.land(flight)
    mod = modulate_all(condition_group, modulation_low)
    if ringed:
        table_mine = gather.rows(share, table_rows)
        feed_flight = feed_gather.issue()
        flight, table_mine, table_other, mod = sync(
            gather.issue(), table_mine, swap_core(table_mine), mod
        )
        gather.land(flight)
        flight = gather.issue()
        distances = [0]
        for distance in range(1, ring.size // 2):
            distances += [-distance, distance]
        places = ring.tok_at(jnp.array(distances + [ring.size // 2], jnp.int32))
    else:
        places = jnp.arange(8, dtype=jnp.int32)
        mine = gather_plain(jnp.concatenate(by_core_pair(attention_pairs)), share)
        everywhere = list(range(8))
        plain_chunks = lambda mine: Chunks(
            [(mine, "all", everywhere)], [(swap_core(mine), "all", everywhere)]
        )
        attention_chunks = plain_chunks(mine)
        feed_chunks = plain_chunks(gather_plain(by_core(*feed_low), share))
        table = lax.all_gather(position_low, "tok").reshape(8, -1, width)

        halves = jnp.split(table, 2, axis=1)
        table_mine, table_other = by_core(*halves), by_core(*halves[::-1])
    table_chunks = Chunks(
        [(table_mine, "all", list(range(8)))], [(table_other, "all", list(range(8)))]
    )
    start, norm_one = start_call(
        core_row, places, kept_count, kept_index, arrived, small, mod, table_chunks, 0,
        table_mine.shape[1], seq_len,
    )
    if ringed:
        flight, feed_flight, start, norm_one = sync(flight, feed_flight, start, norm_one)
        gather.land(flight)
        attention_chunks = gather.chunks(share + table_rows)
        feed_gather.land(feed_flight)
    projected = project_call(core_row, places, norm_one, small, attention_chunks)
    if ringed:
        flight, projected, start = sync(feed_gather.issue(), projected, start)
        feed_gather.land(flight)
    attended = None
    for first, heads in forward_groups:
        attended = attend_call(projected, first, heads, attended)
        if ringed:
            flight, attended, projected = sync(feed_gather.issue(), attended, projected)
            feed_gather.land(flight)
    joined, branch_one, middle, norm_two = mix_call(
        core_row, places, attended[0], start, small, mod, attention_chunks
    )
    if ringed:
        flight, norm_two = sync(feed_gather.issue(), norm_two)
        feed_gather.land(flight)
        (flight,) = sync(feed_gather.issue())
        feed_gather.land(flight)
        feed_chunks = feed_gather.chunks()
    (
        block_output,
        hidden,
        pre_grad,
        grad_two,
        middle_grad,
        grad_one,
        feed_sums,
        up_bias_sum,
    ) = feed_call(
        core_row, places, norm_two, middle, cotangent[0], branch_one, mod, small, feed_chunks
    )
    far, near = 2 - 2 * core_row[:1], 2 * core_row[:1]
    other_up = feed_weight_call(far, norm_two, pre_grad)
    other_up, hidden, grad_one = sync(other_up, hidden, grad_one)
    other_down = feed_weight_call(far, hidden, grad_two)
    got_up, other_down, norm_two = sync(swap_core(other_up), other_down, norm_two)
    feed_chip = feed_weight_call(near, norm_two, pre_grad, got_up, rows=4)
    got_down, feed_chip, hidden = sync(swap_core(other_down), feed_chip, hidden)
    feed_chip = feed_weight_call(near, hidden, grad_two, got_down, feed_chip, 2, 4)
    feed_chip, grad_one = sync(feed_chip, grad_one)
    if ringed:
        feed_scatter = Scatter(ring, feed_chip)
        payload, grad_one = sync(feed_scatter.prepare(), grad_one)
        flight = feed_scatter.send(payload)
    mix_grad = mix_grad_call(core_row, places, grad_one, attention_chunks)
    grads = []
    for group, (first, heads) in enumerate(back_groups):
        grads.append(attend_back_call(projected, attended, mix_grad, first, heads))
        if ringed and group < 2:
            if group:
                flight = feed_scatter.hop()
            flight, grads, mix_grad = sync(flight, grads, mix_grad)
            feed_scatter.land(flight)
    grads = [triple[block] for block in range(3) for triple in grads]

    def attention_weights(owner, norm):
        return attention_weight_call(owner, norm, joined, grad_one, grads)

    def start_back(quarter, earlier, grads):
        return start_back_call(
            quarter, earlier, core_row, places, kept_count, kept_index, grads, middle_grad, start, mod,
            attention_chunks,
        )

    attention_other = attention_weights(1 - core_row[:1], norm_one)
    if ringed:
        flight, attention_other, norm_one, grads = sync(
            feed_scatter.hop(), attention_other, norm_one, grads
        )
        feed_scatter.land(flight)
        feed_flight = feed_scatter.hop()
    attention_mine = attention_weights(core_row[:1], norm_one)
    attention_got = swap_core(attention_other)
    if ringed:
        attention_mine, attention_got, grads = sync(attention_mine, attention_got, grads)
        scatter = CrossScatter(ring, 2 * share // 3, 2 * share // 3, attention_mine, attention_got)
    quarters = []
    slot_grad = None
    for quarter in range(4):
        part = start_back(quarter, slot_grad, grads)
        if ringed:
            if quarter == 0:
                places_crossed, crossed = scatter.cross(scatter.half, scatter.half - 1)
                crossed, part, grads, feed_flight = sync(crossed, part, grads, feed_flight)
                feed_scatter.land(feed_flight)
                feed_shard = feed_scatter.total()
                feed_cross = swap_x(feed_shard)
            else:
                following = (scatter.half - 1 - quarter,)
                if quarter == 3:
                    following = tuple(range(scatter.half - 4, -1, -1))
                places_crossed, crossed = scatter.cross(*following)
                flight, crossed, part, grads = sync(scatter.hop(), crossed, part, grads)
                scatter.land(flight)
            scatter.land_cross(places_crossed, crossed)
        quarters.append(part)
        slot_grad = part[1]
    row_grad = jnp.concatenate([part[0] for part in quarters])
    slot_grad, small_grad = collect_call(
        feed_sums, up_bias_sum, slot_grad, *[part[2] for part in quarters]
    )

    position_grad = row_grad.reshape(tok_count, position_rows, width)
    halves = [
        half.reshape(-1, width)
        for half in (position_grad[:, :table_rows], position_grad[:, table_rows:])
    ]
    table_got = swap_core(jnp.concatenate([by_core(halves[1], halves[0]), small_grad]))
    arrived = exchange(slot_grad)
    table_chip = add_low(jnp.concatenate([by_core(halves[0], halves[1]), small_grad]), table_got)
    small_chip = table_chip[-16:]
    table_chip = table_chip[:-16].reshape(tok_count, table_rows, width)
    half_rows = table_rows // 2
    table_near, table_away = (
        jnp.concatenate(
            [
                lax.dynamic_slice_in_dim(table_chip, half_rows * place, half_rows, 1).reshape(-1, width),
                small_chip,
            ]
        )
        for place in (ring.x_bit, 1 - ring.x_bit)
    )
    table_got = swap_x(table_away)
    if ringed:
        while scatter.distance > 0:
            scatter.land(scatter.hop())
        attention_shard = scatter.total()
        attention_cross = swap_x(attention_shard)
    table_pair = add_low(table_near, table_got)
    table_pair, small_grad, arrived = sync(table_pair[:-16], table_pair[-16:], arrived)
    kept_low = arrived[:, :slots_here]
    modulation_grad_group = arrived[:, slots_here, : modulation_bias.shape[0]]
    condition_part = jnp.einsum(
        "ie,de->id", modulation_grad_group, modulation_low, preferred_element_type=f32
    )
    condition_high = condition_part.astype(bf16)
    condition_rest = (condition_part - condition_high.astype(f32)).astype(bf16)
    table_parts = exchange(
        jnp.concatenate(
            [
                table_pair.reshape(tok_count, half_rows, width),
                jnp.broadcast_to(small_grad[:14], (tok_count, 14, width)),
                condition_high[:, None],
                condition_rest[:, None],
            ],
            axis=1,
        )
    )
    modulation_grad_all = gather_grp(modulation_grad_group)
    modulation_total = jnp.einsum(
        "id,ie->de", condition_all, modulation_grad_all, preferred_element_type=f32
    )
    modulation_bias_total = jnp.sum(modulation_grad_all.astype(f32), axis=0)
    table_sum = jnp.sum(table_parts.astype(f32), axis=0)
    table_shard = table_sum.astype(bf16)
    condition_low_grad = table_sum[-2:-1] + table_sum[-1:]
    step = 4
    while step < lax.axis_size("grp"):
        table_shard = add_low(
            table_shard, lax.ppermute(table_shard, "grp", swap_pairs(lax.axis_size("grp"), step))
        )
        step *= 2
    table_cross = swap_x(table_shard[:half_rows])
    table_half = jnp.concatenate(
        [
            jnp.where(ring.x_bit == 0, table_shard[:half_rows], table_cross),
            jnp.where(ring.x_bit == 0, table_cross, table_shard[:half_rows]),
        ]
    )
    if ringed:
        attention_shard = scatter.join(attention_shard, attention_cross)
        feed_shard = add_low(feed_shard, feed_cross)
    else:
        attention_chip = by_tok(add_low(attention_mine, attention_got), share)
        attention_shard = add_x(scatter_plain(attention_chip))
        feed_shard = add_x(scatter_plain(by_tok(feed_chip, share)))
    table_far = swap_core(table_half)
    position_total = jnp.concatenate(
        [by_core(table_half, table_far), by_core(table_far, table_half)]
    ).astype(f32)
    small_total = lax.dynamic_slice_in_dim(
        table_shard[half_rows:], share * lax.axis_index("tok"), share, 1
    ).astype(f32)
    mask_total, query_bias_total, value_bias_total, output_bias_total, down_bias_total = (
        small_total[number] for number in range(5)
    )
    up_bias_total = small_total[5:9].reshape(-1)
    kept_grad = kept_low.astype(f32)
    far = swap_core(attention_shard)
    first, second = by_core(attention_shard, far).astype(f32), by_core(far, attention_shard).astype(f32)
    input_total = jnp.concatenate([first[:share], first[share:], second[:share]], axis=1)
    output_total = second[share:]
    feed_shard = feed_shard.reshape(4, share, width)
    feed_far = swap_core(feed_shard)
    up_total = unspread_call(core_row, feed_shard[:2], feed_far[:2], tok_count)
    down_total = jnp.concatenate(
        [by_core(feed_shard[2:], feed_far[2:]), by_core(feed_far[2:], feed_shard[2:])]
    ).reshape(-1, width).astype(f32)

    _, silu_back = jax.vjp(jax.nn.silu, condition)
    condition_grad = silu_back(condition_low_grad)[0]
    return (
        block_output[None],
        kept_grad,
        condition_grad,
        mask_total,
        position_total,
        modulation_total,
        modulation_bias_total,
        input_total,
        query_bias_total,
        value_bias_total,
        output_total,
        output_bias_total,
        up_total,
        up_bias_total,
        down_total,
        down_bias_total,
    )


def solution(mesh):
    return jax.shard_map(
        on_device,
        mesh=mesh,
        in_specs=(
            P("grp", "tok", None),
            P(("grp", "tok"), None),
            P(("grp", "tok")),
            P(("grp", "tok"), None),
            P("tok"),
            P("tok", None),
            P(None, "tok"),
            P("tok"),
            P("tok", None),
            P("tok"),
            P("tok"),
            P("tok", None),
            P("tok"),
            P("tok", None),
            P("tok"),
            P("tok", None),
            P("tok"),
            P(("grp", "tok"), None, None),
        ),
        out_specs=(
            P(("grp", "tok"), None, None),
            P("grp", "tok", None),
            P(("grp", "tok"), None),
            P("tok"),
            P("tok", None),
            P(None, "tok"),
            P("tok"),
            P("tok", None),
            P("tok"),
            P("tok"),
            P("tok", None),
            P("tok"),
            P("tok", None),
            P("tok"),
            P("tok", None),
            P("tok"),
        ),
        check_vma=False,
    )
```
